128 devices in a mesh: dp: 32 (over y, z, x_hi), sp: 4 (over x_lo, core).
Axes of the slice: x: 4 (x_hi: 2, x_lo: 2; x = x_hi * 2 + x_lo), y: 4, z: 4, core: 2. Of those that a mesh axis runs over, the one named last changes fastest.
Arguments:
- hidden_in: bfloat16 [32768, 768], P(('dp', 'sp')), may hold values from -6 to 6
- cotangent: bfloat16 [32768, 768], P(('dp', 'sp')), may hold values from -6 to 6
- attn_gain: bfloat16 [768], P(('dp', 'sp')), may hold values from 0.5 to 1.5
- attn_shift: bfloat16 [768], P(('dp', 'sp')), may hold values from -3 to 3
- mlp_gain: bfloat16 [768], P(('dp', 'sp')), may hold values from 0.5 to 1.5
- mlp_shift: bfloat16 [768], P(('dp', 'sp')), may hold values from -3 to 3
- qkv_weight: bfloat16 [768, 2304], P(('dp', 'sp')), may hold values from -0.21875 to 0.21875
- qkv_bias: bfloat16 [2304], P(('dp', 'sp')), may hold values from -3 to 3
- dense_weight: bfloat16 [768, 768], P(('dp', 'sp')), may hold values from -0.875 to 0.875
- dense_bias: bfloat16 [768], P(('dp', 'sp')), may hold values from -3 to 3
- up_weight: bfloat16 [768, 3072], P(('dp', 'sp')), may hold values from -0.21875 to 0.21875
- up_bias: bfloat16 [3072], P(('dp', 'sp')), may hold values from -3 to 3
- down_weight: bfloat16 [3072, 768], P(('dp', 'sp')), may hold values from -0.109375 to 0.109375
- down_bias: bfloat16 [768], P(('dp', 'sp')), may hold values from -3 to 3
Outputs:
- hidden_out: bfloat16 [32768, 768], P(('dp', 'sp'))
- hidden_grad: bfloat16 [32768, 768], P(('dp', 'sp'))
- attention_gain_gradient: float32 [768], P(('dp', 'sp'))
- attn_shift_grad: float32 [768], P(('dp', 'sp'))
- feedforward_gain_gradient: float32 [768], P(('dp', 'sp'))
- mlp_shift_grad: float32 [768], P(('dp', 'sp'))
- qkv_weight_grad: float32 [768, 2304], P(('dp', 'sp'))
- qkv_bias_grad: float32 [2304], P(('dp', 'sp'))
- dense_weight_grad: float32 [768, 768], P(('dp', 'sp'))
- dense_bias_grad: float32 [768], P(('dp', 'sp'))
- up_weight_grad: float32 [768, 3072], P(('dp', 'sp'))
- up_bias_grad: float32 [3072], P(('dp', 'sp'))
- down_weight_grad: float32 [3072, 768], P(('dp', 'sp'))
- down_bias_grad: float32 [768], P(('dp', 'sp'))
The draws below stay inside these ranges and needn't reach their ends.
All inputs are finite; a program needn't handle non-finite values.
Results may differ from the reference program's by a relative error of at most 0.0099.
Values may be sent and summed in bfloat16 or wider, within the bound.
A program may use at most 128 MiB of HBM per device.

```python
import jax
import jax.numpy as jnp
from jax import lax

D = 768
HEADS = 12
HEAD_DIM = 64
ROT = 16
FF = 3072
LEN = 1024
TOKENS = 32768
N_DP = 32


def level_of(rng, dims, shards, smallest, top_value):
    loudness = 1.0
    for dim, parts in shards:
        heights = jax.random.uniform(jax.random.fold_in(jax.random.fold_in(rng, 6), dim), (parts,), jnp.float32, smallest / len(shards), top_value / len(shards))
        loudness = loudness * jnp.repeat(jnp.exp(heights), dims[dim] // parts).reshape((-1,) + (1,) * (len(dims) - 1 - dim))
    return loudness


def gaussian(key, extent, scale, bound, split=(), kind=jnp.bfloat16):
    values = jax.random.normal(key, extent, jnp.float32) * scale
    if len(split) > 0:
        values = level_of(key, extent, split, -0.22, 0.18) * values
    return jnp.clip(values, min=-bound, max=bound).astype(kind)


def setup_inputs(seed: int = 0) -> dict:
    arg_keys = jax.random.split(jax.random.key(seed), 15)
    hidden_in = gaussian(arg_keys[0], (TOKENS, D), 1.0, 6.0, ((0, 128),))
    cotangent = gaussian(arg_keys[1], (TOKENS, D), 1.0, 6.0, ((0, 128),))
    attn_gain = jnp.clip(1.0 + 0.1 * jax.random.normal(arg_keys[2], (D,), jnp.float32), 0.5, 1.5).astype(jnp.bfloat16)
    attn_shift = gaussian(arg_keys[3], (D,), 0.5, 3.0, ((0, 128),))
    mlp_gain = jnp.clip(1.0 + 0.1 * jax.random.normal(arg_keys[4], (D,), jnp.float32), 0.5, 1.5).astype(jnp.bfloat16)
    mlp_shift = gaussian(arg_keys[5], (D,), 0.5, 3.0, ((0, 128),))
    qkv_weight = gaussian(arg_keys[6], (D, 3 * D), D ** -0.5, 0.21875, ((0, 128),))
    qkv_bias = gaussian(arg_keys[7], (3 * D,), 0.5, 3.0, ((0, 128),))
    dense_weight = gaussian(arg_keys[8], (D, D), (D // 16) ** -0.5, 0.875, ((0, 128),))
    dense_bias = gaussian(arg_keys[9], (D,), 0.5, 3.0, ((0, 128),))
    up_weight = gaussian(arg_keys[10], (D, FF), D ** -0.5, 0.21875, ((0, 128),))
    up_bias = gaussian(arg_keys[11], (FF,), 0.5, 3.0, ((0, 128),))
    down_weight = gaussian(arg_keys[12], (FF, D), FF ** -0.5, 0.109375, ((0, 128),))
    down_bias = gaussian(arg_keys[13], (D,), 0.5, 3.0, ((0, 128),))
    return {"hidden_in": hidden_in, "cotangent": cotangent, "attn_gain": attn_gain, "attn_shift": attn_shift, "mlp_gain": mlp_gain, "mlp_shift": mlp_shift, "qkv_weight": qkv_weight, "qkv_bias": qkv_bias, "dense_weight": dense_weight, "dense_bias": dense_bias, "up_weight": up_weight, "up_bias": up_bias, "down_weight": down_weight, "down_bias": down_bias}


@jax.custom_vjp
def low(v):
    return lax.optimization_barrier(v.astype(jnp.bfloat16)).astype(jnp.float32)

@jax.custom_vjp
def low_back(v):
    return v

def low_keep(v):
    return (low(v), None)

def low_pass(kept, grad):
    return (grad,)

def back_keep(v):
    return (v, None)

def back_low(kept, grad):
    return (low(grad),)
low.defvjp(low_keep, low_pass)
low_back.defvjp(back_keep, back_low)

def matmul(left, right):
    return jnp.dot(left, right, preferred_element_type=jnp.float32, precision=lax.Precision.HIGHEST)

def normalize(values_in, norm_gain, shift):
    center = lax.optimization_barrier(jnp.mean(values_in, -1, keepdims=True))
    centered = values_in - center
    spread = lax.optimization_barrier(jnp.mean(centered * centered, -1, keepdims=True))
    return centered * lax.rsqrt(spread + 1e-05) * norm_gain + shift

def rotary_tables(positions):
    halfway = ROT // 2
    frequency = 10000.0 ** (-2.0 * jnp.arange(halfway, dtype=jnp.float32) / ROT)
    angles = positions.astype(jnp.float32)[:, None] * frequency[None, :]
    return (jnp.cos(angles), jnp.sin(angles), halfway)

def rotate(vector, cosine_table, sine_table, halfway):
    lead_half = vector[..., :halfway]
    next_half = vector[..., halfway:ROT]
    cosine_b = cosine_table[:, None, :]
    sine_b = sine_table[:, None, :]
    return jnp.concatenate([lead_half * cosine_b - next_half * sine_b, next_half * cosine_b + lead_half * sine_b, vector[..., ROT:]], -1)

def layer(params, sequence):
    attn_gain, attn_shift, mlp_gain, mlp_shift, qkv_weight, qkv_bias, dense_weight, dense_bias, up_weight, up_bias, down_weight, down_bias = params
    first_normalized = low(normalize(sequence, attn_gain, attn_shift))
    second_normalized = low(normalize(sequence, mlp_gain, mlp_shift))
    qkv = low_back(matmul(first_normalized, qkv_weight) + qkv_bias).reshape(LEN, 3, HEADS, HEAD_DIM)
    cosine_table, sine_table, halfway = rotary_tables(jnp.arange(LEN, dtype=jnp.int32))
    queries = low_back(low(rotate(qkv[:, 0], cosine_table, sine_table, halfway)))
    key_heads = low_back(low(rotate(qkv[:, 1], cosine_table, sine_table, halfway)))
    value_heads = low_back(low(qkv[:, 2]))
    block_rows = min(512, LEN)
    score_scale = HEAD_DIM ** (-0.5)
    key_pos = jnp.arange(LEN, dtype=jnp.int32)

    def attend(block_index):
        first_row = block_index * block_rows
        query_block = lax.dynamic_slice_in_dim(queries, first_row, block_rows, 0)
        raw_scores = low_back(jnp.einsum('qhd,khd->hqk', query_block, key_heads, precision=lax.Precision.HIGHEST))
        query_pos = first_row + jnp.arange(block_rows, dtype=jnp.int32)
        masked = jnp.where(key_pos[None, None, :] <= query_pos[None, :, None], raw_scores * score_scale, -1e+30)
        weights_low = low(jax.nn.softmax(masked, axis=-1))
        return jnp.einsum('hqk,khd->qhd', weights_low, value_heads, precision=lax.Precision.HIGHEST)
    attended = lax.map(jax.checkpoint(attend), jnp.arange(LEN // block_rows, dtype=jnp.int32))
    context = low_back(low(attended.reshape(LEN, D)))
    attn_branch = matmul(context, dense_weight) + dense_bias
    pre_act = low_back(matmul(second_normalized, up_weight) + up_bias)
    activated = low(jax.nn.gelu(pre_act, approximate=False))
    mlp_branch = matmul(activated, down_weight) + down_bias
    return sequence + attn_branch + mlp_branch

def reference(hidden_in, cotangent, attn_gain, attn_shift, mlp_gain, mlp_shift, qkv_weight, qkv_bias, dense_weight, dense_bias, up_weight, up_bias, down_weight, down_bias):
    params = tuple((item.astype(jnp.float32) for item in (attn_gain, attn_shift, mlp_gain, mlp_shift, qkv_weight, qkv_bias, dense_weight, dense_bias, up_weight, up_bias, down_weight, down_bias)))
    inputs_seq = hidden_in.astype(jnp.float32).reshape(N_DP, LEN, D)
    grads_seq = cotangent.astype(jnp.float32).reshape(N_DP, LEN, D)

    def per_sequence(carry, pair):
        sequence, seq_grad = pair
        outputs, pullback = jax.vjp(layer, params, sequence)
        param_grads, input_grad = pullback(seq_grad)
        carry = tuple((total_item + grad_item for total_item, grad_item in zip(carry, param_grads)))
        return (carry, (outputs, input_grad))
    zero_sums = tuple((jnp.zeros_like(item) for item in params))
    sums, (outputs_all, input_grads) = lax.scan(per_sequence, zero_sums, (inputs_seq, grads_seq))
    return (outputs_all.reshape(TOKENS, D).astype(jnp.bfloat16), input_grads.reshape(TOKENS, D).astype(jnp.bfloat16), sums[0], sums[1], sums[2], sums[3], sums[4], sums[5], sums[6], sums[7], sums[8], sums[9], sums[10], sums[11])
```

```python
import jax
import jax.numpy as jnp
from jax import lax
from jax.sharding import PartitionSpec as P

D = 768
HEADS = 12
HEAD_DIM = 64
ROT = 16
FF = 3072
BF = jnp.bfloat16
F32 = jnp.float32
BOTH = ("dp", "sp")


def dot(left, right):
    return jnp.dot(left, right, preferred_element_type=F32)


def contract_rows(left, right):
    return lax.dot_general(left, right, (((0,), (0,)), ((), ())), preferred_element_type=F32)


def contract_cols(left, right):
    return lax.dot_general(left, right, (((1,), (1,)), ((), ())), preferred_element_type=F32)


def norm_components(values_in):
    center = jnp.mean(values_in, -1, keepdims=True)
    centered = values_in - center
    spread = jnp.mean(centered * centered, -1, keepdims=True)
    inverse_deviation = lax.rsqrt(spread + 1e-05)
    return (centered * inverse_deviation, inverse_deviation)


def rotary_tables(length):
    half = ROT // 2
    frequency = 10000.0 ** (-2.0 * jnp.arange(half, dtype=F32) / ROT)
    angles = jnp.arange(length, dtype=F32)[:, None] * frequency[None, :]
    return (jnp.cos(angles)[:, None, :], jnp.sin(angles)[:, None, :])


def rotate(vector, cosine, sine):
    half = ROT // 2
    lead = vector[..., :half]
    after = vector[..., half:ROT]
    return jnp.concatenate(
        [lead * cosine - after * sine, after * cosine + lead * sine, vector[..., ROT:]], -1
    )


def make_local(n_dp, n_sp):
    n_all = n_dp * n_sp
    to_slice = []
    for dp in range(n_dp):
        for sp in range(n_sp):
            to_slice.append((sp * n_dp + dp, dp * n_sp + sp))
    to_owner = [(b, a) for a, b in to_slice]

    def local(
        hidden_in,
        cotangent,
        attn_gain,
        attn_shift,
        mlp_gain,
        mlp_shift,
        qkv_weight,
        qkv_bias,
        dense_weight,
        dense_bias,
        up_weight,
        up_bias,
        down_weight,
        down_bias,
    ):
        sp = lax.axis_index("sp")
        d_model = hidden_in.shape[1]
        heads_here = HEADS // n_sp
        width = heads_here * HEAD_DIM
        ff_here = FF // n_sp

        small = (
            attn_gain,
            attn_shift,
            mlp_gain,
            mlp_shift,
            qkv_bias,
            dense_bias,
            up_bias,
            down_bias,
        )
        sizes = [item.shape[0] for item in small]
        total = sum(sizes)
        packed = jnp.pad(jnp.concatenate(small), (0, 128 - total)).reshape(1, 128)
        packed = lax.all_gather(packed, BOTH, axis=0, tiled=True).astype(F32)
        vectors = []
        at = 0
        for size in sizes:
            vectors.append(packed[:, at : at + size].reshape(-1))
            at += size
        gain_1, shift_1, gain_2, shift_2, qkv_add, dense_add, up_add, down_add = vectors
        qkv_add = lax.dynamic_slice_in_dim(qkv_add.reshape(3, n_sp, width), sp, 1, 1).reshape(-1)
        up_add = lax.dynamic_slice_in_dim(up_add, sp * ff_here, ff_here, 0)

        up_part = lax.all_to_all(
            up_weight.reshape(-1, n_sp, ff_here), "sp", split_axis=1, concat_axis=0, tiled=True
        ).reshape(-1, ff_here)
        down_part = lax.ppermute(down_weight, BOTH, to_slice)
        qkv_part = lax.all_to_all(
            qkv_weight.reshape(-1, 3, n_sp, width).transpose(0, 2, 1, 3).reshape(-1, n_sp, 3 * width),
            "sp",
            split_axis=1,
            concat_axis=0,
            tiled=True,
        ).reshape(-1, 3 * width)
        dense_part = lax.ppermute(dense_weight, BOTH, to_slice)
        up_t = lax.all_gather(up_part, "dp", axis=0, tiled=True)
        down_t = lax.all_gather(down_part, "dp", axis=0, tiled=True)
        qkv_t = lax.all_gather(qkv_part, "dp", axis=0, tiled=True)
        dense_t = lax.all_gather(dense_part, "dp", axis=0, tiled=True)

        x_seq = lax.all_gather(hidden_in, "sp", axis=0, tiled=True).astype(F32)
        g_seq = lax.all_gather(cotangent, "sp", axis=0, tiled=True)
        length = x_seq.shape[0]
        xhat, rstd = norm_components(x_seq)
        normed_1 = (xhat * gain_1 + shift_1).astype(BF)
        normed_2 = (xhat * gain_2 + shift_2).astype(BF)

        pre = dot(normed_2, up_t) + up_add
        cdf = 0.5 * (1.0 + lax.erf(pre * 0.7071067811865476))
        act = (pre * cdf).astype(BF)
        out_part = dot(act, down_t)
        pdf = jnp.exp(-0.5 * pre * pre) * 0.3989422804014327
        dpre = (contract_cols(g_seq, down_t) * (cdf + pre * pdf)).astype(BF)
        down_grad = contract_rows(act, g_seq)
        up_grad = contract_rows(normed_2, dpre)
        up_bias_grad = jnp.sum(dpre.astype(F32), 0)
        dnormed_2 = contract_cols(dpre, up_t)

        qkv = (dot(normed_1, qkv_t) + qkv_add).reshape(length, 3, heads_here, HEAD_DIM)
        cosine, sine = rotary_tables(length)
        q = rotate(qkv[:, 0], cosine, sine).astype(BF).transpose(1, 0, 2)
        k = rotate(qkv[:, 1], cosine, sine).astype(BF).transpose(1, 0, 2)
        v = qkv[:, 2].astype(BF).transpose(1, 0, 2)
        dctx = contract_cols(g_seq, dense_t).astype(BF)
        do = dctx.reshape(length, heads_here, HEAD_DIM).transpose(1, 0, 2)
        scale = HEAD_DIM ** (-0.5)
        scores = jnp.einsum("hqd,hkd->hqk", q, k, preferred_element_type=F32) * scale
        where = jnp.arange(length)[:, None] >= jnp.arange(length)[None, :]
        scores = jnp.where(where[None], scores, -1e30)
        top = jnp.max(scores, -1, keepdims=True)
        probs = jnp.exp(scores - top)
        probs = probs / jnp.sum(probs, -1, keepdims=True)
        probs_low = probs.astype(BF)
        ctx = jnp.einsum("hqk,hkd->hqd", probs_low, v, preferred_element_type=F32)
        ctx = ctx.astype(BF).transpose(1, 0, 2).reshape(length, width)
        out_part = out_part + dot(ctx, dense_t)
        dense_grad = contract_rows(ctx, g_seq)
        dprobs = jnp.einsum("hqd,hkd->hqk", do, v, preferred_element_type=F32)
        delta = jnp.sum(probs * dprobs, -1, keepdims=True)
        dscores = (scale * probs * (dprobs - delta)).astype(BF)
        dq = jnp.einsum("hqk,hkd->qhd", dscores, k, preferred_element_type=F32)
        dk = jnp.einsum("hqk,hqd->khd", dscores, q, preferred_element_type=F32)
        dv = jnp.einsum("hqk,hqd->khd", probs_low, do, preferred_element_type=F32)
        dq = dq.astype(BF).astype(F32)
        dk = dk.astype(BF).astype(F32)
        dqkv = jnp.stack(
            [rotate(dq, cosine, -sine), rotate(dk, cosine, -sine), dv], 1
        ).astype(BF).reshape(length, 3 * width)
        qkv_grad = contract_rows(normed_1, dqkv)
        qkv_bias_grad = jnp.sum(dqkv.astype(F32), 0)
        dnormed_1 = contract_cols(dqkv, qkv_t)

        out_sum = lax.psum_scatter(out_part, "sp", scatter_dimension=0, tiled=True)
        x_here = hidden_in.astype(F32)
        hidden_out = (x_here + out_sum + (dense_add + down_add)).astype(BF)
        dxhat = lax.psum_scatter(
            dnormed_1 * gain_1 + dnormed_2 * gain_2, "sp", scatter_dimension=0, tiled=True
        )
        xhat_here, rstd_here = norm_components(x_here)
        g_here = cotangent.astype(F32)
        hidden_grad = (
            g_here
            + rstd_here
            * (
                dxhat
                - jnp.mean(dxhat, -1, keepdims=True)
                - xhat_here * jnp.mean(dxhat * xhat_here, -1, keepdims=True)
            )
        ).astype(BF)

        up_own = lax.psum_scatter(up_grad, "dp", scatter_dimension=0, tiled=True)
        down_own = lax.psum_scatter(down_grad, "dp", scatter_dimension=0, tiled=True)
        qkv_own = lax.psum_scatter(qkv_grad, "dp", scatter_dimension=0, tiled=True)
        dense_own = lax.psum_scatter(
            jnp.pad(dense_grad.reshape(n_dp, -1, d_model), ((0, 0), (0, 2), (0, 0))),
            "dp",
            scatter_dimension=0,
            tiled=True,
        )[0, : dense_weight.shape[0]]
        rows = up_weight.shape[0]
        up_own = lax.all_to_all(
            up_own.reshape(n_sp, rows, ff_here), "sp", split_axis=0, concat_axis=0, tiled=True
        ).transpose(1, 0, 2).reshape(rows, FF)
        qkv_own = lax.all_to_all(
            qkv_own.reshape(n_sp, rows, 3 * width), "sp", split_axis=0, concat_axis=0, tiled=True
        ).reshape(n_sp, rows, 3, width).transpose(1, 2, 0, 3).reshape(rows, 3 * d_model)
        down_own = lax.ppermute(down_own, BOTH, to_owner)
        dense_own = lax.ppermute(dense_own, BOTH, to_owner)

        zeros_qkv = jnp.zeros((3, n_sp, width), F32)
        qkv_bias_full = lax.dynamic_update_slice(
            zeros_qkv, qkv_bias_grad.reshape(3, 1, width), (0, sp, 0)
        ).reshape(-1)
        up_bias_full = lax.dynamic_update_slice(
            jnp.zeros((FF,), F32), up_bias_grad, (sp * ff_here,)
        )
        g_sum = jnp.sum(g_here, 0)
        full = (
            jnp.sum(dnormed_1 * xhat, 0),
            jnp.sum(dnormed_1, 0),
            jnp.sum(dnormed_2 * xhat, 0),
            jnp.sum(dnormed_2, 0),
            qkv_bias_full,
            g_sum,
            up_bias_full,
        )
        packed = jnp.concatenate([item.reshape(n_all, -1) for item in full], 1)
        packed = jnp.pad(packed, ((0, 0), (0, 128 - packed.shape[1])))
        mine = lax.psum_scatter(packed, BOTH, scatter_dimension=0, tiled=True).reshape(-1)
        parts = []
        at = 0
        for item in full:
            size = item.size // n_all
            parts.append(mine[at : at + size])
            at += size
        return (
            hidden_out,
            hidden_grad,
            parts[0],
            parts[1],
            parts[2],
            parts[3],
            qkv_own,
            parts[4],
            dense_own,
            parts[5],
            up_own,
            parts[6],
            down_own,
            parts[5],
        )

    return local


def solution(mesh):
    matrix = P(BOTH, None)
    vector = P(BOTH)
    ins = (matrix, matrix) + (vector,) * 4 + (matrix, vector) * 4
    outs = (matrix, matrix) + (vector,) * 4 + (matrix, vector) * 4
    return jax.shard_map(
        make_local(mesh.shape["dp"], mesh.shape["sp"]),
        mesh=mesh,
        in_specs=ins,
        out_specs=outs,
        check_vma=False,
    )
```

```python
import functools

import jax
import jax.numpy as jnp
from jax import lax
from jax.experimental import pallas as pl
from jax.experimental.pallas import tpu as pltpu
from jax.sharding import PartitionSpec as P

D = 768
HEADS = 12
HEAD_DIM = 64
ROT = 16
FF = 3072
BF = jnp.bfloat16
F32 = jnp.float32
BOTH = ("dp", "sp")


def dot(left, right):
    return jnp.dot(left, right, preferred_element_type=F32)


def contract_rows(left, right):
    return lax.dot_general(left, right, (((0,), (0,)), ((), ())), preferred_element_type=F32)


def contract_cols(left, right):
    return lax.dot_general(left, right, (((1,), (1,)), ((), ())), preferred_element_type=F32)


def norm_components(values_in):
    center = jnp.mean(values_in, -1, keepdims=True)
    centered = values_in - center
    spread = jnp.mean(centered * centered, -1, keepdims=True)
    inverse_deviation = lax.rsqrt(spread + 1e-05)
    return (centered * inverse_deviation, inverse_deviation)


def rotary_tables(length):
    half = ROT // 2
    frequency = 10000.0 ** (-2.0 * jnp.arange(half, dtype=F32) / ROT)
    angles = jnp.arange(length, dtype=F32)[:, None] * frequency[None, :]
    return (jnp.cos(angles)[:, None, :], jnp.sin(angles)[:, None, :])


def rotate(vector, cosine, sine):
    half = ROT // 2
    lead = vector[..., :half]
    after = vector[..., half:ROT]
    return jnp.concatenate(
        [lead * cosine - after * sine, after * cosine + lead * sine, vector[..., ROT:]], -1
    )


MESH = pl.DeviceIdType.MESH
SMALL = 128


def place():
    return lax.axis_index("dp"), lax.axis_index("sp")


def rows_paths(n_dp, n_sp, dp, sp):
    mine = dp * n_sp + sp

    def owner(b):
        line = sp * n_dp + b
        return line // n_sp, lax.rem(line, n_sp)

    return mine // n_dp, lax.rem(mine, n_dp), owner


def greet(n_dp, n_sp, dp, sp, to_rows, count_rows):
    barrier = pltpu.get_barrier_semaphore()

    def signal(d, s):
        pl.semaphore_signal(barrier, inc=1, device_id=(d, s), device_id_type=MESH)

    @pl.loop(1, n_dp)
    def _(k):
        signal(lax.rem(dp + k, n_dp), sp)

    for k in range(1, n_sp):
        signal(dp, lax.rem(sp + k, n_sp))

    @pl.loop(0, n_dp)
    def _(k):
        d, s = to_rows(k)

        @pl.when(jnp.logical_or(d != dp, s != sp))
        def _():
            signal(d, s)

    pl.semaphore_wait(barrier, n_dp - 1 + n_sp - 1 + count_rows)


def gather_kernel(
    n_dp, n_sp, x_ref, g_ref, cols_ref, rows_ref,
    x_out, g_out, cols_out, rows_out,
    stage, tight_wide, tight,
    local_sem, x_send, x_recv, g_send, g_recv, p_send, p_recv, c_send, c_recv, r_send, r_recv,
):
    dp, sp = place()
    column, slot, owner = rows_paths(n_dp, n_sp, dp, sp)
    count = n_dp - jnp.where(column == sp, 1, 0)
    greet(n_dp, n_sp, dp, sp, owner, count)
    tokens = x_ref.shape[0]
    own_rows = pl.ds(pl.multiple_of(sp * tokens, tokens), tokens)

    def copy(src, dst, send, recv, d, s):
        return pltpu.make_async_remote_copy(
            src_ref=src, dst_ref=dst, send_sem=send, recv_sem=recv,
            device_id=(d, s), device_id_type=MESH,
        )

    def piece(k):
        t = lax.rem(sp + k, n_sp)
        return copy(cols_ref.at[t], stage.at[sp], p_send.at[k - 1], p_recv.at[sp], dp, t)

    def tokens_of(k):
        t = lax.rem(sp + k, n_sp)
        return (
            copy(x_ref, x_out.at[own_rows], x_send.at[k - 1], x_recv.at[sp], dp, t),
            copy(g_ref, g_out.at[own_rows], g_send.at[k - 1], g_recv.at[sp], dp, t),
        )

    for k in range(1, n_sp):
        piece(k).start()
    own = (
        pltpu.make_async_copy(cols_ref.at[sp], stage.at[sp], p_recv.at[sp]),
        pltpu.make_async_copy(x_ref, x_out.at[own_rows], x_recv.at[sp]),
        pltpu.make_async_copy(g_ref, g_out.at[own_rows], g_recv.at[sp]),
    )
    for item in own:
        item.start()

    def rows_to(k):
        d = lax.rem(dp + k, n_dp)
        return copy(rows_ref, rows_out.at[slot], r_send.at[k], r_recv.at[slot], d, column)

    @pl.when(column == sp)
    def _():
        pltpu.make_async_copy(rows_ref, rows_out.at[slot], r_recv.at[slot]).start()

    @pl.when(column != sp)
    def _():
        rows_to(0).start()

    @pl.loop(1, n_dp)
    def _(k):
        rows_to(k).start()

    for k in range(1, n_sp):
        for item in tokens_of(k):
            item.start()

    for s in range(n_sp):
        pltpu.make_async_copy(cols_ref.at[s], stage.at[s], p_recv.at[s]).wait()
    part = stage.shape[1]
    for s in range(n_sp):
        tight_wide[s * part : (s + 1) * part, :] = stage[s].astype(F32)
    tight[...] = tight_wide[...].astype(BF)

    def cols_to(k):
        d = lax.rem(dp + k, n_dp)
        return copy(tight, cols_out.at[dp], c_send.at[k], c_recv.at[dp], d, sp)

    own_cols = pltpu.make_async_copy(tight, cols_out.at[dp], c_recv.at[dp])
    own_cols.start()

    @pl.loop(1, n_dp)
    def _(k):
        cols_to(k).start()

    @pl.loop(0, n_dp)
    def _(b):
        pltpu.make_async_copy(tight, cols_out.at[b], c_recv.at[b]).wait()
        pltpu.make_async_copy(rows_ref, rows_out.at[b], r_recv.at[b]).wait()

    for s in range(n_sp):
        there = pl.ds(s * tokens, tokens)
        pltpu.make_async_copy(x_ref, x_out.at[there], x_recv.at[s]).wait()
        pltpu.make_async_copy(g_ref, g_out.at[there], g_recv.at[s]).wait()

    for k in range(1, n_sp):
        piece(k).wait_send()
        for item in tokens_of(k):
            item.wait_send()

    @pl.when(column != sp)
    def _():
        rows_to(0).wait_send()

    @pl.loop(1, n_dp)
    def _(k):
        rows_to(k).wait_send()
        cols_to(k).wait_send()


def gather_all(n_dp, n_sp, x, g, cols, rows):
    part = cols.shape[1]
    tokens, d_model = x.shape
    dma = pltpu.SemaphoreType.DMA
    return pl.pallas_call(
        functools.partial(gather_kernel, n_dp, n_sp),
        out_shape=(
            jax.ShapeDtypeStruct((tokens * n_sp, d_model), BF),
            jax.ShapeDtypeStruct((tokens * n_sp, d_model), BF),
            jax.ShapeDtypeStruct((n_dp, part * n_sp, cols.shape[2]), BF),
            jax.ShapeDtypeStruct((n_dp,) + rows.shape, BF),
        ),
        in_specs=[pl.BlockSpec(memory_space=pl.ANY)] * 4,
        out_specs=(pl.BlockSpec(memory_space=pl.ANY),) * 4,
        scratch_shapes=[
            pltpu.VMEM(cols.shape, BF),
            pltpu.VMEM((part * n_sp, cols.shape[2]), F32),
            pltpu.VMEM((part * n_sp, cols.shape[2]), BF),
            dma,
        ]
        + [dma((n_sp,))] * 6
        + [dma((n_dp,))] * 4,
        compiler_params=pltpu.CompilerParams(collective_id=0, has_side_effects=True),
        name="gather_all",
    )(x, g, cols, rows)


def reduce_kernel(
    n_dp, n_sp, cols_ref, rows_ref, small_ref, out_ref, dx_ref,
    up_out, qkv_out, rows_out, small_out, hidden_out, dxhat_out,
    cols_in, rows_in, small_in, out_in, dx_in,
    stage, land, small_stage, small_land,
    c_send, c_recv, r_send, r_recv, s_send, s_recv,
    o_send, o_recv, d_send, d_recv, p_send, p_recv, t_send, t_recv,
):
    dp, sp = place()
    column, slot, owner = rows_paths(n_dp, n_sp, dp, sp)
    count = n_dp - jnp.where(column == sp, 1, 0)
    greet(n_dp, n_sp, dp, sp, lambda k: (lax.rem(dp + k, n_dp), column), count)

    def copy(src, dst, send, recv, d, s):
        return pltpu.make_async_remote_copy(
            src_ref=src, dst_ref=dst, send_sem=send, recv_sem=recv,
            device_id=(d, s), device_id_type=MESH,
        )

    def cols_to(k):
        d = lax.rem(dp + k, n_dp)
        return (
            copy(cols_ref.at[d], cols_in.at[dp], c_send.at[k], c_recv.at[dp], d, sp),
            copy(small_ref.at[d], small_in.at[dp], s_send.at[k], s_recv.at[dp], d, sp),
        )

    def rows_to(b):
        d, s = owner(b)
        return copy(rows_ref.at[b], rows_in.at[dp], r_send.at[b], r_recv.at[dp], d, s)

    def place_of(k):
        return lax.rem(slot + k, n_dp)

    def away(b):
        d, s = owner(b)
        return jnp.logical_or(d != dp, s != sp)

    def tokens_to(k):
        t = lax.rem(sp + k, n_sp)
        return (
            copy(out_ref.at[t], out_in.at[sp], o_send.at[k], o_recv.at[sp], dp, t),
            copy(dx_ref.at[t], dx_in.at[sp], d_send.at[k], d_recv.at[sp], dp, t),
        )

    pltpu.make_async_copy(cols_ref.at[dp], cols_in.at[dp], c_recv.at[dp]).start()
    pltpu.make_async_copy(small_ref.at[dp], small_in.at[dp], s_recv.at[dp]).start()
    pltpu.make_async_copy(out_ref.at[sp], out_in.at[sp], o_recv.at[sp]).start()
    pltpu.make_async_copy(dx_ref.at[sp], dx_in.at[sp], d_recv.at[sp]).start()

    @pl.when(column == sp)
    def _():
        pltpu.make_async_copy(rows_ref.at[slot], rows_in.at[dp], r_recv.at[dp]).start()

    @pl.loop(1, n_dp)
    def _(k):
        for item in cols_to(k):
            item.start()

    for k in range(1, n_sp):
        for item in tokens_to(k):
            item.start()

    @pl.loop(0, n_dp)
    def _(k):
        b = place_of(k)

        @pl.when(away(b))
        def _():
            rows_to(b).start()

    @pl.loop(0, n_dp)
    def _(b):
        pltpu.make_async_copy(cols_ref.at[b], cols_in.at[b], c_recv.at[b]).wait()
        pltpu.make_async_copy(small_ref.at[b], small_in.at[b], s_recv.at[b]).wait()

    part = land.shape[1]
    small_stage[...] = jnp.sum(small_in[...], 0)
    total = jnp.sum(cols_in[...].astype(F32), 0)
    for t in range(n_sp):
        stage[t] = total[t * part : (t + 1) * part, :]

    def piece(k):
        t = lax.rem(sp + k, n_sp)
        return (
            copy(stage.at[t], land.at[sp], p_send.at[k], p_recv.at[sp], dp, t),
            copy(small_stage, small_land.at[sp], t_send.at[k], t_recv.at[sp], dp, t),
        )

    pltpu.make_async_copy(stage.at[sp], land.at[sp], p_recv.at[sp]).start()
    pltpu.make_async_copy(small_stage, small_land.at[sp], t_recv.at[sp]).start()
    for k in range(1, n_sp):
        for item in piece(k):
            item.start()

    @pl.loop(0, n_dp)
    def _(b):
        pltpu.make_async_copy(rows_ref.at[b], rows_in.at[b], r_recv.at[b]).wait()

    rows_out[...] = jnp.sum(rows_in[...].astype(F32), 0)

    for s in range(n_sp):
        pltpu.make_async_copy(out_ref.at[s], out_in.at[s], o_recv.at[s]).wait()
        pltpu.make_async_copy(dx_ref.at[s], dx_in.at[s], d_recv.at[s]).wait()
    hidden_out[...] = jnp.sum(out_in[...].astype(F32), 0)
    dxhat_out[...] = jnp.sum(dx_in[...].astype(F32), 0)

    for s in range(n_sp):
        pltpu.make_async_copy(stage.at[s], land.at[s], p_recv.at[s]).wait()
        pltpu.make_async_copy(small_stage, small_land.at[s], t_recv.at[s]).wait()
    ff_here = up_out.shape[1] // n_sp
    width = qkv_out.shape[1] // 3 // n_sp
    for s in range(n_sp):
        block = land[s]
        up_out[:, s * ff_here : (s + 1) * ff_here] = block[:, :ff_here]
        for j in range(3):
            to = (j * n_sp + s) * width
            at = ff_here + j * width
            qkv_out[:, to : to + width] = block[:, at : at + width]
    small_out[...] = jnp.sum(small_land[...], 0)

    for k in range(1, n_sp):
        for item in piece(k) + tokens_to(k):
            item.wait_send()

    @pl.loop(1, n_dp)
    def _(k):
        for item in cols_to(k):
            item.wait_send()

    @pl.loop(0, n_dp)
    def _(b):
        @pl.when(away(b))
        def _():
            rows_to(b).wait_send()


def reduce_all(n_dp, n_sp, cols, rows, small, out, dx):
    part = cols.shape[1] // n_sp
    d_model = rows.shape[2]
    dma = pltpu.SemaphoreType.DMA
    vmem = pl.BlockSpec(memory_space=pltpu.VMEM)
    return pl.pallas_call(
        functools.partial(reduce_kernel, n_dp, n_sp),
        out_shape=(
            jax.ShapeDtypeStruct((part, FF), F32),
            jax.ShapeDtypeStruct((part, 3 * d_model), F32),
            jax.ShapeDtypeStruct(rows.shape[1:], F32),
            jax.ShapeDtypeStruct(small.shape[1:], F32),
            jax.ShapeDtypeStruct(out.shape[1:], F32),
            jax.ShapeDtypeStruct(dx.shape[1:], F32),
        ),
        in_specs=[pl.BlockSpec(memory_space=pl.ANY)] * 5,
        out_specs=(vmem,) * 6,
        scratch_shapes=[
            pltpu.VMEM(cols.shape, BF),
            pltpu.VMEM(rows.shape, BF),
            pltpu.VMEM(small.shape, F32),
            pltpu.VMEM(out.shape, BF),
            pltpu.VMEM(dx.shape, BF),
            pltpu.VMEM((n_sp, part, cols.shape[2]), F32),
            pltpu.VMEM((n_sp, part, cols.shape[2]), F32),
            pltpu.VMEM(small.shape[1:], F32),
            pltpu.VMEM((n_sp,) + small.shape[1:], F32),
        ]
        + [dma((n_dp,))] * 6
        + [dma((n_sp,))] * 8,
        compiler_params=pltpu.CompilerParams(
            collective_id=1, has_side_effects=True, vmem_limit_bytes=40 * 1024 * 1024
        ),
        name="reduce_all",
    )(cols, rows, small, out, dx)


def make_local(n_dp, n_sp):
    n_all = n_dp * n_sp
    def local(
        hidden_in,
        cotangent,
        attn_gain,
        attn_shift,
        mlp_gain,
        mlp_shift,
        qkv_weight,
        qkv_bias,
        dense_weight,
        dense_bias,
        up_weight,
        up_bias,
        down_weight,
        down_bias,
    ):
        sp = lax.axis_index("sp")
        d_model = hidden_in.shape[1]
        heads_here = HEADS // n_sp
        width = heads_here * HEAD_DIM
        ff_here = FF // n_sp

        small = (
            attn_gain,
            attn_shift,
            mlp_gain,
            mlp_shift,
            qkv_bias,
            dense_bias,
            up_bias,
            down_bias,
        )
        sizes = [item.shape[0] for item in small]
        total = sum(sizes)
        part = up_weight.shape[0]
        packed = jnp.pad(jnp.concatenate(small), (0, SMALL - total)).reshape(1, 1, SMALL)
        packed = jnp.pad(jnp.broadcast_to(packed, (n_sp, 1, SMALL)), ((0, 0), (0, part - 1), (0, 0)))
        cols = jnp.concatenate(
            [
                up_weight.reshape(part, n_sp, ff_here).transpose(1, 0, 2),
                qkv_weight.reshape(part, 3, n_sp, width)
                .transpose(2, 0, 1, 3)
                .reshape(n_sp, part, 3 * width),
                packed,
            ],
            2,
        )
        block = down_weight.shape[0]
        fill = jnp.zeros((-(block + part) % 16, d_model), BF)
        rows = jnp.concatenate([down_weight, dense_weight, fill], 0)
        x_seq, g_seq, cols, rows = gather_all(n_dp, n_sp, hidden_in, cotangent, cols, rows)
        split = ff_here + 3 * width
        up_t = cols[:, :, :ff_here].reshape(d_model, ff_here)
        qkv_t = cols[:, :, ff_here:split].reshape(d_model, 3 * width)
        down_t = rows[:, :block].reshape(ff_here, d_model)
        dense_t = rows[:, block : block + part].reshape(width, d_model)
        packed = cols[:, ::part, split:].reshape(n_all, SMALL).astype(F32)
        vectors = []
        at = 0
        for size in sizes:
            vectors.append(packed[:, at : at + size].reshape(-1))
            at += size
        gain_1, shift_1, gain_2, shift_2, qkv_add, dense_add, up_add, down_add = vectors
        qkv_add = lax.dynamic_slice_in_dim(qkv_add.reshape(3, n_sp, width), sp, 1, 1).reshape(-1)
        up_add = lax.dynamic_slice_in_dim(up_add, sp * ff_here, ff_here, 0)
        x_seq = x_seq.astype(F32)
        length = x_seq.shape[0]
        xhat, rstd = norm_components(x_seq)
        normed_1 = (xhat * gain_1 + shift_1).astype(BF)
        normed_2 = (xhat * gain_2 + shift_2).astype(BF)

        pre = dot(normed_2, up_t) + up_add
        cdf = 0.5 * (1.0 + lax.erf(pre * 0.7071067811865476))
        act = (pre * cdf).astype(BF)
        out_part = dot(act, down_t)
        pdf = jnp.exp(-0.5 * pre * pre) * 0.3989422804014327
        dpre = (contract_cols(g_seq, down_t) * (cdf + pre * pdf)).astype(BF)
        down_grad = contract_rows(act, g_seq)
        up_grad = contract_rows(normed_2, dpre)
        up_bias_grad = jnp.sum(dpre.astype(F32), 0)
        dnormed_2 = contract_cols(dpre, up_t)

        qkv = (dot(normed_1, qkv_t) + qkv_add).reshape(length, 3, heads_here, HEAD_DIM)
        cosine, sine = rotary_tables(length)
        q = rotate(qkv[:, 0], cosine, sine).astype(BF).transpose(1, 0, 2)
        k = rotate(qkv[:, 1], cosine, sine).astype(BF).transpose(1, 0, 2)
        v = qkv[:, 2].astype(BF).transpose(1, 0, 2)
        dctx = contract_cols(g_seq, dense_t).astype(BF)
        do = dctx.reshape(length, heads_here, HEAD_DIM).transpose(1, 0, 2)
        scale = HEAD_DIM ** (-0.5)
        scores = jnp.einsum("hqd,hkd->hqk", q, k, preferred_element_type=F32) * scale
        where = jnp.arange(length)[:, None] >= jnp.arange(length)[None, :]
        scores = jnp.where(where[None], scores, -1e30)
        top = jnp.max(scores, -1, keepdims=True)
        probs = jnp.exp(scores - top)
        probs = probs / jnp.sum(probs, -1, keepdims=True)
        probs_low = probs.astype(BF)
        ctx = jnp.einsum("hqk,hkd->hqd", probs_low, v, preferred_element_type=F32)
        ctx = ctx.astype(BF).transpose(1, 0, 2).reshape(length, width)
        out_part = out_part + dot(ctx, dense_t)
        dense_grad = contract_rows(ctx, g_seq)
        dprobs = jnp.einsum("hqd,hkd->hqk", do, v, preferred_element_type=F32)
        delta = jnp.sum(probs * dprobs, -1, keepdims=True)
        dscores = (scale * probs * (dprobs - delta)).astype(BF)
        dq = jnp.einsum("hqk,hkd->qhd", dscores, k, preferred_element_type=F32)
        dk = jnp.einsum("hqk,hqd->khd", dscores, q, preferred_element_type=F32)
        dv = jnp.einsum("hqk,hqd->khd", probs_low, do, preferred_element_type=F32)
        dq = dq.astype(BF).astype(F32)
        dk = dk.astype(BF).astype(F32)
        dqkv = jnp.stack(
            [rotate(dq, cosine, -sine), rotate(dk, cosine, -sine), dv], 1
        ).astype(BF).reshape(length, 3 * width)
        qkv_grad = contract_rows(normed_1, dqkv)
        qkv_bias_grad = jnp.sum(dqkv.astype(F32), 0)
        dnormed_1 = contract_cols(dqkv, qkv_t)

        g_here = cotangent.astype(F32)
        zeros_qkv = jnp.zeros((3, n_sp, width), F32)
        qkv_bias_full = lax.dynamic_update_slice(
            zeros_qkv, qkv_bias_grad.reshape(3, 1, width), (0, sp, 0)
        ).reshape(-1)
        up_bias_full = lax.dynamic_update_slice(
            jnp.zeros((FF,), F32), up_bias_grad, (sp * ff_here,)
        )
        full = (
            jnp.sum(dnormed_1 * xhat, 0),
            jnp.sum(dnormed_1, 0),
            jnp.sum(dnormed_2 * xhat, 0),
            jnp.sum(dnormed_2, 0),
            qkv_bias_full,
            jnp.sum(g_here, 0),
            up_bias_full,
        )
        packed = jnp.concatenate([item.reshape(n_all, -1) for item in full], 1)
        packed = jnp.pad(packed, ((0, 0), (0, SMALL - packed.shape[1])))
        packed = jnp.pad(packed.reshape(n_dp, n_sp, SMALL), ((0, 0), (0, -n_sp % 8), (0, 0)))

        cols = jnp.concatenate([up_grad.astype(BF), qkv_grad.astype(BF)], 1)
        rows = jnp.concatenate(
            [
                down_grad.astype(BF).reshape(n_dp, block, d_model),
                dense_grad.astype(BF).reshape(n_dp, part, d_model),
                jnp.zeros((n_dp, fill.shape[0], d_model), BF),
            ],
            1,
        )
        here = hidden_in.shape[0]
        up_own, qkv_own, rows_own, packed, out_sum, dxhat = reduce_all(
            n_dp,
            n_sp,
            cols.reshape(n_dp, part * n_sp, split),
            rows,
            packed,
            out_part.astype(BF).reshape(n_sp, here, d_model),
            (dnormed_1 * gain_1 + dnormed_2 * gain_2).astype(BF).reshape(n_sp, here, d_model),
        )
        down_own = rows_own[:block]
        dense_own = rows_own[block : block + part]
        mine = lax.dynamic_slice_in_dim(packed, sp, 1, 0).reshape(-1)

        x_here = hidden_in.astype(F32)
        hidden_out = (x_here + out_sum + (dense_add + down_add)).astype(BF)
        xhat_here, rstd_here = norm_components(x_here)
        hidden_grad = (
            g_here
            + rstd_here
            * (
                dxhat
                - jnp.mean(dxhat, -1, keepdims=True)
                - xhat_here * jnp.mean(dxhat * xhat_here, -1, keepdims=True)
            )
        ).astype(BF)
        parts = []
        at = 0
        for item in full:
            size = item.size // n_all
            parts.append(mine[at : at + size])
            at += size
        return (
            hidden_out,
            hidden_grad,
            parts[0],
            parts[1],
            parts[2],
            parts[3],
            qkv_own,
            parts[4],
            dense_own,
            parts[5],
            up_own,
            parts[6],
            down_own,
            parts[5],
        )

    return local


def solution(mesh):
    matrix = P(BOTH, None)
    vector = P(BOTH)
    ins = (matrix, matrix) + (vector,) * 4 + (matrix, vector) * 4
    outs = (matrix, matrix) + (vector,) * 4 + (matrix, vector) * 4
    return jax.shard_map(
        make_local(mesh.shape["dp"], mesh.shape["sp"]),
        mesh=mesh,
        in_specs=ins,
        out_specs=outs,
        check_vma=False,
    )
```

```python
import jax
import jax.numpy as jnp
from jax import lax
from jax.experimental import pallas as pl
from jax.experimental.pallas import tpu as pltpu
from jax.sharding import PartitionSpec as P

D = 768
HEADS = 12
HEAD_DIM = 64
ROT = 16
FF = 3072
BF = jnp.bfloat16
F32 = jnp.float32
BOTH = ("dp", "sp")


def dot(left, right):
    return jnp.dot(left, right, preferred_element_type=F32)


def contract_rows(left, right):
    return lax.dot_general(left, right, (((0,), (0,)), ((), ())), preferred_element_type=F32)


def contract_cols(left, right):
    return lax.dot_general(left, right, (((1,), (1,)), ((), ())), preferred_element_type=F32)


def norm_components(values_in):
    center = jnp.mean(values_in, -1, keepdims=True)
    centered = values_in - center
    spread = jnp.mean(centered * centered, -1, keepdims=True)
    inverse_deviation = lax.rsqrt(spread + 1e-05)
    return (centered * inverse_deviation, inverse_deviation)


def rotary_tables(length):
    half = ROT // 2
    frequency = 10000.0 ** (-2.0 * jnp.arange(half, dtype=F32) / ROT)
    angles = jnp.arange(length, dtype=F32)[:, None] * frequency[None, :]
    return (jnp.cos(angles)[:, None, :], jnp.sin(angles)[:, None, :])


def rotate(vector, cosine, sine):
    half = ROT // 2
    lead = vector[..., :half]
    after = vector[..., half:ROT]
    return jnp.concatenate(
        [lead * cosine - after * sine, after * cosine + lead * sine, vector[..., ROT:]], -1
    )


MESH = pl.DeviceIdType.MESH
SMALL = 128
PAGE = 768
NY, NZ, NX = 4, 4, 2
GROUP = NZ * NX
N_SP = 4
PART = 6


def place():
    dp, sp = lax.axis_index("dp"), lax.axis_index("sp")
    return dp, sp, dp // GROUP, lax.rem(dp // NX, NZ), lax.rem(dp, NX)


def send(src, dst, send_sem, recv_sem, device):
    return pltpu.make_async_remote_copy(
        src_ref=src,
        dst_ref=dst,
        send_sem=send_sem,
        recv_sem=recv_sem,
        device_id=device,
        device_id_type=MESH,
    )


def index_of(y, z, x):
    return (y * NZ + z) * NX + x


def slot_device(dp, sp):
    line = dp * N_SP + sp
    return lax.rem(line, NY * GROUP), line // (NY * GROUP)


def owner_device(dp, sp):
    line = sp * NY * GROUP + dp
    return line // N_SP, lax.rem(line, N_SP)


def differs(device, dp, sp):
    return jnp.logical_or(device[0] != dp, device[1] != sp)


class Plane:
    def __init__(self, last):
        self.last = last
        dp, sp, y, z, x = place()
        self.sp, self.y, self.z, self.x = sp, y, z, x
        self.mine = (z if last == "y" else y) * NX + x
        self.axis = y if last == "y" else z

    def member(self, k):
        e = lax.rem(self.mine + k, GROUP)
        a, x = e // NX, lax.rem(e, NX)
        y, z = (self.y, a) if self.last == "y" else (a, self.z)
        return (index_of(y, z, x), self.sp), e, a, x

    def along(self, k):
        a = lax.rem(self.axis + k, NY)
        y, z = (a, self.z) if self.last == "y" else (self.y, a)
        return (index_of(y, z, self.x), self.sp), a

    def block(self, ref, a):
        return ref.at[a] if self.last == "y" else ref.at[:, a]

    def chunk(self, ref, e):
        a, x = e // NX, lax.rem(e, NX)
        return ref.at[self.y, a, x] if self.last == "y" else ref.at[a, self.z, x]


def greet(partner_in, partner_out):
    dp, sp, y, z, x = place()
    barrier = pltpu.get_barrier_semaphore()

    def signal(device):
        pl.semaphore_signal(barrier, inc=1, device_id=device, device_id_type=MESH)

    for k in range(1, N_SP):
        signal((dp, lax.rem(sp + k, N_SP)))
    by_y, by_z = Plane("y"), Plane("z")
    for k in range(1, GROUP):
        signal(by_y.member(k)[0])
        signal(by_z.member(k)[0])

    @pl.when(differs(partner_in, dp, sp))
    def _():
        signal(partner_in)

    count = N_SP - 1 + 2 * (GROUP - 1)
    pl.semaphore_wait(barrier, count + jnp.where(differs(partner_out, dp, sp), 1, 0))


def gather_kernel(
    x_ref, g_ref, up_ref, qkv_ref, small_ref, down_ref, dense_ref,
    x_out, g_out, up_out, qk_out, down_out, dense_out,
    pieces, landed, tight_wide, up_tight, qk_tight,
    t_send, t_recv, p_send, p_recv, r_send, r_recv, a_send, a_recv, b_send, b_recv,
):
    dp, sp, y, z, x = place()
    to_slot, from_owner = slot_device(dp, sp), owner_device(dp, sp)
    sibling = sp + 1 - 2 * lax.rem(sp, 2)
    across = lax.rem(sp + 2, N_SP)
    greet(from_owner, to_slot)
    by_y, by_z = Plane("y"), Plane("z")

    row_arrays = ((dense_ref, dense_out), (down_ref, down_out))
    slot = to_slot[0]
    slot_at = (slot // GROUP, lax.rem(slot // NX, NZ), lax.rem(slot, NX))
    moves = differs(to_slot, dp, sp)

    @pl.when(moves)
    def _():
        for i, (src, dst) in enumerate(row_arrays):
            send(src, dst.at[slot_at], r_send.at[i], r_recv.at[i], to_slot).start()

    @pl.when(jnp.logical_not(moves))
    def _():
        for i, (src, dst) in enumerate(row_arrays):
            pltpu.make_async_copy(src, dst.at[y, z, x], r_recv.at[i]).start()

    wide = qkv_ref[...].astype(F32)
    third = wide.shape[1] // 3
    width = third // N_SP
    for t in range(N_SP):
        pieces[t, :, :PAGE] = up_ref[:, t * PAGE : (t + 1) * PAGE].astype(F32)
        for j in range(3):
            at = j * third + t * width
            pieces[t, :, PAGE + j * width : PAGE + (j + 1) * width] = wide[:, at : at + width]
        pieces[t, :, PAGE + third * 3 // N_SP :] = jnp.zeros((PART, PAGE - third * 3 // N_SP), F32)
        pieces[t, 0:1, PAGE + third * 3 // N_SP : PAGE + third * 3 // N_SP + SMALL] = small_ref[...]

    def piece(k):
        t = lax.rem(sp + k, N_SP)
        return send(pieces.at[t], landed.at[sp], p_send.at[k], p_recv.at[sp], (dp, t))

    for k in range(1, N_SP):
        piece(k).start()
    pltpu.make_async_copy(pieces.at[sp], landed.at[sp], p_recv.at[sp]).start()

    tokens = x_ref.shape[0]
    token_arrays = ((x_ref, x_out), (g_ref, g_out))

    def rows_of(s):
        return pl.ds(pl.multiple_of(s * tokens, tokens), tokens)

    def token_copies(kind):
        made = []
        for i, (src, dst) in enumerate(token_arrays):
            if kind == "pass":
                there = dst.at[rows_of(across)]
                made.append(send(there, there, t_send.at[i, 2], t_recv.at[i, across], (dp, sibling)))
            else:
                to, n = (across, 0) if kind == "across" else (sibling, 1)
                made.append(
                    send(src, dst.at[rows_of(sp)], t_send.at[i, n], t_recv.at[i, sp], (dp, to))
                )
        return made

    def token_wait(s):
        for i, (src, dst) in enumerate(token_arrays):
            pltpu.make_async_copy(src, dst.at[rows_of(s)], t_recv.at[i, s]).wait()

    for item in token_copies("across") + token_copies("sibling"):
        item.start()
    for i, (src, dst) in enumerate(token_arrays):
        pltpu.make_async_copy(src, dst.at[rows_of(sp)], t_recv.at[i, sp]).start()

    arrays = ((by_y, up_out), (by_z, qk_out), (by_y, dense_out), (by_z, down_out))

    def stage_a(n, src):
        plane, out = arrays[n]
        mine = out.at[y, z, x]
        return [
            send(
                mine if src is None else src, mine, a_send.at[n, k], a_recv.at[n, plane.mine],
                plane.member(k)[0],
            )
            for k in range(1, GROUP)
        ]

    def stage_b(n):
        plane, out = arrays[n]
        there = plane.block(out, plane.axis)
        return [
            send(there, there, b_send.at[n, k], b_recv.at[n, plane.axis], plane.along(k)[0])
            for k in range(1, NY)
        ]

    for s in range(N_SP):
        pltpu.make_async_copy(pieces.at[s], landed.at[s], p_recv.at[s]).wait()
    for s in range(N_SP):
        tight_wide[s * PART : (s + 1) * PART, :] = landed[s]
    up_tight[...] = tight_wide[:, :PAGE].astype(BF)
    qk_tight[...] = tight_wide[:, PAGE:].astype(BF)
    sources = (up_tight, qk_tight, None, None)
    for n in (0, 1):
        for item in stage_a(n, sources[n]):
            item.start()
        pltpu.make_async_copy(
            sources[n], arrays[n][1].at[y, z, x], a_recv.at[n, arrays[n][0].mine]
        ).start()
    for i, (src, dst) in enumerate(row_arrays):
        pltpu.make_async_copy(src, dst.at[y, z, x], r_recv.at[i]).wait()
        for item in stage_a(2 + i, None):
            item.start()
    for n in range(4):
        plane, out = arrays[n]
        for k in range(0 if n < 2 else 1, GROUP):
            e = lax.rem(plane.mine + k, GROUP)
            there = plane.chunk(out, e)
            pltpu.make_async_copy(there, there, a_recv.at[n, e]).wait()
        for item in stage_b(n):
            item.start()
    token_wait(across)
    for item in token_copies("pass"):
        item.start()
    for s in (sp, sibling, lax.rem(sibling + 2, N_SP)):
        token_wait(s)
    for n in range(4):
        plane, out = arrays[n]
        for k in range(1, NY):
            a = plane.along(k)[1]
            there = plane.block(out, a)
            pltpu.make_async_copy(there, there, b_recv.at[n, a]).wait()

    for kind in ("across", "sibling", "pass"):
        for item in token_copies(kind):
            item.wait_send()
    for k in range(1, N_SP):
        piece(k).wait_send()

    @pl.when(moves)
    def _():
        for i, (src, dst) in enumerate(row_arrays):
            send(src, dst.at[slot_at], r_send.at[i], r_recv.at[i], to_slot).wait_send()

    for n in range(4):
        for item in stage_a(n, sources[n]) + stage_b(n):
            item.wait_send()


def gather_all(x, g, up, qkv, small, down, dense):
    tokens, d_model = x.shape
    dma = pltpu.SemaphoreType.DMA
    anywhere = pl.BlockSpec(memory_space=pl.ANY)
    vmem = pl.BlockSpec(memory_space=pltpu.VMEM)
    grid = (NY, NZ, NX)
    own = PART * N_SP
    return pl.pallas_call(
        gather_kernel,
        out_shape=(
            jax.ShapeDtypeStruct((tokens * N_SP, d_model), BF),
            jax.ShapeDtypeStruct((tokens * N_SP, d_model), BF),
            jax.ShapeDtypeStruct(grid + (own, PAGE), BF),
            jax.ShapeDtypeStruct(grid + (own, PAGE), BF),
            jax.ShapeDtypeStruct(grid + down.shape, BF),
            jax.ShapeDtypeStruct(grid + dense.shape, BF),
        ),
        in_specs=[anywhere, anywhere, vmem, vmem, vmem, anywhere, anywhere],
        out_specs=(anywhere,) * 6,
        scratch_shapes=[
            pltpu.VMEM((N_SP, PART, 2 * PAGE), F32),
            pltpu.VMEM((N_SP, PART, 2 * PAGE), F32),
            pltpu.VMEM((own, 2 * PAGE), F32),
            pltpu.VMEM((own, PAGE), BF),
            pltpu.VMEM((own, PAGE), BF),
            dma((2, 3)),
            dma((2, N_SP)),
            dma((N_SP,)),
            dma((N_SP,)),
            dma((2,)),
            dma((2,)),
            dma((4, GROUP)),
            dma((4, GROUP)),
            dma((4, NY)),
            dma((4, NY)),
        ],
        compiler_params=pltpu.CompilerParams(collective_id=0, has_side_effects=True),
        name="gather_all",
    )(x, g, up, qkv, small, down, dense)


def reduce_kernel(
    up_ref, qk_ref, dense_ref, down_ref, small_ref, out_ref, dx_ref,
    up_out, qkv_out, down_out, dense_out, small_out, hidden_out, dxhat_out,
    up_1, qk_1, dense_1, down_1, small_1,
    up_m, qk_m, dense_m, down_m, small_m,
    up_2, qk_2, dense_2, down_2, small_2,
    token_own, token_in, token_mid, token_far,
    pieces, landed, small_land, down_sum, dense_sum,
    b_send, b_recv, a_send, a_recv, t_own, t_send, t_recv, f_send, f_recv,
    p_send, p_recv, s_send, s_recv, r_send, r_recv,
):
    dp, sp, y, z, x = place()
    to_owner, from_slot = owner_device(dp, sp), slot_device(dp, sp)
    sibling = sp + 1 - 2 * lax.rem(sp, 2)
    across = lax.rem(sp + 2, N_SP)
    greet(from_slot, to_owner)
    by_y, by_z = Plane("y"), Plane("z")
    arrays = (
        (by_y, up_ref, up_1, up_m, up_2),
        (by_z, qk_ref, qk_1, qk_m, qk_2),
        (by_z, down_ref, down_1, down_m, down_2),
        (by_y, dense_ref, dense_1, dense_m, dense_2),
        (by_y, small_ref, small_1, small_m, small_2),
    )

    def stage_1(n):
        plane, src, land = arrays[n][:3]
        made = []
        for k in range(1, NY):
            device, a = plane.along(k)
            made.append(
                send(
                    plane.block(src, a), land.at[plane.axis], b_send.at[n, k],
                    b_recv.at[n, plane.axis], device,
                )
            )
        return made

    def stage_2(n):
        plane, _, _, mid, land = arrays[n]
        made = []
        for k in range(1, GROUP):
            device, e, a, xx = plane.member(k)
            made.append(
                send(
                    mid.at[a, xx], land.at[plane.mine], a_send.at[n, k],
                    a_recv.at[n, plane.mine], device,
                )
            )
        return made

    for n, (plane, src, land, mid, last) in enumerate(arrays):
        for item in stage_1(n):
            item.start()
        pltpu.make_async_copy(
            plane.block(src, plane.axis), land.at[plane.axis], b_recv.at[n, plane.axis]
        ).start()

    token_arrays = (out_ref, dx_ref)
    sib_across = lax.rem(sibling + 2, N_SP)

    def token_pair(i):
        src = token_arrays[i]
        return [
            send(src.at[t], token_in.at[i, n], t_send.at[i, n], t_recv.at[i, n], (dp, sibling))
            for n, t in enumerate((sibling, sib_across))
        ]

    def token_own_copy(i):
        src = token_arrays[i]
        return [
            pltpu.make_async_copy(src.at[t], token_own.at[i, n], t_own.at[i, n])
            for n, t in enumerate((sp, across))
        ]

    def token_far_copy(i):
        return send(token_mid.at[i], token_far.at[i], f_send.at[i], f_recv.at[i], (dp, across))

    for i in range(2):
        for item in token_pair(i) + token_own_copy(i):
            item.start()
    for i in range(2):
        for item in token_own_copy(i):
            item.wait()
        for item in token_pair(i):
            item.wait_recv()
        token_mid[i] = (token_own[i, 1].astype(F32) + token_in[i, 1].astype(F32)).astype(BF)
        token_far_copy(i).start()

    for n, (plane, src, land, mid, last) in enumerate(arrays):
        for a in range(NY):
            pltpu.make_async_copy(plane.block(src, a), land.at[a], b_recv.at[n, a]).wait()
        for a in range(mid.shape[0]):
            for xx in range(NX):
                total = land[0, a, xx].astype(F32)
                for s in range(1, NY):
                    total = total + land[s, a, xx].astype(F32)
                mid[a, xx] = total.astype(mid.dtype)
        for item in stage_2(n):
            item.start()
        own = mid.at[plane.mine // NX, lax.rem(plane.mine, NX)]
        pltpu.make_async_copy(own, last.at[plane.mine], a_recv.at[n, plane.mine]).start()

    def finish(n):
        plane, src, land, mid, last = arrays[n]
        for e in range(GROUP):
            pltpu.make_async_copy(mid.at[0, 0], last.at[e], a_recv.at[n, e]).wait()
        total = last[0].astype(F32)
        for e in range(1, GROUP):
            total = total + last[e].astype(F32)
        return total

    total = finish(0)
    for t in range(N_SP):
        pieces[t, :, :PAGE] = total[t * PART : (t + 1) * PART, :]
    total = finish(1)
    for t in range(N_SP):
        pieces[t, :, PAGE:] = total[t * PART : (t + 1) * PART, :]

    def piece(k):
        t = lax.rem(sp + k, N_SP)
        return send(pieces.at[t], landed.at[sp], p_send.at[k], p_recv.at[sp], (dp, t))

    for k in range(1, N_SP):
        piece(k).start()
    pltpu.make_async_copy(pieces.at[sp], landed.at[sp], p_recv.at[sp]).start()

    down_sum[...] = finish(2)
    dense_sum[...] = finish(3)
    row_arrays = ((down_sum, down_out), (dense_sum, dense_out))
    moves = differs(to_owner, dp, sp)

    @pl.when(moves)
    def _():
        for i, (src, dst) in enumerate(row_arrays):
            send(src, dst, r_send.at[i], r_recv.at[i], to_owner).start()

    @pl.when(jnp.logical_not(moves))
    def _():
        for i, (src, dst) in enumerate(row_arrays):
            pltpu.make_async_copy(src, dst, r_recv.at[i]).start()

    small_land[sp] = finish(4)

    def small_copy(k):
        there = small_land.at[sp]
        return send(
            there, there, s_send.at[k], s_recv.at[sp], (dp, lax.rem(sp + k, N_SP))
        )

    for k in range(1, N_SP):
        small_copy(k).start()

    for i, result in enumerate((hidden_out, dxhat_out)):
        token_far_copy(i).wait()
        result[...] = (
            token_own[i, 0].astype(F32) + token_in[i, 0].astype(F32) + token_far[i].astype(F32)
        )

    for s in range(N_SP):
        pltpu.make_async_copy(pieces.at[s], landed.at[s], p_recv.at[s]).wait()
    third = qkv_out.shape[1] // 3
    width = third // N_SP
    for s in range(N_SP):
        up_out[:, s * PAGE : (s + 1) * PAGE] = landed[s, :, :PAGE]
        block = landed[s, :, PAGE:]
        for j in range(3):
            to = j * third + s * width
            qkv_out[:, to : to + width] = block[:, j * width : (j + 1) * width]
    for k in range(1, N_SP):
        s = lax.rem(sp + k, N_SP)
        pltpu.make_async_copy(small_land.at[s], small_land.at[s], s_recv.at[s]).wait()
    small_out[...] = jnp.sum(small_land[...], 0)
    for i, (src, dst) in enumerate(row_arrays):
        pltpu.make_async_copy(src, dst, r_recv.at[i]).wait()

    @pl.when(moves)
    def _():
        for i, (src, dst) in enumerate(row_arrays):
            send(src, dst, r_send.at[i], r_recv.at[i], to_owner).wait_send()

    for k in range(1, N_SP):
        piece(k).wait_send()
        small_copy(k).wait_send()
    for i in range(2):
        for item in token_pair(i):
            item.wait_send()
    for n in range(len(arrays)):
        for item in stage_1(n) + stage_2(n):
            item.wait_send()


def reduce_all(up, qk, dense, down, small, out, dx):
    dma = pltpu.SemaphoreType.DMA
    anywhere = pl.BlockSpec(memory_space=pl.ANY)
    vmem = pl.BlockSpec(memory_space=pltpu.VMEM)
    chunks = (up, qk, dense, down, small)
    tokens = out.shape[1:]
    first = [pltpu.VMEM((NY, NZ, NX) + item.shape[3:], item.dtype) for item in chunks]
    mid = [pltpu.VMEM((NZ, NX) + item.shape[3:], item.dtype) for item in chunks]
    last = [pltpu.VMEM((GROUP,) + item.shape[3:], item.dtype) for item in chunks]
    return pl.pallas_call(
        reduce_kernel,
        out_shape=(
            jax.ShapeDtypeStruct((PART, N_SP * PAGE), F32),
            jax.ShapeDtypeStruct((PART, 3 * D), F32),
            jax.ShapeDtypeStruct(down.shape[3:], F32),
            jax.ShapeDtypeStruct(dense.shape[3:], F32),
            jax.ShapeDtypeStruct(small.shape[3:], F32),
            jax.ShapeDtypeStruct(tokens, F32),
            jax.ShapeDtypeStruct(tokens, F32),
        ),
        in_specs=[anywhere] * 7,
        out_specs=(vmem,) * 7,
        scratch_shapes=first
        + mid
        + last
        + [
            pltpu.VMEM((2, 2) + tokens, BF),
            pltpu.VMEM((2, 2) + tokens, BF),
            pltpu.VMEM((2,) + tokens, BF),
            pltpu.VMEM((2,) + tokens, BF),
            pltpu.VMEM((N_SP, PART, 2 * PAGE), F32),
            pltpu.VMEM((N_SP, PART, 2 * PAGE), F32),
            pltpu.VMEM((N_SP,) + small.shape[3:], F32),
            pltpu.VMEM(down.shape[3:], F32),
            pltpu.VMEM(dense.shape[3:], F32),
        ]
        + [
            dma((5, NY)),
            dma((5, NY)),
            dma((5, GROUP)),
            dma((5, GROUP)),
            dma((2, 2)),
            dma((2, 2)),
            dma((2, 2)),
            dma((2,)),
            dma((2,)),
            dma((N_SP,)),
            dma((N_SP,)),
            dma((N_SP,)),
            dma((N_SP,)),
            dma((2,)),
            dma((2,)),
        ],
        compiler_params=pltpu.CompilerParams(
            collective_id=1, has_side_effects=True, vmem_limit_bytes=40 * 1024 * 1024
        ),
        name="reduce_all",
    )(up, qk, dense, down, small, out, dx)


def make_local(n_dp, n_sp):
    n_all = n_dp * n_sp
    def local(
        hidden_in,
        cotangent,
        attn_gain,
        attn_shift,
        mlp_gain,
        mlp_shift,
        qkv_weight,
        qkv_bias,
        dense_weight,
        dense_bias,
        up_weight,
        up_bias,
        down_weight,
        down_bias,
    ):
        sp = lax.axis_index("sp")
        d_model = hidden_in.shape[1]
        heads_here = HEADS // n_sp
        width = heads_here * HEAD_DIM
        ff_here = FF // n_sp

        small = (
            attn_gain,
            attn_shift,
            mlp_gain,
            mlp_shift,
            qkv_bias,
            dense_bias,
            up_bias,
            down_bias,
        )
        sizes = [item.shape[0] for item in small]
        part = up_weight.shape[0]
        part = up_weight.shape[0]
        packed = jnp.zeros((SMALL,), F32)
        at = 0
        for item in small:
            size = item.shape[0]
            packed = packed + jnp.pad(item.astype(F32), (at, SMALL - at - size))
            at += size
        x_seq, g_seq, up_t, qk, down_t, dense_t = gather_all(
            hidden_in,
            cotangent,
            up_weight,
            qkv_weight,
            packed.reshape(1, SMALL),
            down_weight,
            dense_weight,
        )
        up_t = up_t.reshape(d_model, ff_here)
        down_t = down_t.reshape(ff_here, d_model)
        dense_t = dense_t.reshape(width, d_model)
        qk = qk.reshape(d_model, PAGE)
        qkv_t = qk[:, : 3 * width]
        packed = qk[::part, 3 * width : 3 * width + SMALL].astype(F32)
        vectors = []
        at = 0
        for size in sizes:
            vectors.append(packed[:, at : at + size].reshape(-1))
            at += size
        gain_1, shift_1, gain_2, shift_2, qkv_add, dense_add, up_add, down_add = vectors
        qkv_add = lax.dynamic_slice_in_dim(qkv_add.reshape(3, n_sp, width), sp, 1, 1).reshape(-1)
        up_add = lax.dynamic_slice_in_dim(up_add, sp * ff_here, ff_here, 0)
        x_seq = x_seq.astype(F32)
        length = x_seq.shape[0]
        xhat, rstd = norm_components(x_seq)
        normed_1 = (xhat * gain_1 + shift_1).astype(BF)
        normed_2 = (xhat * gain_2 + shift_2).astype(BF)

        pre = dot(normed_2, up_t) + up_add
        cdf = 0.5 * (1.0 + lax.erf(pre * 0.7071067811865476))
        act = (pre * cdf).astype(BF)
        out_part = dot(act, down_t)
        pdf = jnp.exp(-0.5 * pre * pre) * 0.3989422804014327
        dpre = (contract_cols(g_seq, down_t) * (cdf + pre * pdf)).astype(BF)
        down_grad = contract_rows(act, g_seq)
        up_grad = contract_rows(normed_2, dpre)
        up_bias_grad = jnp.sum(dpre.astype(F32), 0)
        dnormed_2 = contract_cols(dpre, up_t)

        qkv = (dot(normed_1, qkv_t) + qkv_add).reshape(length, 3, heads_here, HEAD_DIM)
        cosine, sine = rotary_tables(length)
        q = rotate(qkv[:, 0], cosine, sine).astype(BF).transpose(1, 0, 2)
        k = rotate(qkv[:, 1], cosine, sine).astype(BF).transpose(1, 0, 2)
        v = qkv[:, 2].astype(BF).transpose(1, 0, 2)
        dctx = contract_cols(g_seq, dense_t).astype(BF)
        do = dctx.reshape(length, heads_here, HEAD_DIM).transpose(1, 0, 2)
        scale = HEAD_DIM ** (-0.5)
        scores = jnp.einsum("hqd,hkd->hqk", q, k, preferred_element_type=F32) * scale
        where = jnp.arange(length)[:, None] >= jnp.arange(length)[None, :]
        scores = jnp.where(where[None], scores, -1e30)
        top = jnp.max(scores, -1, keepdims=True)
        probs = jnp.exp(scores - top)
        probs = probs / jnp.sum(probs, -1, keepdims=True)
        probs_low = probs.astype(BF)
        ctx = jnp.einsum("hqk,hkd->hqd", probs_low, v, preferred_element_type=F32)
        ctx = ctx.astype(BF).transpose(1, 0, 2).reshape(length, width)
        out_part = out_part + dot(ctx, dense_t)
        dense_grad = contract_rows(ctx, g_seq)
        dprobs = jnp.einsum("hqd,hkd->hqk", do, v, preferred_element_type=F32)
        delta = jnp.sum(probs * dprobs, -1, keepdims=True)
        dscores = (scale * probs * (dprobs - delta)).astype(BF)
        dq = jnp.einsum("hqk,hkd->qhd", dscores, k, preferred_element_type=F32)
        dk = jnp.einsum("hqk,hqd->khd", dscores, q, preferred_element_type=F32)
        dv = jnp.einsum("hqk,hqd->khd", probs_low, do, preferred_element_type=F32)
        dq = dq.astype(BF).astype(F32)
        dk = dk.astype(BF).astype(F32)
        dqkv = jnp.stack(
            [rotate(dq, cosine, -sine), rotate(dk, cosine, -sine), dv], 1
        ).astype(BF).reshape(length, 3 * width)
        qkv_grad = contract_rows(normed_1, dqkv)
        qkv_bias_grad = jnp.sum(dqkv.astype(F32), 0)
        dnormed_1 = contract_cols(dqkv, qkv_t)

        g_here = cotangent.astype(F32)
        zeros_qkv = jnp.zeros((3, n_sp, width), F32)
        qkv_bias_full = lax.dynamic_update_slice(
            zeros_qkv, qkv_bias_grad.reshape(3, 1, width), (0, sp, 0)
        ).reshape(-1)
        up_bias_full = lax.dynamic_update_slice(
            jnp.zeros((FF,), F32), up_bias_grad, (sp * ff_here,)
        )
        full = (
            jnp.sum(dnormed_1 * xhat, 0),
            jnp.sum(dnormed_1, 0),
            jnp.sum(dnormed_2 * xhat, 0),
            jnp.sum(dnormed_2, 0),
            qkv_bias_full,
            jnp.sum(g_here, 0),
            up_bias_full,
        )
        packed = jnp.concatenate([item.reshape(n_all, -1) for item in full], 1)
        packed = jnp.pad(packed, ((0, 0), (0, SMALL - packed.shape[1])))
        packed = jnp.pad(packed.reshape(n_dp, n_sp, SMALL), ((0, 0), (0, -n_sp % 8), (0, 0)))

        here = hidden_in.shape[0]
        grid = (NY, NZ, NX)
        own = part * n_sp
        up_own, qkv_own, down_own, dense_own, packed, out_sum, dxhat = reduce_all(
            up_grad.astype(BF).reshape(grid + (own, ff_here)),
            jnp.pad(qkv_grad.astype(BF), ((0, 0), (0, PAGE - 3 * width))).reshape(
                grid + (own, PAGE)
            ),
            dense_grad.astype(BF).reshape(grid + (part, d_model)),
            down_grad.astype(BF).reshape(grid + (own, d_model)),
            packed.reshape(grid + packed.shape[1:]),
            out_part.astype(BF).reshape(n_sp, here, d_model),
            (dnormed_1 * gain_1 + dnormed_2 * gain_2).astype(BF).reshape(n_sp, here, d_model),
        )
        mine = lax.dynamic_slice_in_dim(packed, sp, 1, 0).reshape(-1)

        x_here = hidden_in.astype(F32)
        hidden_out = (x_here + out_sum + (dense_add + down_add)).astype(BF)
        xhat_here, rstd_here = norm_components(x_here)
        hidden_grad = (
            g_here
            + rstd_here
            * (
                dxhat
                - jnp.mean(dxhat, -1, keepdims=True)
                - xhat_here * jnp.mean(dxhat * xhat_here, -1, keepdims=True)
            )
        ).astype(BF)
        parts = []
        at = 0
        for item in full:
            size = item.size // n_all
            parts.append(mine[at : at + size])
            at += size
        return (
            hidden_out,
            hidden_grad,
            parts[0],
            parts[1],
            parts[2],
            parts[3],
            qkv_own,
            parts[4],
            dense_own,
            parts[5],
            up_own,
            parts[6],
            down_own,
            parts[5],
        )

    return local


def solution(mesh):
    matrix = P(BOTH, None)
    vector = P(BOTH)
    ins = (matrix, matrix) + (vector,) * 4 + (matrix, vector) * 4
    outs = (matrix, matrix) + (vector,) * 4 + (matrix, vector) * 4
    return jax.shard_map(
        make_local(mesh.shape["dp"], mesh.shape["sp"]),
        mesh=mesh,
        in_specs=ins,
        out_specs=outs,
        check_vma=False,
    )
```

```python
import jax
import jax.numpy as jnp
import numpy as np
from jax import lax
from jax.experimental import pallas as pl
from jax.experimental.pallas import tpu as pltpu
from jax.sharding import PartitionSpec as P

D = 768
HEADS = 12
HEAD_DIM = 64
ROT = 16
FF = 3072
BF = jnp.bfloat16
F32 = jnp.float32
BOTH = ("dp", "sp")


def dot(left, right):
    return jnp.dot(left, right, preferred_element_type=F32)


def norm_components(values_in):
    center = jnp.mean(values_in, -1, keepdims=True)
    centered = values_in - center
    spread = jnp.mean(centered * centered, -1, keepdims=True)
    inverse_deviation = lax.rsqrt(spread + 1e-05)
    return (centered * inverse_deviation, inverse_deviation)


MESH = pl.DeviceIdType.MESH
SMALL = 128
PAGE = 768
NY, NZ, NX = 4, 4, 2
GROUP = NZ * NX
N_SP = 4
PART = 6


def place():
    dp, sp = lax.axis_index("dp"), lax.axis_index("sp")
    return dp, sp, dp // GROUP, lax.rem(dp // NX, NZ), lax.rem(dp, NX)


def send(src, dst, send_sem, recv_sem, device):
    return pltpu.make_async_remote_copy(
        src_ref=src,
        dst_ref=dst,
        send_sem=send_sem,
        recv_sem=recv_sem,
        device_id=device,
        device_id_type=MESH,
    )


def index_of(y, z, x):
    return (y * NZ + z) * NX + x


def slot_device(dp, sp):
    line = dp * N_SP + sp
    return lax.rem(line, NY * GROUP), line // (NY * GROUP)


def owner_device(dp, sp):
    line = sp * NY * GROUP + dp
    return line // N_SP, lax.rem(line, N_SP)


def differs(device, dp, sp):
    return jnp.logical_or(device[0] != dp, device[1] != sp)


class Plane:
    def __init__(self, last):
        self.last = last
        dp, sp, y, z, x = place()
        self.sp, self.y, self.z, self.x = sp, y, z, x
        self.mine = (z if last == "y" else y) * NX + x
        self.axis = y if last == "y" else z

    def member(self, k):
        e = lax.rem(self.mine + k, GROUP)
        a, x = e // NX, lax.rem(e, NX)
        y, z = (self.y, a) if self.last == "y" else (a, self.z)
        return (index_of(y, z, x), self.sp), e, a, x

    def along(self, k):
        a = lax.rem(self.axis + k, NY)
        y, z = (a, self.z) if self.last == "y" else (self.y, a)
        return (index_of(y, z, self.x), self.sp), a

    def block(self, ref, a):
        return ref.at[a] if self.last == "y" else ref.at[:, a]

    def chunk(self, ref, e):
        a, x = e // NX, lax.rem(e, NX)
        return ref.at[self.y, a, x] if self.last == "y" else ref.at[a, self.z, x]


def greet(partner_in, partner_out):
    dp, sp, y, z, x = place()
    barrier = pltpu.get_barrier_semaphore()

    def signal(device):
        pl.semaphore_signal(barrier, inc=1, device_id=device, device_id_type=MESH)

    for k in range(1, N_SP):
        signal((dp, lax.rem(sp + k, N_SP)))
    by_y, by_z = Plane("y"), Plane("z")
    for k in range(1, GROUP):
        signal(by_y.member(k)[0])
        signal(by_z.member(k)[0])

    @pl.when(differs(partner_in, dp, sp))
    def _():
        signal(partner_in)

    count = N_SP - 1 + 2 * (GROUP - 1)
    pl.semaphore_wait(barrier, count + jnp.where(differs(partner_out, dp, sp), 1, 0))


def gather_kernel(
    x_ref, g_ref, up_ref, qkv_ref, small_ref, down_ref, dense_ref,
    x_out, g_out, up_out, qk_out, down_out, dense_out,
    pieces, landed, tight_wide, up_tight, qk_tight,
    t_send, t_recv, p_send, p_recv, r_send, r_recv, a_send, a_recv, b_send, b_recv,
):
    dp, sp, y, z, x = place()
    to_slot, from_owner = slot_device(dp, sp), owner_device(dp, sp)
    sibling = sp + 1 - 2 * lax.rem(sp, 2)
    across = lax.rem(sp + 2, N_SP)
    greet(from_owner, to_slot)
    by_y, by_z = Plane("y"), Plane("z")

    row_arrays = ((dense_ref, dense_out), (down_ref, down_out))
    slot = to_slot[0]
    slot_at = (slot // GROUP, lax.rem(slot // NX, NZ), lax.rem(slot, NX))
    moves = differs(to_slot, dp, sp)

    @pl.when(moves)
    def _():
        for i, (src, dst) in enumerate(row_arrays):
            send(src, dst.at[slot_at], r_send.at[i], r_recv.at[i], to_slot).start()

    @pl.when(jnp.logical_not(moves))
    def _():
        for i, (src, dst) in enumerate(row_arrays):
            pltpu.make_async_copy(src, dst.at[y, z, x], r_recv.at[i]).start()

    wide = qkv_ref[...].astype(F32)
    third = wide.shape[1] // 3
    width = third // N_SP
    for t in range(N_SP):
        pieces[t, :, :PAGE] = up_ref[:, t * PAGE : (t + 1) * PAGE].astype(F32)
        for j in range(3):
            at = j * third + t * width
            pieces[t, :, PAGE + j * width : PAGE + (j + 1) * width] = wide[:, at : at + width]
        pieces[t, :, PAGE + third * 3 // N_SP :] = jnp.zeros((PART, PAGE - third * 3 // N_SP), F32)
        pieces[t, 0:1, PAGE + third * 3 // N_SP : PAGE + third * 3 // N_SP + SMALL] = small_ref[...]

    def piece(k):
        t = lax.rem(sp + k, N_SP)
        return send(pieces.at[t], landed.at[sp], p_send.at[k], p_recv.at[sp], (dp, t))

    for k in range(1, N_SP):
        piece(k).start()
    pltpu.make_async_copy(pieces.at[sp], landed.at[sp], p_recv.at[sp]).start()

    tokens = x_ref.shape[0]
    token_arrays = ((x_ref, x_out), (g_ref, g_out))

    def rows_of(s):
        return pl.ds(pl.multiple_of(s * tokens, tokens), tokens)

    def token_copies(kind):
        made = []
        for i, (src, dst) in enumerate(token_arrays):
            if kind == "pass":
                there = dst.at[rows_of(across)]
                made.append(send(there, there, t_send.at[i, 2], t_recv.at[i, across], (dp, sibling)))
            else:
                to, n = (across, 0) if kind == "across" else (sibling, 1)
                made.append(
                    send(src, dst.at[rows_of(sp)], t_send.at[i, n], t_recv.at[i, sp], (dp, to))
                )
        return made

    def token_wait(s):
        for i, (src, dst) in enumerate(token_arrays):
            pltpu.make_async_copy(src, dst.at[rows_of(s)], t_recv.at[i, s]).wait()

    for item in token_copies("across") + token_copies("sibling"):
        item.start()
    for i, (src, dst) in enumerate(token_arrays):
        pltpu.make_async_copy(src, dst.at[rows_of(sp)], t_recv.at[i, sp]).start()

    arrays = ((by_y, up_out), (by_z, qk_out), (by_y, dense_out), (by_z, down_out))

    def stage_a(n, src):
        plane, out = arrays[n]
        mine = out.at[y, z, x]
        return [
            send(
                mine if src is None else src, mine, a_send.at[n, k], a_recv.at[n, plane.mine],
                plane.member(k)[0],
            )
            for k in range(1, GROUP)
        ]

    def stage_b(n):
        plane, out = arrays[n]
        there = plane.block(out, plane.axis)
        return [
            send(there, there, b_send.at[n, k], b_recv.at[n, plane.axis], plane.along(k)[0])
            for k in range(1, NY)
        ]

    for s in range(N_SP):
        pltpu.make_async_copy(pieces.at[s], landed.at[s], p_recv.at[s]).wait()
    for s in range(N_SP):
        tight_wide[s * PART : (s + 1) * PART, :] = landed[s]
    up_tight[...] = tight_wide[:, :PAGE].astype(BF)
    qk_tight[...] = tight_wide[:, PAGE:].astype(BF)
    sources = (up_tight, qk_tight, None, None)
    for n in (0, 1):
        for item in stage_a(n, sources[n]):
            item.start()
        pltpu.make_async_copy(
            sources[n], arrays[n][1].at[y, z, x], a_recv.at[n, arrays[n][0].mine]
        ).start()
    for i, (src, dst) in enumerate(row_arrays):
        pltpu.make_async_copy(src, dst.at[y, z, x], r_recv.at[i]).wait()
        for item in stage_a(2 + i, None):
            item.start()
    for n in range(4):
        plane, out = arrays[n]
        for k in range(0 if n < 2 else 1, GROUP):
            e = lax.rem(plane.mine + k, GROUP)
            there = plane.chunk(out, e)
            pltpu.make_async_copy(there, there, a_recv.at[n, e]).wait()
        for item in stage_b(n):
            item.start()
    token_wait(across)
    for item in token_copies("pass"):
        item.start()
    for s in (sp, sibling, lax.rem(sibling + 2, N_SP)):
        token_wait(s)
    for n in range(4):
        plane, out = arrays[n]
        for k in range(1, NY):
            a = plane.along(k)[1]
            there = plane.block(out, a)
            pltpu.make_async_copy(there, there, b_recv.at[n, a]).wait()

    for kind in ("across", "sibling", "pass"):
        for item in token_copies(kind):
            item.wait_send()
    for k in range(1, N_SP):
        piece(k).wait_send()

    @pl.when(moves)
    def _():
        for i, (src, dst) in enumerate(row_arrays):
            send(src, dst.at[slot_at], r_send.at[i], r_recv.at[i], to_slot).wait_send()

    for n in range(4):
        for item in stage_a(n, sources[n]) + stage_b(n):
            item.wait_send()


def gather_all(x, g, up, qkv, small, down, dense):
    tokens, d_model = x.shape
    dma = pltpu.SemaphoreType.DMA
    anywhere = pl.BlockSpec(memory_space=pl.ANY)
    vmem = pl.BlockSpec(memory_space=pltpu.VMEM)
    grid = (NY, NZ, NX)
    own = PART * N_SP
    return pl.pallas_call(
        gather_kernel,
        out_shape=(
            jax.ShapeDtypeStruct((tokens * N_SP, d_model), BF),
            jax.ShapeDtypeStruct((tokens * N_SP, d_model), BF),
            jax.ShapeDtypeStruct(grid + (own, PAGE), BF),
            jax.ShapeDtypeStruct(grid + (own, PAGE), BF),
            jax.ShapeDtypeStruct(grid + down.shape, BF),
            jax.ShapeDtypeStruct(grid + dense.shape, BF),
        ),
        in_specs=[anywhere, anywhere, vmem, vmem, vmem, anywhere, anywhere],
        out_specs=(anywhere,) * 6,
        scratch_shapes=[
            pltpu.VMEM((N_SP, PART, 2 * PAGE), F32),
            pltpu.VMEM((N_SP, PART, 2 * PAGE), F32),
            pltpu.VMEM((own, 2 * PAGE), F32),
            pltpu.VMEM((own, PAGE), BF),
            pltpu.VMEM((own, PAGE), BF),
            dma((2, 3)),
            dma((2, N_SP)),
            dma((N_SP,)),
            dma((N_SP,)),
            dma((2,)),
            dma((2,)),
            dma((4, GROUP)),
            dma((4, GROUP)),
            dma((4, NY)),
            dma((4, NY)),
        ],
        compiler_params=pltpu.CompilerParams(collective_id=0, has_side_effects=True),
        name="gather_all",
    )(x, g, up, qkv, small, down, dense)


def reduce_kernel(
    up_ref, qk_ref, dense_ref, down_ref, small_ref, out_ref, dx_ref,
    up_out, qkv_out, down_out, dense_out, small_out, hidden_out, dxhat_out,
    up_1, qk_1, dense_1, down_1, small_1,
    up_m, qk_m, dense_m, down_m, small_m,
    up_2, qk_2, dense_2, down_2, small_2,
    token_own, token_in, token_mid, token_far,
    pieces, landed, small_land, down_sum, dense_sum,
    b_send, b_recv, a_send, a_recv, t_own, t_send, t_recv, f_send, f_recv,
    p_send, p_recv, s_send, s_recv, r_send, r_recv,
):
    dp, sp, y, z, x = place()
    to_owner, from_slot = owner_device(dp, sp), slot_device(dp, sp)
    sibling = sp + 1 - 2 * lax.rem(sp, 2)
    across = lax.rem(sp + 2, N_SP)
    greet(from_slot, to_owner)
    by_y, by_z = Plane("y"), Plane("z")
    arrays = (
        (by_y, up_ref, up_1, up_m, up_2),
        (by_z, qk_ref, qk_1, qk_m, qk_2),
        (by_z, down_ref, down_1, down_m, down_2),
        (by_y, dense_ref, dense_1, dense_m, dense_2),
        (by_y, small_ref, small_1, small_m, small_2),
    )

    def stage_1(n):
        plane, src, land = arrays[n][:3]
        made = []
        for k in range(1, NY):
            device, a = plane.along(k)
            made.append(
                send(
                    plane.block(src, a), land.at[plane.axis], b_send.at[n, k],
                    b_recv.at[n, plane.axis], device,
                )
            )
        return made

    def stage_2(n):
        plane, _, _, mid, land = arrays[n]
        made = []
        for k in range(1, GROUP):
            device, e, a, xx = plane.member(k)
            made.append(
                send(
                    mid.at[a, xx], land.at[plane.mine], a_send.at[n, k],
                    a_recv.at[n, plane.mine], device,
                )
            )
        return made

    for n, (plane, src, land, mid, last) in enumerate(arrays):
        for item in stage_1(n):
            item.start()
        pltpu.make_async_copy(
            plane.block(src, plane.axis), land.at[plane.axis], b_recv.at[n, plane.axis]
        ).start()

    token_arrays = (out_ref, dx_ref)
    sib_across = lax.rem(sibling + 2, N_SP)

    def token_pair(i):
        src = token_arrays[i]
        return [
            send(src.at[t], token_in.at[i, n], t_send.at[i, n], t_recv.at[i, n], (dp, sibling))
            for n, t in enumerate((sibling, sib_across))
        ]

    def token_own_copy(i):
        src = token_arrays[i]
        return [
            pltpu.make_async_copy(src.at[t], token_own.at[i, n], t_own.at[i, n])
            for n, t in enumerate((sp, across))
        ]

    def token_far_copy(i):
        return send(token_mid.at[i], token_far.at[i], f_send.at[i], f_recv.at[i], (dp, across))

    for i in range(2):
        for item in token_pair(i) + token_own_copy(i):
            item.start()
    for i in range(2):
        for item in token_own_copy(i):
            item.wait()
        for item in token_pair(i):
            item.wait_recv()
        token_mid[i] = (token_own[i, 1].astype(F32) + token_in[i, 1].astype(F32)).astype(BF)
        token_far_copy(i).start()

    for n, (plane, src, land, mid, last) in enumerate(arrays):
        for a in range(NY):
            pltpu.make_async_copy(plane.block(src, a), land.at[a], b_recv.at[n, a]).wait()
        for a in range(mid.shape[0]):
            for xx in range(NX):
                total = land[0, a, xx].astype(F32)
                for s in range(1, NY):
                    total = total + land[s, a, xx].astype(F32)
                mid[a, xx] = total.astype(mid.dtype)
        for item in stage_2(n):
            item.start()
        own = mid.at[plane.mine // NX, lax.rem(plane.mine, NX)]
        pltpu.make_async_copy(own, last.at[plane.mine], a_recv.at[n, plane.mine]).start()

    def finish(n):
        plane, src, land, mid, last = arrays[n]
        for e in range(GROUP):
            pltpu.make_async_copy(mid.at[0, 0], last.at[e], a_recv.at[n, e]).wait()
        total = last[0].astype(F32)
        for e in range(1, GROUP):
            total = total + last[e].astype(F32)
        return total

    total = finish(0)
    for t in range(N_SP):
        pieces[t, :, :PAGE] = total[t * PART : (t + 1) * PART, :]
    total = finish(1)
    for t in range(N_SP):
        pieces[t, :, PAGE:] = total[t * PART : (t + 1) * PART, :]

    def piece(k):
        t = lax.rem(sp + k, N_SP)
        return send(pieces.at[t], landed.at[sp], p_send.at[k], p_recv.at[sp], (dp, t))

    for k in range(1, N_SP):
        piece(k).start()
    pltpu.make_async_copy(pieces.at[sp], landed.at[sp], p_recv.at[sp]).start()

    down_sum[...] = finish(2)
    dense_sum[...] = finish(3)
    row_arrays = ((down_sum, down_out), (dense_sum, dense_out))
    moves = differs(to_owner, dp, sp)

    @pl.when(moves)
    def _():
        for i, (src, dst) in enumerate(row_arrays):
            send(src, dst, r_send.at[i], r_recv.at[i], to_owner).start()

    @pl.when(jnp.logical_not(moves))
    def _():
        for i, (src, dst) in enumerate(row_arrays):
            pltpu.make_async_copy(src, dst, r_recv.at[i]).start()

    small_land[sp] = finish(4)

    def small_copy(k):
        there = small_land.at[sp]
        return send(
            there, there, s_send.at[k], s_recv.at[sp], (dp, lax.rem(sp + k, N_SP))
        )

    for k in range(1, N_SP):
        small_copy(k).start()

    for i, result in enumerate((hidden_out, dxhat_out)):
        token_far_copy(i).wait()
        result[...] = (
            token_own[i, 0].astype(F32) + token_in[i, 0].astype(F32) + token_far[i].astype(F32)
        )

    for s in range(N_SP):
        pltpu.make_async_copy(pieces.at[s], landed.at[s], p_recv.at[s]).wait()
    third = qkv_out.shape[1] // 3
    width = third // N_SP
    for s in range(N_SP):
        up_out[:, s * PAGE : (s + 1) * PAGE] = landed[s, :, :PAGE]
        block = landed[s, :, PAGE:]
        for j in range(3):
            to = j * third + s * width
            qkv_out[:, to : to + width] = block[:, j * width : (j + 1) * width]
    for k in range(1, N_SP):
        s = lax.rem(sp + k, N_SP)
        pltpu.make_async_copy(small_land.at[s], small_land.at[s], s_recv.at[s]).wait()
    small_out[...] = jnp.sum(small_land[...], 0)
    for i, (src, dst) in enumerate(row_arrays):
        pltpu.make_async_copy(src, dst, r_recv.at[i]).wait()

    @pl.when(moves)
    def _():
        for i, (src, dst) in enumerate(row_arrays):
            send(src, dst, r_send.at[i], r_recv.at[i], to_owner).wait_send()

    for k in range(1, N_SP):
        piece(k).wait_send()
        small_copy(k).wait_send()
    for i in range(2):
        for item in token_pair(i):
            item.wait_send()
    for n in range(len(arrays)):
        for item in stage_1(n) + stage_2(n):
            item.wait_send()


def reduce_all(up, qk, dense, down, small, out, dx):
    dma = pltpu.SemaphoreType.DMA
    anywhere = pl.BlockSpec(memory_space=pl.ANY)
    vmem = pl.BlockSpec(memory_space=pltpu.VMEM)
    chunks = (up, qk, dense, down, small)
    tokens = out.shape[1:]
    first = [pltpu.VMEM((NY, NZ, NX) + item.shape[3:], item.dtype) for item in chunks]
    mid = [pltpu.VMEM((NZ, NX) + item.shape[3:], item.dtype) for item in chunks]
    last = [pltpu.VMEM((GROUP,) + item.shape[3:], item.dtype) for item in chunks]
    return pl.pallas_call(
        reduce_kernel,
        out_shape=(
            jax.ShapeDtypeStruct((PART, N_SP * PAGE), F32),
            jax.ShapeDtypeStruct((PART, 3 * D), F32),
            jax.ShapeDtypeStruct(down.shape[3:], F32),
            jax.ShapeDtypeStruct(dense.shape[3:], F32),
            jax.ShapeDtypeStruct(small.shape[3:], F32),
            jax.ShapeDtypeStruct(tokens, F32),
            jax.ShapeDtypeStruct(tokens, F32),
        ),
        in_specs=[anywhere] * 7,
        out_specs=(vmem,) * 7,
        scratch_shapes=first
        + mid
        + last
        + [
            pltpu.VMEM((2, 2) + tokens, BF),
            pltpu.VMEM((2, 2) + tokens, BF),
            pltpu.VMEM((2,) + tokens, BF),
            pltpu.VMEM((2,) + tokens, BF),
            pltpu.VMEM((N_SP, PART, 2 * PAGE), F32),
            pltpu.VMEM((N_SP, PART, 2 * PAGE), F32),
            pltpu.VMEM((N_SP,) + small.shape[3:], F32),
            pltpu.VMEM(down.shape[3:], F32),
            pltpu.VMEM(dense.shape[3:], F32),
        ]
        + [
            dma((5, NY)),
            dma((5, NY)),
            dma((5, GROUP)),
            dma((5, GROUP)),
            dma((2, 2)),
            dma((2, 2)),
            dma((2, 2)),
            dma((2,)),
            dma((2,)),
            dma((N_SP,)),
            dma((N_SP,)),
            dma((N_SP,)),
            dma((N_SP,)),
            dma((2,)),
            dma((2,)),
        ],
        compiler_params=pltpu.CompilerParams(
            collective_id=1, has_side_effects=True, vmem_limit_bytes=40 * 1024 * 1024
        ),
        name="reduce_all",
    )(up, qk, dense, down, small, out, dx)


BLOCK = 256


def dot_nt(left, right):
    return lax.dot_general(left, right, (((1,), (1,)), ((), ())), preferred_element_type=F32)


def dot_tn(left, right):
    return lax.dot_general(left, right, (((0,), (0,)), ((), ())), preferred_element_type=F32)


def iota(shape, axis):
    return lax.broadcasted_iota(jnp.int32, shape, axis)


def rotary_tables(length):
    half = ROT // 2
    frequency = np.float32(10000.0) ** (np.float32(-2.0) * np.arange(half, dtype=np.float32) / ROT)
    angles = np.arange(length, dtype=np.float32)[:, None] * frequency[None, :].astype(np.float32)
    cosine = np.ones((length, HEAD_DIM), np.float32)
    sine = np.zeros((length, HEAD_DIM), np.float32)
    cosine[:, :half] = cosine[:, half:ROT] = np.cos(angles)
    sine[:, :half] = -np.sin(angles)
    sine[:, half:ROT] = np.sin(angles)
    return jnp.asarray(np.tile(cosine, (1, 2))), jnp.asarray(np.tile(sine, (1, 2)))


def swap_halves(u):
    low = lax.rem(iota(u.shape, 1), 16) < 8
    return jnp.where(low, pltpu.roll(u, 120, 1), pltpu.roll(u, 8, 1))


def column_of(c, sp, kind):
    if kind == "qkv":
        width = D // N_SP
        return (c // width) * D + sp * width + lax.rem(c, width)
    return c + sp * (FF // N_SP) if kind == "up" else c


VECTORS_IN = (
    (0, 6, "", D), (6, 6, "", D), (12, 6, "", D), (18, 6, "", D),
    (24, 18, "qkv", PAGE), (42, 6, "", D), (48, 24, "up", PAGE), (72, 6, "", D),
)
VECTORS_OUT = (
    (0, 6, "", D), (6, 6, "", D), (12, 6, "", D), (18, 6, "", D),
    (24, 18, "qkv", PAGE), (42, 6, "", D), (48, 24, "up", PAGE),
)


def compute_kernel(
    x_ref, g_ref, up_ref, qk_ref, down_ref, dense_ref, cos_ref, sin_ref,
    up_out, qk_out, dense_out, down_out, small_out, out_out, dx_out, bias_out,
    xhat_s, n1_s, n2_s, act_s, dpre_s, dx_s, sum_s, e_s, dqkv_s,
    q_s, k_s, v_s, do_s, kt_s, vt_s, dk_s, dv_s, ctxt_s, dense_wide, dense_s, vec_s,
):
    sp = lax.axis_index("sp")
    length = x_ref.shape[0]
    heads = HEADS // N_SP
    width = heads * HEAD_DIM
    n_own = NY * NZ * NX * N_SP
    steps = length // BLOCK

    pick = (iota((n_own, D), 1) == PART * iota((n_own, D), 0)).astype(BF)
    packed = dot(pick, qk_ref[:, 3 * width : 3 * width + SMALL]).astype(BF)
    for n, (start, each, kind, size) in enumerate(VECTORS_IN):
        lane = column_of(iota((SMALL, size), 1), sp, kind)
        spread = (iota((SMALL, size), 0) == start + lax.rem(lane, each)).astype(BF)
        lane = column_of(iota((n_own, size), 1), sp, kind)
        values = jnp.where(lane // each == iota((n_own, size), 0), dot(packed, spread), 0.0)
        vec_s[n : n + 1, :] = jnp.sum(values, 0, keepdims=True)
    gain_1, shift_1, gain_2, shift_2 = (vec_s[n : n + 1, :] for n in range(4))
    lanes = iota((1, PAGE), 1)
    qkv_add = jnp.where(lanes < 3 * width, vec_s[4:5, :], 0.0)
    up_add = vec_s[6:7, :]
    bias_out[...] = vec_s[5:6, :] + vec_s[7:8, :]
    for e in range(dense_ref.shape[0]):
        dense_wide[e * PART : (e + 1) * PART, :] = dense_ref[e].astype(F32)
    dense_s[...] = dense_wide[...].astype(BF)

    def fold(values):
        return jnp.sum(values.reshape(-1, 8, values.shape[-1]), 0)

    def rows_at(i):
        return pl.ds(pl.multiple_of(i * BLOCK, BLOCK), BLOCK)

    zeros = jnp.zeros((8, D), F32)

    def first(i, sums):
        rows = rows_at(i)
        x = x_ref[rows, :].astype(F32)
        centered = x - jnp.mean(x, -1, keepdims=True)
        xhat = centered * lax.rsqrt(jnp.mean(centered * centered, -1, keepdims=True) + 1e-05)
        xhat_s[rows, :] = xhat
        n1_s[rows, :] = (xhat * gain_1 + shift_1).astype(BF)
        n2 = (xhat * gain_2 + shift_2).astype(BF)
        n2_s[rows, :] = n2
        g = g_ref[rows, :]
        pre = dot(n2, up_ref[...]) + up_add
        cdf = 0.5 * (1.0 + lax.erf(pre * 0.7071067811865476))
        act = (pre * cdf).astype(BF)
        act_s[rows, :] = act
        pdf = jnp.exp(-0.5 * pre * pre) * 0.3989422804014327
        dpre = (dot_nt(g, down_ref[...]) * (cdf + pre * pdf)).astype(BF)
        dpre_s[rows, :] = dpre
        sum_s[rows, :] = dot(act, down_ref[...])
        dn2 = dot_nt(dpre, up_ref[...])
        dx_s[rows, :] = dn2 * gain_2
        bias, gain, shift = sums
        return (bias + fold(dpre.astype(F32)), gain + fold(dn2 * xhat), shift + fold(dn2))

    up_bias, gain_2_grad, shift_2_grad = lax.fori_loop(0, steps, first, (zeros,) * 3)

    @pl.loop(0, steps)
    def _(i):
        rows = rows_at(i)
        y = dot(n1_s[rows, :], qk_ref[...]) + qkv_add
        cosine, sine = cos_ref[rows, :], sin_ref[rows, :]
        turned = []
        for p in range(2 * width // 128):
            u = y[:, p * 128 : (p + 1) * 128]
            turned.append(u * cosine + swap_halves(u) * sine)
        d = dot_nt(g_ref[rows, :], dense_s[...])

        def head(n):
            u = turned[n // 2]
            return u[:, (n % 2) * HEAD_DIM : (n % 2 + 1) * HEAD_DIM]

        for h in range(heads):
            at = 2 * width + h * HEAD_DIM
            q_s[h, rows, :] = head(h).astype(BF)
            k_s[h, rows, :] = head(heads + h).astype(BF)
            v_s[h, rows, :] = y[:, at : at + HEAD_DIM].astype(BF)
            do_s[h, rows, :] = d[:, h * HEAD_DIM : (h + 1) * HEAD_DIM].astype(BF)

    scale = HEAD_DIM ** (-0.5)

    @pl.loop(0, heads)
    def _(h):
        kt_s[...] = k_s[h].astype(F32).T.astype(BF)
        vt_s[...] = v_s[h].astype(F32).T.astype(BF)
        for i in reversed(range(steps)):
            keys = (i + 1) * BLOCK
            rows = slice(i * BLOCK, (i + 1) * BLOCK)
            q, do = q_s[h, rows, :], do_s[h, rows, :]
            scores = dot_nt(k_s[h, :keys, :], q) * scale
            hidden = iota((BLOCK, BLOCK), 0) > iota((BLOCK, BLOCK), 1)
            corner = jnp.where(hidden, -1e30, scores[i * BLOCK :, :])
            if i:
                scores = jnp.concatenate([scores[: i * BLOCK, :], corner], 0)
            else:
                scores = corner
            expo = jnp.exp(scores - jnp.max(scores, 0, keepdims=True))
            probs = expo * (1.0 / jnp.sum(expo, 0, keepdims=True))
            low = probs.astype(BF)
            ctxt_s[h, :, rows] = dot(vt_s[:, :keys], low).astype(BF)
            dprobs = dot_nt(v_s[h, :keys, :], do)
            delta = jnp.sum(probs * dprobs, 0, keepdims=True)
            dscores = (probs * (dprobs - delta) * scale).astype(BF)
            dq = dot(kt_s[:, :keys], dscores)
            e_s[h, rows, :] = dq.T
            dk = dot(dscores, q)
            dv = dot(low, do)
            if i == steps - 1:
                dk_s[h] = dk
                dv_s[h] = dv
            else:
                dk_s[h, :keys, :] += dk
                dv_s[h, :keys, :] += dv

    ctxt = ctxt_s[...].reshape(width, length)

    def last(i, sums):
        rows = rows_at(i)
        cosine, sine = cos_ref[rows, :], sin_ref[rows, :]
        parts = [ref[h, rows, :] for ref in (e_s, dk_s, dv_s) for h in range(heads)]
        for p in range(2 * width // 128):
            u = jnp.concatenate(parts[2 * p : 2 * p + 2], 1).astype(BF).astype(F32)
            dqkv_s[rows, p * 128 : (p + 1) * 128] = (u * cosine - swap_halves(u) * sine).astype(BF)
        rest = jnp.concatenate(
            parts[2 * heads :] + [jnp.zeros((BLOCK, PAGE - 3 * width), F32)], 1
        )
        dqkv_s[rows, 2 * width :] = rest.astype(BF)
        dqkv = dqkv_s[rows, :]
        dn1 = dot_nt(dqkv, qk_ref[...])
        dx_out[rows, :] = (dx_s[rows, :] + dn1 * gain_1).astype(BF)
        bias, gain, shift = sums
        return (
            bias + fold(dqkv.astype(F32)),
            gain + fold(dn1 * xhat_s[rows, :]),
            shift + fold(dn1),
        )

    qkv_bias, gain_1_grad, shift_1_grad = lax.fori_loop(0, steps, last, (zeros,) * 3)
    for i in range(steps):
        rows = slice(i * BLOCK, (i + 1) * BLOCK)
        out_out[rows, :] = (sum_s[rows, :] + dot_tn(ctxt[:, rows], dense_s[...])).astype(BF)

    @pl.loop(0, D // BLOCK)
    def _(i):
        cols = rows_at(i)
        up_out[:, cols] = dot_tn(n2_s[...], dpre_s[:, cols]).astype(BF)
        down_out[:, cols] = dot_tn(act_s[...], g_ref[:, cols]).astype(BF)
        qk_out[:, cols] = dot_tn(n1_s[...], dqkv_s[:, cols]).astype(BF)

    dense_grad = dot(ctxt, g_ref[...])
    for e in range(dense_out.shape[0]):
        dense_out[e] = dense_grad[e * PART : (e + 1) * PART, :].astype(BF)

    here = length // N_SP
    g_here = g_ref[pl.ds(pl.multiple_of(sp * here, here), here), :].astype(F32)
    n_rows = 2 * n_own
    values = (
        gain_1_grad, shift_1_grad, gain_2_grad, shift_2_grad, qkv_bias, fold(g_here), up_bias
    )
    result = jnp.zeros((n_rows, SMALL), F32)
    for (start, each, kind, size), item in zip(VECTORS_OUT, values):
        vector = jnp.sum(item, 0, keepdims=True)
        lane = column_of(iota((n_rows, size), 1), sp, kind)
        row = iota((n_rows, size), 0)
        mine = jnp.logical_and(lane // each == row // 8 * N_SP + lax.rem(row, 8), lax.rem(row, 8) < N_SP)
        if kind == "qkv":
            mine = jnp.logical_and(mine, iota((n_rows, size), 1) < 3 * width)
        rest = jnp.where(mine, vector, 0.0)
        lane = column_of(iota((size, SMALL), 0), sp, kind)
        gather = (iota((size, SMALL), 1) == start + lax.rem(lane, each)).astype(BF)
        for _ in range(3):
            piece = rest.astype(BF)
            result = result + dot(piece, gather)
            rest = rest - piece.astype(F32)
    small_out[...] = result


def compute_all(x, g, up, qk, down, dense):
    length = x.shape[0]
    heads = HEADS // N_SP
    width = heads * HEAD_DIM
    n_dp = NY * NZ * NX
    cosine, sine = rotary_tables(length)
    vmem = pl.BlockSpec(memory_space=pltpu.VMEM)

    def array(shape, kind):
        return pltpu.VMEM(shape, kind)

    return pl.pallas_call(
        compute_kernel,
        out_shape=(
            jax.ShapeDtypeStruct((D, PAGE), BF),
            jax.ShapeDtypeStruct((D, PAGE), BF),
            jax.ShapeDtypeStruct((n_dp, PART, D), BF),
            jax.ShapeDtypeStruct((PAGE, D), BF),
            jax.ShapeDtypeStruct((n_dp * 8, SMALL), F32),
            jax.ShapeDtypeStruct((length, D), BF),
            jax.ShapeDtypeStruct((length, D), BF),
            jax.ShapeDtypeStruct((1, D), F32),
        ),
        in_specs=[vmem] * 8,
        out_specs=(vmem,) * 8,
        scratch_shapes=[
            array((length, D), F32),
            array((length, D), BF),
            array((length, D), BF),
            array((length, PAGE), BF),
            array((length, PAGE), BF),
            array((length, D), F32),
            array((length, D), F32),
            array((heads, length, HEAD_DIM), F32),
            array((length, PAGE), BF),
            array((heads, length, HEAD_DIM), BF),
            array((heads, length, HEAD_DIM), BF),
            array((heads, length, HEAD_DIM), BF),
            array((heads, length, HEAD_DIM), BF),
            array((HEAD_DIM, length), BF),
            array((HEAD_DIM, length), BF),
            array((heads, length, HEAD_DIM), F32),
            array((heads, length, HEAD_DIM), F32),
            array((heads, HEAD_DIM, length), BF),
            array((width, D), F32),
            array((width, D), BF),
            array((8, PAGE), F32),
        ],
        compiler_params=pltpu.CompilerParams(vmem_limit_bytes=58 * 1024 * 1024),
        cost_estimate=pl.CostEstimate(
            flops=14_000_000_000, bytes_accessed=16_000_000, transcendentals=6_000_000
        ),
        name="compute_all",
    )(x, g, up, qk, down, dense, cosine, sine)


def local(
    hidden_in,
    cotangent,
    attn_gain,
    attn_shift,
    mlp_gain,
    mlp_shift,
    qkv_weight,
    qkv_bias,
    dense_weight,
    dense_bias,
    up_weight,
    up_bias,
    down_weight,
    down_bias,
):
    sp = lax.axis_index("sp")
    small = (
        attn_gain,
        attn_shift,
        mlp_gain,
        mlp_shift,
        qkv_bias,
        dense_bias,
        up_bias,
        down_bias,
    )
    packed = jnp.zeros((SMALL,), F32)
    at = 0
    for item in small:
        size = item.shape[0]
        packed = packed + jnp.pad(item.astype(F32), (at, SMALL - at - size))
        at += size
    x_seq, g_seq, up_t, qk, down_t, dense_t = gather_all(
        hidden_in,
        cotangent,
        up_weight,
        qkv_weight,
        packed.reshape(1, SMALL),
        down_weight,
        dense_weight,
    )
    n_dp = NY * NZ * NX
    up_grad, qk_grad, dense_grad, down_grad, packed, out_part, dxhat, bias = compute_all(
        x_seq,
        g_seq,
        up_t.reshape(D, PAGE),
        qk.reshape(D, PAGE),
        down_t.reshape(PAGE, D),
        dense_t.reshape(n_dp, PART, D),
    )
    here = hidden_in.shape[0]
    grid = (NY, NZ, NX)
    up_own, qkv_own, down_own, dense_own, packed, out_sum, dxhat = reduce_all(
        up_grad.reshape(grid + (PART * N_SP, PAGE)),
        qk_grad.reshape(grid + (PART * N_SP, PAGE)),
        dense_grad.reshape(grid + (PART, D)),
        down_grad.reshape(grid + (PART * N_SP, D)),
        packed.reshape(grid + (8, SMALL)),
        out_part.reshape(N_SP, here, D),
        dxhat.reshape(N_SP, here, D),
    )
    mine = lax.dynamic_slice_in_dim(packed, sp, 1, 0).reshape(-1)
    x_here = hidden_in.astype(F32)
    hidden_out = (x_here + out_sum + bias).astype(BF)
    xhat, rstd = norm_components(x_here)
    hidden_grad = (
        cotangent.astype(F32)
        + rstd
        * (
            dxhat
            - jnp.mean(dxhat, -1, keepdims=True)
            - xhat * jnp.mean(dxhat * xhat, -1, keepdims=True)
        )
    ).astype(BF)
    parts = [mine[start : start + each] for start, each, _, _ in VECTORS_OUT]
    return (
        hidden_out,
        hidden_grad,
        parts[0],
        parts[1],
        parts[2],
        parts[3],
        qkv_own,
        parts[4],
        dense_own,
        parts[5],
        up_own,
        parts[6],
        down_own,
        parts[5],
    )


def solution(mesh):
    matrix = P(BOTH, None)
    vector = P(BOTH)
    split = (matrix, matrix) + (vector,) * 4 + (matrix, vector) * 4
    return jax.shard_map(local, mesh=mesh, in_specs=split, out_specs=split, check_vma=False)
```

```python
import functools
import types

import jax
import jax.numpy as jnp
import numpy as np
from jax import lax
from jax.experimental import pallas as pl
from jax.experimental.pallas import tpu as pltpu
from jax.sharding import PartitionSpec as P

D = 768
HEADS = 12
HEAD_DIM = 64
ROT = 16
FF = 3072
BF = jnp.bfloat16
F32 = jnp.float32
BOTH = ("dp", "sp")


def dot(left, right):
    return jnp.dot(left, right, preferred_element_type=F32)


MESH = pl.DeviceIdType.MESH
SMALL = 128
PAGE = 768
NY, NZ, NX = 4, 4, 2
GROUP = NZ * NX
N_SP = 4
PART = 6


def place():
    dp, sp = lax.axis_index("dp"), lax.axis_index("sp")
    return dp, sp, dp // GROUP, lax.rem(dp // NX, NZ), lax.rem(dp, NX)


def send(src, dst, send_sem, recv_sem, device):
    return pltpu.make_async_remote_copy(
        src_ref=src,
        dst_ref=dst,
        send_sem=send_sem,
        recv_sem=recv_sem,
        device_id=device,
        device_id_type=MESH,
    )


def index_of(y, z, x):
    return (y * NZ + z) * NX + x


def slot_device(dp, sp):
    line = dp * N_SP + sp
    return lax.rem(line, NY * GROUP), line // (NY * GROUP)


def owner_device(dp, sp):
    line = sp * NY * GROUP + dp
    return line // N_SP, lax.rem(line, N_SP)


def differs(device, dp, sp):
    return jnp.logical_or(device[0] != dp, device[1] != sp)


class Plane:
    def __init__(self, last):
        self.last = last
        dp, sp, y, z, x = place()
        self.sp, self.y, self.z, self.x = sp, y, z, x
        self.mine = (z if last == "y" else y) * NX + x
        self.axis = y if last == "y" else z

    def member(self, k):
        e = lax.rem(self.mine + k, GROUP)
        a, x = e // NX, lax.rem(e, NX)
        y, z = (self.y, a) if self.last == "y" else (a, self.z)
        return (index_of(y, z, x), self.sp), e, a, x

    def along(self, k):
        a = lax.rem(self.axis + k, NY)
        y, z = (a, self.z) if self.last == "y" else (self.y, a)
        return (index_of(y, z, self.x), self.sp), a

    def block(self, ref, a):
        return ref.at[a] if self.last == "y" else ref.at[:, a]

    def chunk(self, ref, e):
        a, x = e // NX, lax.rem(e, NX)
        return ref.at[self.y, a, x] if self.last == "y" else ref.at[a, self.z, x]


def greet(*partners):
    dp, sp, y, z, x = place()
    barrier = pltpu.get_barrier_semaphore()

    def signal(device):
        pl.semaphore_signal(barrier, inc=1, device_id=device, device_id_type=MESH)

    for k in range(1, N_SP):
        signal((dp, lax.rem(sp + k, N_SP)))
    by_y, by_z = Plane("y"), Plane("z")
    for k in range(1, GROUP):
        signal(by_y.member(k)[0])
        signal(by_z.member(k)[0])

    @pl.when(differs(partners[0], dp, sp))
    def _():
        for partner in partners:
            signal(partner)

    count = N_SP - 1 + 2 * (GROUP - 1)
    more = jnp.where(differs(partners[0], dp, sp), len(partners), 0)
    pl.semaphore_wait(barrier, count + more)


BLOCK = 256


def dot_nt(left, right):
    return lax.dot_general(left, right, (((1,), (1,)), ((), ())), preferred_element_type=F32)


def dot_tn(left, right):
    return lax.dot_general(left, right, (((0,), (0,)), ((), ())), preferred_element_type=F32)


def iota(shape, axis):
    return lax.broadcasted_iota(jnp.int32, shape, axis)


def rotary_tables(length):
    half = ROT // 2
    frequency = np.float32(10000.0) ** (np.float32(-2.0) * np.arange(half, dtype=np.float32) / ROT)
    angles = np.arange(length, dtype=np.float32)[:, None] * frequency[None, :].astype(np.float32)
    cosine = np.ones((length, HEAD_DIM), np.float32)
    sine = np.zeros((length, HEAD_DIM), np.float32)
    cosine[:, :half] = cosine[:, half:ROT] = np.cos(angles)
    sine[:, :half] = -np.sin(angles)
    sine[:, half:ROT] = np.sin(angles)
    return jnp.asarray(np.tile(cosine, (1, 2))), jnp.asarray(np.tile(sine, (1, 2)))


def swap_halves(u):
    low = lax.rem(iota(u.shape, 1), 16) < 8
    return jnp.where(low, pltpu.roll(u, 120, 1), pltpu.roll(u, 8, 1))


def column_of(c, sp, kind):
    if kind == "qkv":
        width = D // N_SP
        return (c // width) * D + sp * width + lax.rem(c, width)
    return c + sp * (FF // N_SP) if kind == "up" else c


VECTORS_IN = (
    (0, 6, "", D), (6, 6, "", D), (12, 6, "", D), (18, 6, "", D),
    (24, 18, "qkv", PAGE), (42, 6, "", D), (48, 24, "up", PAGE), (72, 6, "", D),
)
VECTORS_OUT = (
    (0, 6, "", D), (6, 6, "", D), (12, 6, "", D), (18, 6, "", D),
    (24, 18, "qkv", PAGE), (42, 6, "", D), (48, 24, "up", PAGE),
)


QK = 640


def layer_kernel(names, *refs):
    r = types.SimpleNamespace(**dict(zip(names, refs)))
    dp, sp, y, z, x = place()
    to_slot, to_owner = slot_device(dp, sp), owner_device(dp, sp)
    sibling = sp + 1 - 2 * lax.rem(sp, 2)
    across = lax.rem(sp + 2, N_SP)
    sib_across = lax.rem(sibling + 2, N_SP)
    moves = differs(to_slot, dp, sp)
    stays = jnp.logical_not(moves)
    by_y, by_z = Plane("y"), Plane("z")
    length = r.x_all.shape[0]
    tokens = length // N_SP
    heads = HEADS // N_SP
    width = heads * HEAD_DIM
    n_own = NY * NZ * NX * N_SP
    steps = length // BLOCK
    slot = to_slot[0]
    slot_at = (slot // GROUP, lax.rem(slot // NX, NZ), lax.rem(slot, NX))

    def local_wait(ref, sem):
        pltpu.make_async_copy(ref, ref, sem).wait()

    def rows_of(s):
        return pl.ds(pl.multiple_of(s * tokens, tokens), tokens)

    def rows_at(i):
        return pl.ds(pl.multiple_of(i * BLOCK, BLOCK), BLOCK)

    greet(to_slot, to_owner)

    row_arrays = ((r.down_ref, r.down_all), (r.dense_ref, r.dense_all))

    def row_copies():
        return [
            send(src, dst.at[slot_at], r.r_send.at[i], r.r_recv.at[i], to_slot)
            for i, (src, dst) in enumerate(row_arrays)
        ]

    @pl.when(moves)
    def _():
        for item in row_copies():
            item.start()

    @pl.when(stays)
    def _():
        for i, (src, dst) in enumerate(row_arrays):
            pltpu.make_async_copy(src, dst.at[y, z, x], r.r_recv.at[i]).start()

    end = PAGE + 3 * width
    wide = r.qkv_ref[...].astype(F32)
    for t in range(N_SP):
        r.pieces[t, :, :PAGE] = r.up_ref[:, t * PAGE : (t + 1) * PAGE].astype(F32)
        for j in range(3):
            at = j * D + t * width
            r.pieces[t, :, PAGE + j * width : PAGE + (j + 1) * width] = wide[:, at : at + width]
        r.pieces[t, :, end : PAGE + QK] = jnp.zeros((PART, PAGE + QK - end), F32)
        r.pieces[t, 0:1, PAGE + QK :] = r.small_ref[...]
        r.pieces[t, 1:, PAGE + QK :] = jnp.zeros((PART - 1, SMALL), F32)

    def piece(k):
        t = lax.rem(sp + k, N_SP)
        return send(r.pieces.at[t], r.landed.at[sp], r.p_send.at[k], r.p_recv.at[sp], (dp, t))

    for k in range(1, N_SP):
        piece(k).start()
    pltpu.make_async_copy(r.pieces.at[sp], r.landed.at[sp], r.p_recv.at[sp]).start()

    token_arrays = ((r.x_ref, r.x_all), (r.g_ref, r.g_all))

    def token_copies(kind):
        made = []
        for i, (src, dst) in enumerate(token_arrays):
            if kind == "pass":
                there = dst.at[rows_of(across)]
                pair = (r.t_send.at[i, 2], r.t_recv.at[i, across])
                made.append(send(there, there, *pair, (dp, sibling)))
            else:
                to, n = (across, 0) if kind == "across" else (sibling, 1)
                pair = (r.t_send.at[i, n], r.t_recv.at[i, sp])
                made.append(send(src, dst.at[rows_of(sp)], *pair, (dp, to)))
        return made

    def token_wait(s):
        for i, (src, dst) in enumerate(token_arrays):
            pltpu.make_async_copy(src, dst.at[rows_of(s)], r.t_recv.at[i, s]).wait()

    for item in token_copies("across") + token_copies("sibling"):
        item.start()
    for i, (src, dst) in enumerate(token_arrays):
        pltpu.make_async_copy(src, dst.at[rows_of(sp)], r.t_recv.at[i, sp]).start()

    SMALLS, UP, DOWN, QKV, DENSE = range(5)
    gathered = (
        (by_y, r.small_all), (by_y, r.up_all), (by_z, r.down_all), (by_z, r.qk_all),
        (by_y, r.dense_all),
    )

    def stage_a(n):
        plane, out = gathered[n]
        mine = out.at[y, z, x]
        return [
            send(mine, mine, r.a_send.at[n, k], r.a_recv.at[n, plane.mine], plane.member(k)[0])
            for k in range(1, GROUP)
        ]

    def stage_b(n):
        plane, out = gathered[n]
        there = plane.block(out, plane.axis)
        return [
            send(there, there, r.b_send.at[n, k], r.b_recv.at[n, plane.axis], plane.along(k)[0])
            for k in range(1, NY)
        ]

    def start_a(n):
        for item in stage_a(n):
            item.start()

    def start_b(n):
        plane, out = gathered[n]
        for k in range(1, GROUP):
            e = lax.rem(plane.mine + k, GROUP)
            local_wait(plane.chunk(out, e), r.a_recv.at[n, e])
        for item in stage_b(n):
            item.start()

    def wait_b(n):
        plane, out = gathered[n]
        for k in range(1, NY):
            a = plane.along(k)[1]
            local_wait(plane.block(out, a), r.b_recv.at[n, a])

    for s in range(N_SP):
        local_wait(r.landed.at[s], r.p_recv.at[s])
    for s in range(N_SP):
        r.tight[s * PART : (s + 1) * PART, :] = r.landed[s]
    r.small_all[y, z, x] = jnp.zeros((8, SMALL), F32)
    for s in range(N_SP):
        r.small_all[y, z, x, s : s + 1, :] = r.landed[s, 0:1, PAGE + QK :]
    r.up_all[y, z, x] = r.tight[:, :PAGE].astype(BF)
    r.qk_all[y, z, x] = r.tight[:, PAGE : PAGE + QK].astype(BF)
    start_a(SMALLS)
    start_a(UP)
    local_wait(r.down_all.at[y, z, x], r.r_recv.at[0])
    start_a(DOWN)
    local_wait(r.dense_all.at[y, z, x], r.r_recv.at[1])
    start_b(SMALLS)
    start_b(UP)
    start_b(DOWN)
    token_wait(across)
    for item in token_copies("pass"):
        item.start()
    start_a(QKV)
    start_a(DENSE)

    wait_b(SMALLS)
    packed = r.small_all[...].reshape(2 * n_own, SMALL).astype(BF)
    n_rows = 2 * n_own

    def owner_rows(size):
        row = iota((n_rows, size), 0)
        inside = lax.rem(row, 8)
        return jnp.where(inside < N_SP, row // 8 * N_SP + inside, -1)

    for n, (start, each, kind, size) in enumerate(VECTORS_IN):
        lane = column_of(iota((SMALL, size), 1), sp, kind)
        spread = (iota((SMALL, size), 0) == start + lax.rem(lane, each)).astype(BF)
        lane = column_of(iota((n_rows, size), 1), sp, kind)
        values = jnp.where(lane // each == owner_rows(size), dot(packed, spread), 0.0)
        r.vec_s[n : n + 1, :] = jnp.sum(values, 0, keepdims=True)
    gain_1, shift_1, gain_2, shift_2 = (r.vec_s[n : n + 1, :] for n in range(4))
    qkv_add = r.vec_s[4:5, :QK]
    up_add = r.vec_s[6:7, :]
    bias = r.vec_s[5:6, :] + r.vec_s[7:8, :]

    def fold(values):
        return jnp.sum(values.reshape(-1, 8, values.shape[-1]), 0)

    for s in (sp, sibling, sib_across):
        token_wait(s)

    @pl.loop(0, steps)
    def _(i):
        rows = rows_at(i)
        values = r.x_all[rows, :].astype(F32)
        centered = values - jnp.mean(values, -1, keepdims=True)
        xhat = centered * lax.rsqrt(jnp.mean(centered * centered, -1, keepdims=True) + 1e-05)
        r.xhat_s[rows, :] = xhat
        r.n1_s[rows, :] = (xhat * gain_1 + shift_1).astype(BF)
        r.n2_s[rows, :] = (xhat * gain_2 + shift_2).astype(BF)

    def join(src, dst):
        @pl.loop(0, NY * NZ)
        def _(i):
            a, b = i // NZ, lax.rem(i, NZ)
            pair = [src[a, b, e].astype(F32) for e in range(NX)]
            own = pair[0].shape[0] * NX
            dst[pl.ds(pl.multiple_of(i * own, own), own), :] = jnp.concatenate(pair, 0).astype(BF)

    start_b(QKV)
    start_b(DENSE)
    wait_b(UP)
    join(r.up_all, r.up_s)
    wait_b(DOWN)
    join(r.down_all, r.down_s)

    zeros = jnp.zeros((8, D), F32)

    def first(i, sums):
        rows = rows_at(i)
        g = r.g_all[rows, :]
        pre = dot(r.n2_s[rows, :], r.up_s[...]) + up_add
        cdf = 0.5 * (1.0 + lax.erf(pre * 0.7071067811865476))
        act = (pre * cdf).astype(BF)
        r.act_s[rows, :] = act
        pdf = jnp.exp(-0.5 * pre * pre) * 0.3989422804014327
        dpre = (dot_nt(g, r.down_s[...]) * (cdf + pre * pdf)).astype(BF)
        r.dpre_s[rows, :] = dpre
        r.sum_s[rows, :] = dot(act, r.down_s[...])
        dn2 = dot_nt(dpre, r.up_s[...])
        r.dx_s[rows, :] = dn2 * gain_2
        one, two, three = sums
        return (
            one + fold(dpre.astype(F32)),
            two + fold(dn2 * r.xhat_s[rows, :]),
            three + fold(dn2),
        )

    up_bias, gain_2_grad, shift_2_grad = lax.fori_loop(0, steps, first, (zeros,) * 3)

    half = D // 2
    in_half = half // (PART * N_SP)

    def weight_grad(left, right, out):
        @pl.loop(0, 2)
        def _(i):
            lanes = pl.ds(pl.multiple_of(i * half, half), half)
            value = dot_tn(left[:, lanes], right[...])
            own = PART * N_SP
            for c in range(in_half):
                at = (i * (NY // 2) + c // GROUP, c // NX % NZ, c % NX)
                out[at[0], at[1], at[2]] = value[c * own : (c + 1) * own, :].astype(BF)

    reduced = (
        (by_y, r.small_g, r.small_1, r.small_m, r.small_2),
        (by_y, r.up_g, r.up_1, r.up_m, r.up_2),
        (by_z, r.down_g, r.down_1, r.down_m, r.down_2),
        (by_z, r.qk_g, r.qk_1, r.qk_m, r.qk_2),
        (by_y, r.dense_g, r.dense_1, r.dense_m, r.dense_2),
    )

    def stage_1(n):
        plane, src, land = reduced[n][:3]
        made = []
        for k in range(1, NY):
            device, a = plane.along(k)
            pair = (r.e_send.at[n, k], r.e_recv.at[n, plane.axis])
            made.append(send(plane.block(src, a), land.at[plane.axis], *pair, device))
        return made

    def stage_2(n):
        plane, _, _, mid, land = reduced[n]
        made = []
        for k in range(1, GROUP):
            device, e, a, xx = plane.member(k)
            pair = (r.f_send.at[n, k], r.f_recv.at[n, plane.mine])
            made.append(send(mid.at[a, xx], land.at[plane.mine], *pair, device))
        return made

    def start_1(n):
        for item in stage_1(n):
            item.start()

    def start_2(n):
        plane, src, land, mid, _ = reduced[n]
        for k in range(1, NY):
            a = plane.along(k)[1]
            local_wait(land.at[a], r.e_recv.at[n, a])

        @pl.loop(0, GROUP)
        def _(e):
            a, xx = e // NX, lax.rem(e, NX)
            own = src[plane.axis, a, xx] if plane.last == "y" else src[a, plane.axis, xx]
            total = own.astype(F32)
            for k in range(1, NY):
                total = total + land[lax.rem(plane.axis + k, NY), a, xx].astype(F32)
            mid[a, xx] = total.astype(mid.dtype)

        for item in stage_2(n):
            item.start()

    def finish(n):
        plane, _, _, mid, land = reduced[n]
        for k in range(1, GROUP):
            e = lax.rem(plane.mine + k, GROUP)
            local_wait(land.at[e], r.f_recv.at[n, e])
        total = mid[plane.mine // NX, lax.rem(plane.mine, NX)].astype(F32)
        for k in range(1, GROUP):
            total = total + land[lax.rem(plane.mine + k, GROUP)].astype(F32)
        return total

    weight_grad(r.act_s, r.g_all, r.down_g)
    start_1(DOWN)
    weight_grad(r.n2_s, r.dpre_s, r.up_g)
    start_1(UP)

    wait_b(QKV)
    join(r.qk_all, r.qk_s)
    wait_b(DENSE)
    for e in range(NY * NZ * NX):
        r.dense_wide[e * PART : (e + 1) * PART, :] = r.dense_all[
            e // GROUP, e // NX % NZ, e % NX
        ].astype(F32)
    r.dense_s[...] = r.dense_wide[...].astype(BF)

    @pl.loop(0, steps)
    def _(i):
        rows = rows_at(i)
        y_rows = dot(r.n1_s[rows, :], r.qk_s[...]) + qkv_add
        cosine, sine = r.cos_ref[rows, :], r.sin_ref[rows, :]
        turned = []
        for p in range(2 * width // 128):
            u = y_rows[:, p * 128 : (p + 1) * 128]
            turned.append(u * cosine + swap_halves(u) * sine)
        d = dot_nt(r.g_all[rows, :], r.dense_s[...])

        def head(n):
            u = turned[n // 2]
            return u[:, (n % 2) * HEAD_DIM : (n % 2 + 1) * HEAD_DIM]

        for h in range(heads):
            at = 2 * width + h * HEAD_DIM
            r.q_s[h, rows, :] = head(h).astype(BF)
            r.k_s[h, rows, :] = head(heads + h).astype(BF)
            r.v_s[h, rows, :] = y_rows[:, at : at + HEAD_DIM].astype(BF)
            r.do_s[h, rows, :] = d[:, h * HEAD_DIM : (h + 1) * HEAD_DIM].astype(BF)

    scale = HEAD_DIM ** (-0.5)

    def attend(h):
        r.kt_s[...] = r.k_s[h].astype(F32).T.astype(BF)
        r.vt_s[...] = r.v_s[h].astype(F32).T.astype(BF)
        for i in reversed(range(steps)):
            keys = (i + 1) * BLOCK
            rows = slice(i * BLOCK, (i + 1) * BLOCK)
            q, do = r.q_s[h, rows, :], r.do_s[h, rows, :]
            scores = dot_nt(r.k_s[h, :keys, :], q) * scale
            hidden = iota((BLOCK, BLOCK), 0) > iota((BLOCK, BLOCK), 1)
            corner = jnp.where(hidden, -1e30, scores[i * BLOCK :, :])
            scores = jnp.concatenate([scores[: i * BLOCK, :], corner], 0) if i else corner
            expo = jnp.exp(scores - jnp.max(scores, 0, keepdims=True))
            probs = expo * (1.0 / jnp.sum(expo, 0, keepdims=True))
            low = probs.astype(BF)
            r.ctxt_s[h, :, rows] = dot(r.vt_s[:, :keys], low).astype(BF)
            dprobs = dot_nt(r.v_s[h, :keys, :], do)
            delta = jnp.sum(probs * dprobs, 0, keepdims=True)
            dscores = (probs * (dprobs - delta) * scale).astype(BF)
            r.dq_s[h, rows, :] = dot(r.kt_s[:, :keys], dscores).T.astype(BF)
            dk = dot(dscores, q)
            dv = dot(low, do)
            if i == steps - 1:
                r.dk_s[h] = dk
                r.dv_s[h] = dv
            else:
                r.dk_s[h, :keys, :] += dk
                r.dv_s[h, :keys, :] += dv

    @pl.loop(0, heads)
    def _(h):
        attend(h)

        @pl.when(h == 0)
        def _():
            start_2(DOWN)

        @pl.when(h == 1)
        def _():
            start_2(UP)

    sums_of = (r.act_s, r.dpre_s)

    def token_pair(i):
        src = sums_of[i]
        return [
            send(
                src.at[rows_of(t)], r.token_in.at[i, n], r.g_send.at[i, n], r.g_recv.at[i, n],
                (dp, sibling),
            )
            for n, t in enumerate((sibling, sib_across))
        ]

    def token_far_copy(i):
        pair = (r.h_send.at[i], r.h_recv.at[i])
        return send(r.token_mid.at[i], r.token_far.at[i], *pair, (dp, across))

    def token_cross(i):
        for item in token_pair(i):
            item.wait_recv()
        own = sums_of[i][rows_of(across), :].astype(F32)
        r.token_mid[i] = (own + r.token_in[i, 1].astype(F32)).astype(BF)
        token_far_copy(i).start()

    def token_total(i):
        token_far_copy(i).wait()
        own = sums_of[i][rows_of(sp), :].astype(F32)
        return own + r.token_in[i, 0].astype(F32) + r.token_far[i].astype(F32)

    ctxt = r.ctxt_s[...].reshape(width, length)
    for i in range(steps):
        rows = slice(i * BLOCK, (i + 1) * BLOCK)
        r.act_s[rows, :] = (r.sum_s[rows, :] + dot_tn(ctxt[:, rows], r.dense_s[...])).astype(BF)
    for item in token_pair(0):
        item.start()

    def last(i, sums):
        rows = rows_at(i)
        cosine, sine = r.cos_ref[rows, :], r.sin_ref[rows, :]
        parts = [
            ref[h, rows, :].astype(F32) for ref in (r.dq_s, r.dk_s, r.dv_s) for h in range(heads)
        ]
        blocks = []
        for p in range(2 * width // 128):
            u = jnp.concatenate(parts[2 * p : 2 * p + 2], 1).astype(BF).astype(F32)
            blocks.append((u * cosine - swap_halves(u) * sine).astype(BF))
        rest = parts[2 * heads :] + [jnp.zeros((BLOCK, QK - 3 * width), F32)]
        dqkv = jnp.concatenate(blocks + [jnp.concatenate(rest, 1).astype(BF)], 1)
        r.dqkv_s[rows, :] = dqkv
        dn1 = dot_nt(dqkv, r.qk_s[...])
        r.dpre_s[rows, :] = (r.dx_s[rows, :] + dn1 * gain_1).astype(BF)
        one, two, three = sums
        return (
            one + fold(dqkv.astype(F32)),
            two + fold(dn1 * r.xhat_s[rows, :]),
            three + fold(dn1),
        )

    qkv_bias, gain_1_grad, shift_1_grad = lax.fori_loop(
        0, steps, last, (jnp.zeros((8, QK), F32), zeros, zeros)
    )
    weight_grad(r.n1_s, r.dqkv_s, r.qk_g)
    start_1(QKV)
    for item in token_pair(1):
        item.start()
    token_cross(0)
    dense_grad = dot(ctxt, r.g_all[...])
    for e in range(NY * NZ * NX):
        r.dense_g[e // GROUP, e // NX % NZ, e % NX] = dense_grad[
            e * PART : (e + 1) * PART, :
        ].astype(BF)
    start_1(DENSE)

    g_here = r.g_all[rows_of(sp), :].astype(F32)
    values = (
        gain_1_grad, shift_1_grad, gain_2_grad, shift_2_grad, qkv_bias, fold(g_here), up_bias
    )
    result = jnp.zeros((n_rows, SMALL), F32)
    for (start, each, kind, _), item in zip(VECTORS_OUT, values):
        vector = jnp.sum(item, 0, keepdims=True)
        size = vector.shape[1]
        lane = column_of(iota((n_rows, size), 1), sp, kind)
        mine = lane // each == owner_rows(size)
        if kind == "qkv":
            mine = jnp.logical_and(mine, iota((n_rows, size), 1) < 3 * width)
        rest = jnp.where(mine, vector, 0.0)
        lane = column_of(iota((size, SMALL), 0), sp, kind)
        pick = (iota((size, SMALL), 1) == start + lax.rem(lane, each)).astype(BF)
        for _ in range(3):
            part = rest.astype(BF)
            result = result + dot(part, pick)
            rest = rest - part.astype(F32)
    for e in range(NY * NZ * NX):
        r.small_g[e // GROUP, e // NX % NZ, e % NX] = result[e * 8 : (e + 1) * 8, :]
    start_1(SMALLS)
    token_cross(1)
    start_2(QKV)

    up_total = finish(UP)
    for t in range(N_SP):
        r.up_p[t] = up_total[t * PART : (t + 1) * PART, :]

    def back(n, k):
        src, land = ((r.up_p, r.up_l), (r.qk_p, r.qk_l))[n]
        t = lax.rem(sp + k, N_SP)
        return send(src.at[t], land.at[sp], r.i_send.at[n, k], r.i_recv.at[n, sp], (dp, t))

    for k in range(1, N_SP):
        back(0, k).start()
    owned = ((r.down_t, r.down_out), (r.dense_t, r.dense_out))

    def own_copy(i):
        src, dst = owned[i]
        return send(src, dst, r.j_send.at[i], r.j_recv.at[i], to_owner)

    def start_own(i):
        @pl.when(moves)
        def _():
            own_copy(i).start()

        @pl.when(stays)
        def _():
            pltpu.make_async_copy(*owned[i], r.j_recv.at[i]).start()

    r.down_t[...] = finish(DOWN)
    start_own(0)
    start_2(DENSE)
    start_2(SMALLS)
    qk_total = finish(QKV)
    for t in range(N_SP):
        r.qk_p[t] = qk_total[t * PART : (t + 1) * PART, :]
    for k in range(1, N_SP):
        back(1, k).start()
    r.dense_t[...] = finish(DENSE)
    start_own(1)
    r.small_l[sp] = finish(SMALLS)

    def small_copy(k):
        there = r.small_l.at[sp]
        return send(
            there, there, r.k_send.at[k], r.k_recv.at[sp], (dp, lax.rem(sp + k, N_SP))
        )

    for k in range(1, N_SP):
        small_copy(k).start()

    x_here = r.x_all[rows_of(sp), :].astype(F32)
    r.hidden_out[...] = (x_here + token_total(0) + bias).astype(BF)
    dxhat = token_total(1)
    centered = x_here - jnp.mean(x_here, -1, keepdims=True)
    rstd = lax.rsqrt(jnp.mean(centered * centered, -1, keepdims=True) + 1e-05)
    xhat = centered * rstd
    r.hidden_grad[...] = (
        r.g_all[rows_of(sp), :].astype(F32)
        + rstd
        * (
            dxhat
            - jnp.mean(dxhat, -1, keepdims=True)
            - xhat * jnp.mean(dxhat * xhat, -1, keepdims=True)
        )
    ).astype(BF)

    r.up_l[sp] = r.up_p[sp]
    r.qk_l[sp] = r.qk_p[sp]
    for n, land in enumerate((r.up_l, r.qk_l)):
        for k in range(1, N_SP):
            s = lax.rem(sp + k, N_SP)
            local_wait(land.at[s], r.i_recv.at[n, s])
    for s in range(N_SP):
        r.up_out[:, s * PAGE : (s + 1) * PAGE] = r.up_l[s]
        block = r.qk_l[s]
        for j in range(3):
            to = j * D + s * width
            r.qkv_out[:, to : to + width] = block[:, j * width : (j + 1) * width]
    for k in range(1, N_SP):
        s = lax.rem(sp + k, N_SP)
        local_wait(r.small_l.at[s], r.k_recv.at[s])
    r.small_out[...] = jnp.sum(r.small_l[...], 0)
    for i in range(2):
        pltpu.make_async_copy(*owned[i], r.j_recv.at[i]).wait()

    for kind in ("across", "sibling", "pass"):
        for item in token_copies(kind):
            item.wait_send()

    @pl.when(moves)
    def _():
        for item in row_copies():
            item.wait_send()
        for i in range(2):
            own_copy(i).wait_send()

    for k in range(1, N_SP):
        piece(k).wait_send()
        back(0, k).wait_send()
        back(1, k).wait_send()
        small_copy(k).wait_send()
    for i in range(2):
        for item in token_pair(i):
            item.wait_send()
    for n in range(5):
        for item in stage_a(n) + stage_b(n) + stage_1(n) + stage_2(n):
            item.wait_send()


def layer(x, g, up, qkv, small, down, dense):
    tokens = x.shape[0]
    length = tokens * N_SP
    heads = HEADS // N_SP
    width = heads * HEAD_DIM
    grid = (NY, NZ, NX)
    own = PART * N_SP
    cosine, sine = rotary_tables(length)
    dma = pltpu.SemaphoreType.DMA
    anywhere = pl.BlockSpec(memory_space=pl.ANY)
    vmem = pl.BlockSpec(memory_space=pltpu.VMEM)
    ins = ("x_ref", "g_ref", "up_ref", "qkv_ref", "small_ref", "down_ref", "dense_ref")
    ins += ("cos_ref", "sin_ref")
    outs = {
        "hidden_out": ((tokens, D), BF),
        "hidden_grad": ((tokens, D), BF),
        "up_out": ((PART, FF), F32),
        "qkv_out": ((PART, 3 * D), F32),
        "down_out": ((own, D), F32),
        "dense_out": ((PART, D), F32),
        "small_out": ((8, SMALL), F32),
    }
    chunk = {
        "up": ((own, PAGE), BF),
        "down": ((own, D), BF),
        "qk": ((own, QK), BF),
        "dense": ((PART, D), BF),
        "small": ((8, SMALL), F32),
    }
    scratch = {}
    for name, (shape, kind) in chunk.items():
        scratch[name + "_all"] = (grid + shape, kind)
        scratch[name + "_g"] = (grid + shape, kind)
        scratch[name + "_1"] = (grid + shape, kind)
        scratch[name + "_m"] = ((GROUP // NX, NX) + shape, kind)
        scratch[name + "_2"] = ((GROUP,) + shape, kind)
    per_head = (heads, length, HEAD_DIM)
    scratch.update(
        x_all=((length, D), BF),
        g_all=((length, D), BF),
        pieces=((N_SP, PART, PAGE + QK + SMALL), F32),
        landed=((N_SP, PART, PAGE + QK + SMALL), F32),
        tight=((own, PAGE + QK + SMALL), F32),
        up_s=((D, PAGE), BF),
        down_s=((PAGE, D), BF),
        qk_s=((D, QK), BF),
        dense_wide=((width, D), F32),
        dense_s=((width, D), BF),
        vec_s=((8, PAGE), F32),
        xhat_s=((length, D), F32),
        n1_s=((length, D), BF),
        n2_s=((length, D), BF),
        act_s=((length, PAGE), BF),
        dpre_s=((length, PAGE), BF),
        sum_s=((length, D), F32),
        dx_s=((length, D), F32),
        dqkv_s=((length, QK), BF),
        q_s=(per_head, BF),
        k_s=(per_head, BF),
        v_s=(per_head, BF),
        do_s=(per_head, BF),
        dq_s=(per_head, BF),
        dk_s=(per_head, F32),
        dv_s=(per_head, F32),
        kt_s=((HEAD_DIM, length), BF),
        vt_s=((HEAD_DIM, length), BF),
        ctxt_s=((heads, HEAD_DIM, length), BF),
        token_in=((2, 2, tokens, D), BF),
        token_mid=((2, tokens, D), BF),
        token_far=((2, tokens, D), BF),
        up_p=((N_SP, PART, PAGE), F32),
        up_l=((N_SP, PART, PAGE), F32),
        qk_p=((N_SP, PART, QK), F32),
        qk_l=((N_SP, PART, QK), F32),
        down_t=((own, D), F32),
        dense_t=((PART, D), F32),
        small_l=((N_SP, 8, SMALL), F32),
    )
    semaphores = {
        "r": (2,), "p": (N_SP,), "t": (2, N_SP), "a": (5, GROUP), "b": (5, NY), "e": (5, NY),
        "f": (5, GROUP), "g": (2, 2), "h": (2,), "i": (2, N_SP), "j": (2,), "k": (N_SP,),
    }
    names = list(ins) + list(outs) + list(scratch)
    shapes = [pltpu.VMEM(shape, kind) for shape, kind in scratch.values()]
    for name, shape in semaphores.items():
        names += [name + "_send", name + "_recv"]
        shapes += [dma(shape), dma(shape)]
    return pl.pallas_call(
        functools.partial(layer_kernel, names),
        out_shape=tuple(jax.ShapeDtypeStruct(*item) for item in outs.values()),
        in_specs=[anywhere, anywhere, vmem, vmem, vmem, anywhere, anywhere, vmem, vmem],
        out_specs=(vmem,) * len(outs),
        scratch_shapes=shapes,
        compiler_params=pltpu.CompilerParams(
            collective_id=0, has_side_effects=True, vmem_limit_bytes=61 * 1024 * 1024
        ),
        cost_estimate=pl.CostEstimate(
            flops=14_000_000_000, bytes_accessed=16_000_000, transcendentals=6_000_000
        ),
        name="layer",
    )(x, g, up, qkv, small, down, dense, cosine, sine)


def local(
    hidden_in,
    cotangent,
    attn_gain,
    attn_shift,
    mlp_gain,
    mlp_shift,
    qkv_weight,
    qkv_bias,
    dense_weight,
    dense_bias,
    up_weight,
    up_bias,
    down_weight,
    down_bias,
):
    sp = lax.axis_index("sp")
    small = (
        attn_gain,
        attn_shift,
        mlp_gain,
        mlp_shift,
        qkv_bias,
        dense_bias,
        up_bias,
        down_bias,
    )
    packed = jnp.zeros((SMALL,), F32)
    at = 0
    for item in small:
        size = item.shape[0]
        packed = packed + jnp.pad(item.astype(F32), (at, SMALL - at - size))
        at += size
    hidden_out, hidden_grad, up_own, qkv_own, down_own, dense_own, packed = layer(
        hidden_in,
        cotangent,
        up_weight,
        qkv_weight,
        packed.reshape(1, SMALL),
        down_weight,
        dense_weight,
    )
    mine = lax.dynamic_slice_in_dim(packed, sp, 1, 0).reshape(-1)
    parts = [mine[start : start + each] for start, each, _, _ in VECTORS_OUT]
    return (
        hidden_out,
        hidden_grad,
        parts[0],
        parts[1],
        parts[2],
        parts[3],
        qkv_own,
        parts[4],
        dense_own,
        parts[5],
        up_own,
        parts[6],
        down_own,
        parts[5],
    )


def solution(mesh):
    matrix = P(BOTH, None)
    vector = P(BOTH)
    split = (matrix, matrix) + (vector,) * 4 + (matrix, vector) * 4
    return jax.shard_map(local, mesh=mesh, in_specs=split, out_specs=split, check_vma=False)
```

```python
import functools
import types

import jax
import jax.numpy as jnp
import numpy as np
from jax import lax
from jax.experimental import pallas as pl
from jax.experimental.pallas import tpu as pltpu
from jax.sharding import PartitionSpec as P

D = 768
HEADS = 12
HEAD_DIM = 64
ROT = 16
FF = 3072
BF = jnp.bfloat16
F32 = jnp.float32
BOTH = ("dp", "sp")


def dot(left, right):
    return jnp.dot(left, right, preferred_element_type=F32)


MESH = pl.DeviceIdType.MESH
SMALL = 128
PAGE = 768
NY, NZ, NX = 4, 4, 2
GROUP = NZ * NX
N_SP = 4
PART = 6


def place():
    dp, sp = lax.axis_index("dp"), lax.axis_index("sp")
    return dp, sp, dp // GROUP, lax.rem(dp // NX, NZ), lax.rem(dp, NX)


def send(src, dst, send_sem, recv_sem, device):
    return pltpu.make_async_remote_copy(
        src_ref=src,
        dst_ref=dst,
        send_sem=send_sem,
        recv_sem=recv_sem,
        device_id=device,
        device_id_type=MESH,
    )


def index_of(y, z, x):
    return (y * NZ + z) * NX + x


def slot_device(dp, sp):
    line = dp * N_SP + sp
    return lax.rem(line, NY * GROUP), line // (NY * GROUP)


def owner_device(dp, sp):
    line = sp * NY * GROUP + dp
    return line // N_SP, lax.rem(line, N_SP)


def differs(device, dp, sp):
    return jnp.logical_or(device[0] != dp, device[1] != sp)


class Plane:
    def __init__(self, last):
        self.last = last
        dp, sp, y, z, x = place()
        self.sp, self.y, self.z, self.x = sp, y, z, x
        self.mine = (z if last == "y" else y) * NX + x
        self.axis = y if last == "y" else z

    def member(self, k):
        e = lax.rem(self.mine + k, GROUP)
        a, x = e // NX, lax.rem(e, NX)
        y, z = (self.y, a) if self.last == "y" else (a, self.z)
        return (index_of(y, z, x), self.sp), e, a, x

    def along(self, k):
        a = lax.rem(self.axis + k, NY)
        y, z = (a, self.z) if self.last == "y" else (self.y, a)
        return (index_of(y, z, self.x), self.sp), a

    def block(self, ref, a):
        return ref.at[a] if self.last == "y" else ref.at[:, a]

    def chunk(self, ref, e):
        a, x = e // NX, lax.rem(e, NX)
        return ref.at[self.y, a, x] if self.last == "y" else ref.at[a, self.z, x]


def greet(*partners):
    dp, sp, y, z, x = place()
    barrier = pltpu.get_barrier_semaphore()

    def signal(device):
        pl.semaphore_signal(barrier, inc=1, device_id=device, device_id_type=MESH)

    for k in range(1, N_SP):
        signal((dp, lax.rem(sp + k, N_SP)))
    by_y, by_z = Plane("y"), Plane("z")
    for k in range(1, GROUP):
        signal(by_y.member(k)[0])
        signal(by_z.member(k)[0])

    @pl.when(differs(partners[0], dp, sp))
    def _():
        for partner in partners:
            signal(partner)


def await_greetings(*partners):
    dp, sp, y, z, x = place()
    count = N_SP - 1 + 2 * (GROUP - 1)
    more = jnp.where(differs(partners[0], dp, sp), len(partners), 0)
    pl.semaphore_wait(pltpu.get_barrier_semaphore(), count + more)


BLOCK = 256


def dot_nt(left, right):
    return lax.dot_general(left, right, (((1,), (1,)), ((), ())), preferred_element_type=F32)


def dot_tn(left, right):
    return lax.dot_general(left, right, (((0,), (0,)), ((), ())), preferred_element_type=F32)


def iota(shape, axis):
    return lax.broadcasted_iota(jnp.int32, shape, axis)


def rotary_tables(length):
    half = ROT // 2
    frequency = np.float32(10000.0) ** (np.float32(-2.0) * np.arange(half, dtype=np.float32) / ROT)
    angles = np.arange(length, dtype=np.float32)[:, None] * frequency[None, :].astype(np.float32)
    cosine = np.ones((length, HEAD_DIM), np.float32)
    sine = np.zeros((length, HEAD_DIM), np.float32)
    cosine[:, :half] = cosine[:, half:ROT] = np.cos(angles)
    sine[:, :half] = -np.sin(angles)
    sine[:, half:ROT] = np.sin(angles)
    return jnp.asarray(np.tile(cosine, (1, 2))), jnp.asarray(np.tile(sine, (1, 2)))


def swap_halves(u):
    low = lax.rem(iota(u.shape, 1), 16) < 8
    return jnp.where(low, pltpu.roll(u, 120, 1), pltpu.roll(u, 8, 1))


def column_of(c, sp, kind):
    if kind == "qkv":
        width = D // N_SP
        return (c // width) * D + sp * width + lax.rem(c, width)
    return c + sp * (FF // N_SP) if kind == "up" else c


VECTORS_IN = (
    (0, 6, "", D), (6, 6, "", D), (12, 6, "", D), (18, 6, "", D),
    (24, 18, "qkv", PAGE), (42, 6, "", D), (48, 24, "up", PAGE), (72, 6, "", D),
)
VECTORS_OUT = (
    (0, 6, "", D), (6, 6, "", D), (12, 6, "", D), (18, 6, "", D),
    (24, 18, "qkv", PAGE), (42, 6, "", D), (48, 24, "up", PAGE),
)


QK = 640


def layer_kernel(names, *refs):
    r = types.SimpleNamespace(**dict(zip(names, refs)))
    dp, sp, y, z, x = place()
    to_slot, to_owner = slot_device(dp, sp), owner_device(dp, sp)
    sibling = sp + 1 - 2 * lax.rem(sp, 2)
    across = lax.rem(sp + 2, N_SP)
    sib_across = lax.rem(sibling + 2, N_SP)
    moves = differs(to_slot, dp, sp)
    stays = jnp.logical_not(moves)
    by_y, by_z = Plane("y"), Plane("z")
    length = r.x_all.shape[0]
    tokens = length // N_SP
    heads = HEADS // N_SP
    width = heads * HEAD_DIM
    n_own = NY * NZ * NX * N_SP
    steps = length // BLOCK
    slot = to_slot[0]
    slot_at = (slot // GROUP, lax.rem(slot // NX, NZ), lax.rem(slot, NX))

    def local_wait(ref, sem):
        pltpu.make_async_copy(ref, ref, sem).wait()

    def rows_of(s):
        return pl.ds(pl.multiple_of(s * tokens, tokens), tokens)

    def rows_at(i):
        return pl.ds(pl.multiple_of(i * BLOCK, BLOCK), BLOCK)

    greet(to_slot, to_owner)

    end = PAGE + 3 * width
    wide = r.qkv_ref[...].astype(F32)
    for t in range(N_SP):
        r.pieces[t, :, :PAGE] = r.up_ref[:, t * PAGE : (t + 1) * PAGE].astype(F32)
        for j in range(3):
            at = j * D + t * width
            r.pieces[t, :, PAGE + j * width : PAGE + (j + 1) * width] = wide[:, at : at + width]
        r.pieces[t, :, end : PAGE + QK] = jnp.zeros((PART, PAGE + QK - end), F32)
        r.pieces[t, 0:1, PAGE + QK :] = r.small_ref[...]
        r.pieces[t, 1:, PAGE + QK :] = jnp.zeros((PART - 1, SMALL), F32)

    await_greetings(to_slot, to_owner)

    def piece(k):
        t = lax.rem(sp + k, N_SP)
        return send(r.pieces.at[t], r.landed.at[sp], r.p_send.at[k], r.p_recv.at[sp], (dp, t))

    for k in range(1, N_SP):
        piece(k).start()
    pltpu.make_async_copy(r.pieces.at[sp], r.landed.at[sp], r.p_recv.at[sp]).start()

    def row_copies():
        return [
            send(r.down_ref, r.down_in, r.r_send.at[0], r.r_recv.at[0], to_slot),
            send(
                r.dense_ref, r.dense_all.at[slot_at], r.r_send.at[1], r.r_recv.at[1], to_slot
            ),
        ]

    @pl.when(moves)
    def _():
        for item in row_copies():
            item.start()

    @pl.when(stays)
    def _():
        pltpu.make_async_copy(r.down_ref, r.down_in, r.r_recv.at[0]).start()
        pltpu.make_async_copy(r.dense_ref, r.dense_all.at[y, z, x], r.r_recv.at[1]).start()

    token_arrays = ((r.x_ref, r.x_all), (r.g_ref, r.g_all))

    def token_copies(i, kind):
        src, dst = token_arrays[i]
        if kind == "pass":
            there = dst.at[rows_of(across)]
            pair = (r.t_send.at[i, 2], r.t_recv.at[i, across])
            return send(there, there, *pair, (dp, sibling))
        to, n = (across, 0) if kind == "across" else (sibling, 1)
        pair = (r.t_send.at[i, n], r.t_recv.at[i, sp])
        return send(src, dst.at[rows_of(sp)], *pair, (dp, to))

    def token_start(i):
        src, dst = token_arrays[i]
        token_copies(i, "across").start()
        token_copies(i, "sibling").start()
        pltpu.make_async_copy(src, dst.at[rows_of(sp)], r.t_recv.at[i, sp]).start()

    def token_wait(i, s):
        src, dst = token_arrays[i]
        pltpu.make_async_copy(src, dst.at[rows_of(s)], r.t_recv.at[i, s]).wait()

    def token_pass(i):
        token_wait(i, across)
        token_copies(i, "pass").start()

    def token_rest(i):
        for s in (sp, sibling, sib_across):
            token_wait(i, s)

    token_start(0)

    smalls, up_0, up_1, down_0, down_1, qkv_n, dense_n = range(7)
    gathered = (
        (by_y, r.small_all), (by_y, r.up_a), (by_z, r.up_b), (by_y, r.down_a), (by_z, r.down_b),
        (by_z, r.qk_all), (by_y, r.dense_all),
    )
    cut = PAGE // 2

    def stage_a(n):
        plane, out = gathered[n]
        mine = out.at[y, z, x]
        return [
            send(mine, mine, r.a_send.at[n, k], r.a_recv.at[n, plane.mine], plane.member(k)[0])
            for k in range(1, GROUP)
        ]

    def stage_b(n):
        plane, out = gathered[n]
        there = plane.block(out, plane.axis)
        return [
            send(there, there, r.b_send.at[n, k], r.b_recv.at[n, plane.axis], plane.along(k)[0])
            for k in range(1, NY)
        ]

    def start_a(n):
        for item in stage_a(n):
            item.start()

    def start_b(n):
        plane, out = gathered[n]
        for k in range(1, GROUP):
            e = lax.rem(plane.mine + k, GROUP)
            local_wait(plane.chunk(out, e), r.a_recv.at[n, e])
        for item in stage_b(n):
            item.start()

    def wait_b(n):
        plane, out = gathered[n]
        for k in range(1, NY):
            a = plane.along(k)[1]
            local_wait(plane.block(out, a), r.b_recv.at[n, a])

    for s in range(N_SP):
        local_wait(r.landed.at[s], r.p_recv.at[s])
    for s in range(N_SP):
        r.tight[s * PART : (s + 1) * PART, :] = r.landed[s]
    r.small_all[y, z, x] = jnp.zeros((8, SMALL), F32)
    for s in range(N_SP):
        r.small_all[y, z, x, s : s + 1, :] = r.landed[s, 0:1, PAGE + QK :]
    r.up_a[y, z, x] = r.tight[:, :cut].astype(BF)
    r.up_b[y, z, x] = r.tight[:, cut:PAGE].astype(BF)
    r.qk_all[y, z, x] = r.tight[:, PAGE : PAGE + QK].astype(BF)
    start_a(smalls)
    start_a(up_0)
    start_a(up_1)
    local_wait(r.down_in, r.r_recv.at[0])
    r.down_a[y, z, x] = r.down_in[:, :cut]
    r.down_b[y, z, x] = r.down_in[:, cut:]
    start_a(down_0)
    start_a(down_1)
    token_start(1)
    start_b(smalls)
    start_b(up_0)
    start_b(up_1)
    token_pass(0)
    start_b(down_0)
    start_b(down_1)
    local_wait(r.dense_all.at[y, z, x], r.r_recv.at[1])
    start_a(qkv_n)
    start_a(dense_n)

    wait_b(smalls)
    packed = r.small_all[...].reshape(2 * n_own, SMALL).astype(BF)
    n_rows = 2 * n_own

    def owner_rows(size):
        row = iota((n_rows, size), 0)
        inside = lax.rem(row, 8)
        return jnp.where(inside < N_SP, row // 8 * N_SP + inside, -1)

    for n, (start, each, kind, size) in enumerate(VECTORS_IN):
        lane = column_of(iota((SMALL, size), 1), sp, kind)
        spread = (iota((SMALL, size), 0) == start + lax.rem(lane, each)).astype(BF)
        lane = column_of(iota((n_rows, size), 1), sp, kind)
        values = jnp.where(lane // each == owner_rows(size), dot(packed, spread), 0.0)
        r.vec_s[n : n + 1, :] = jnp.sum(values, 0, keepdims=True)
    gain_1, shift_1, gain_2, shift_2 = (r.vec_s[n : n + 1, :] for n in range(4))
    qkv_add = r.vec_s[4:5, :QK]
    up_add = r.vec_s[6:7, :]
    bias = r.vec_s[5:6, :] + r.vec_s[7:8, :]

    def fold(values):
        return jnp.sum(values.reshape(-1, 8, values.shape[-1]), 0)

    token_rest(0)

    @pl.loop(0, steps)
    def _(i):
        rows = rows_at(i)
        values = r.x_all[rows, :].astype(F32)
        centered = values - jnp.mean(values, -1, keepdims=True)
        xhat = centered * lax.rsqrt(jnp.mean(centered * centered, -1, keepdims=True) + 1e-05)
        r.xhat_s[rows, :] = xhat
        r.n1_s[rows, :] = (xhat * gain_1 + shift_1).astype(BF)
        r.n2_s[rows, :] = (xhat * gain_2 + shift_2).astype(BF)

    def join(src, dst, lane=0):
        @pl.loop(0, NY * NZ)
        def _(i):
            a, b = i // NZ, lax.rem(i, NZ)
            pair = [src[a, b, e].astype(F32) for e in range(NX)]
            own, wide_here = pair[0].shape[0] * NX, pair[0].shape[1]
            here = (pl.ds(pl.multiple_of(i * own, own), own), pl.ds(lane, wide_here))
            dst[here] = jnp.concatenate(pair, 0).astype(BF)

    token_pass(1)
    wait_b(up_0)
    join(r.up_a, r.up_s)
    wait_b(up_1)
    join(r.up_b, r.up_s, cut)

    zeros = jnp.zeros((8, D), F32)

    @pl.loop(0, steps)
    def _(i):
        rows = rows_at(i)
        pre = dot(r.n2_s[rows, :], r.up_s[...]) + up_add
        cdf = 0.5 * (1.0 + lax.erf(pre * 0.7071067811865476))
        r.act_s[rows, :] = (pre * cdf).astype(BF)
        pdf = jnp.exp(-0.5 * pre * pre) * 0.3989422804014327
        r.sum_s[rows, :] = cdf + pre * pdf

    start_b(qkv_n)
    start_b(dense_n)
    wait_b(down_0)
    join(r.down_a, r.down_s)
    wait_b(down_1)
    join(r.down_b, r.down_s, cut)
    token_rest(1)

    def first(i, sums):
        rows = rows_at(i)
        dact = dot_nt(r.g_all[rows, :], r.down_s[...])
        dpre = (dact * r.sum_s[rows, :]).astype(BF)
        r.dpre_s[rows, :] = dpre
        r.sum_s[rows, :] = dot(r.act_s[rows, :], r.down_s[...])
        dn2 = dot_nt(dpre, r.up_s[...])
        r.dx_s[rows, :] = dn2 * gain_2
        one, two, three = sums
        return (
            one + fold(dpre.astype(F32)),
            two + fold(dn2 * r.xhat_s[rows, :]),
            three + fold(dn2),
        )

    up_bias, gain_2_grad, shift_2_grad = lax.fori_loop(0, steps, first, (zeros,) * 3)

    half = D // 2
    in_half = half // (PART * N_SP)

    def weight_grad(left, right, out):
        @pl.loop(0, 2)
        def _(i):
            lanes = pl.ds(pl.multiple_of(i * half, half), half)
            value = dot_tn(left[:, lanes], right[...])
            own = PART * N_SP
            for c in range(in_half):
                at = (i * (NY // 2) + c // GROUP, c // NX % NZ, c % NX)
                out[at[0], at[1], at[2]] = value[c * own : (c + 1) * own, :].astype(BF)

    SMALLS, UP, DOWN, QKV, DENSE = range(5)
    reduced = (
        (by_y, r.small_g, r.small_1, r.small_m, r.small_2),
        (by_y, r.up_g, r.up_1, r.up_m, r.up_2),
        (by_z, r.down_g, r.down_1, r.down_m, r.down_2),
        (by_z, r.qk_g, r.qk_1, r.qk_m, r.qk_2),
        (by_y, r.dense_g, r.dense_1, r.dense_m, r.dense_2),
    )

    def stage_1(n):
        plane, src, land = reduced[n][:3]
        made = []
        for k in range(1, NY):
            device, a = plane.along(k)
            pair = (r.e_send.at[n, k], r.e_recv.at[n, plane.axis])
            made.append(send(plane.block(src, a), land.at[plane.axis], *pair, device))
        return made

    def stage_2(n):
        plane, _, _, mid, land = reduced[n]
        made = []
        for k in range(1, GROUP):
            device, e, a, xx = plane.member(k)
            pair = (r.f_send.at[n, k], r.f_recv.at[n, plane.mine])
            made.append(send(mid.at[a, xx], land.at[plane.mine], *pair, device))
        return made

    def start_1(n):
        for item in stage_1(n):
            item.start()

    def start_2(n):
        plane, src, land, mid, _ = reduced[n]
        for k in range(1, NY):
            a = plane.along(k)[1]
            local_wait(land.at[a], r.e_recv.at[n, a])

        @pl.loop(0, GROUP)
        def _(e):
            a, xx = e // NX, lax.rem(e, NX)
            own = src[plane.axis, a, xx] if plane.last == "y" else src[a, plane.axis, xx]
            total = own.astype(F32)
            for k in range(1, NY):
                total = total + land[lax.rem(plane.axis + k, NY), a, xx].astype(F32)
            mid[a, xx] = total.astype(mid.dtype)

        for item in stage_2(n):
            item.start()

    def finish(n):
        plane, _, _, mid, land = reduced[n]
        for k in range(1, GROUP):
            e = lax.rem(plane.mine + k, GROUP)
            local_wait(land.at[e], r.f_recv.at[n, e])
        total = mid[plane.mine // NX, lax.rem(plane.mine, NX)].astype(F32)
        for k in range(1, GROUP):
            total = total + land[lax.rem(plane.mine + k, GROUP)].astype(F32)
        return total

    weight_grad(r.act_s, r.g_all, r.down_g)
    start_1(DOWN)
    weight_grad(r.n2_s, r.dpre_s, r.up_g)
    start_1(UP)

    wait_b(qkv_n)
    join(r.qk_all, r.qk_s)
    wait_b(dense_n)
    for e in range(NY * NZ * NX):
        r.dense_wide[e * PART : (e + 1) * PART, :] = r.dense_all[
            e // GROUP, e // NX % NZ, e % NX
        ].astype(F32)
    r.dense_s[...] = r.dense_wide[...].astype(BF)

    @pl.loop(0, steps)
    def _(i):
        rows = rows_at(i)
        y_rows = dot(r.n1_s[rows, :], r.qk_s[...]) + qkv_add
        cosine, sine = r.cos_ref[rows, :], r.sin_ref[rows, :]
        turned = []
        for p in range(2 * width // 128):
            u = y_rows[:, p * 128 : (p + 1) * 128]
            turned.append(u * cosine + swap_halves(u) * sine)
        d = dot_nt(r.g_all[rows, :], r.dense_s[...])

        def head(n):
            u = turned[n // 2]
            return u[:, (n % 2) * HEAD_DIM : (n % 2 + 1) * HEAD_DIM]

        for h in range(heads):
            at = 2 * width + h * HEAD_DIM
            r.q_s[h, rows, :] = head(h).astype(BF)
            r.k_s[h, rows, :] = head(heads + h).astype(BF)
            r.v_s[h, rows, :] = y_rows[:, at : at + HEAD_DIM].astype(BF)
            r.do_s[h, rows, :] = d[:, h * HEAD_DIM : (h + 1) * HEAD_DIM].astype(BF)

    scale = HEAD_DIM ** (-0.5)

    def attend(h):
        r.kt_s[...] = r.k_s[h].astype(F32).T.astype(BF)
        r.vt_s[...] = r.v_s[h].astype(F32).T.astype(BF)
        for i in reversed(range(steps)):
            keys = (i + 1) * BLOCK
            rows = slice(i * BLOCK, (i + 1) * BLOCK)
            q, do = r.q_s[h, rows, :], r.do_s[h, rows, :]
            scores = dot_nt(r.k_s[h, :keys, :], q) * scale
            hidden = iota((BLOCK, BLOCK), 0) > iota((BLOCK, BLOCK), 1)
            corner = jnp.where(hidden, -1e30, scores[i * BLOCK :, :])
            scores = jnp.concatenate([scores[: i * BLOCK, :], corner], 0) if i else corner
            expo = jnp.exp(scores - jnp.max(scores, 0, keepdims=True))
            probs = expo * (1.0 / jnp.sum(expo, 0, keepdims=True))
            low = probs.astype(BF)
            r.ctxt_s[h, :, rows] = dot(r.vt_s[:, :keys], low).astype(BF)
            dprobs = dot_nt(r.v_s[h, :keys, :], do)
            delta = jnp.sum(probs * dprobs, 0, keepdims=True)
            dscores = (probs * (dprobs - delta) * scale).astype(BF)
            r.dq_s[h, rows, :] = dot(r.kt_s[:, :keys], dscores).T.astype(BF)
            dk = dot(dscores, q)
            dv = dot(low, do)
            if i == steps - 1:
                r.dk_s[h] = dk
                r.dv_s[h] = dv
            else:
                r.dk_s[h, :keys, :] += dk
                r.dv_s[h, :keys, :] += dv

    @pl.loop(0, heads)
    def _(h):
        attend(h)

        @pl.when(h == 0)
        def _():
            start_2(DOWN)

        @pl.when(h == 1)
        def _():
            start_2(UP)

    sums_of = (r.act_s, r.dpre_s)

    def token_pair(i):
        src = sums_of[i]
        return [
            send(
                src.at[rows_of(t)], r.token_in.at[i, n], r.g_send.at[i, n], r.g_recv.at[i, n],
                (dp, sibling),
            )
            for n, t in enumerate((sibling, sib_across))
        ]

    def token_far_copy(i):
        pair = (r.h_send.at[i], r.h_recv.at[i])
        return send(r.token_mid.at[i], r.token_far.at[i], *pair, (dp, across))

    def token_cross(i):
        for item in token_pair(i):
            item.wait_recv()
        own = sums_of[i][rows_of(across), :].astype(F32)
        r.token_mid[i] = (own + r.token_in[i, 1].astype(F32)).astype(BF)
        token_far_copy(i).start()

    def token_total(i):
        token_far_copy(i).wait()
        own = sums_of[i][rows_of(sp), :].astype(F32)
        return own + r.token_in[i, 0].astype(F32) + r.token_far[i].astype(F32)

    ctxt = r.ctxt_s[...].reshape(width, length)
    for i in range(steps):
        rows = slice(i * BLOCK, (i + 1) * BLOCK)
        r.act_s[rows, :] = (r.sum_s[rows, :] + dot_tn(ctxt[:, rows], r.dense_s[...])).astype(BF)
    for item in token_pair(0):
        item.start()

    def last(i, sums):
        rows = rows_at(i)
        cosine, sine = r.cos_ref[rows, :], r.sin_ref[rows, :]
        parts = [
            ref[h, rows, :].astype(F32) for ref in (r.dq_s, r.dk_s, r.dv_s) for h in range(heads)
        ]
        blocks = []
        for p in range(2 * width // 128):
            u = jnp.concatenate(parts[2 * p : 2 * p + 2], 1).astype(BF).astype(F32)
            blocks.append((u * cosine - swap_halves(u) * sine).astype(BF))
        rest = parts[2 * heads :] + [jnp.zeros((BLOCK, QK - 3 * width), F32)]
        dqkv = jnp.concatenate(blocks + [jnp.concatenate(rest, 1).astype(BF)], 1)
        r.dqkv_s[rows, :] = dqkv
        dn1 = dot_nt(dqkv, r.qk_s[...])
        r.dpre_s[rows, :] = (r.dx_s[rows, :] + dn1 * gain_1).astype(BF)
        one, two, three = sums
        return (
            one + fold(dqkv.astype(F32)),
            two + fold(dn1 * r.xhat_s[rows, :]),
            three + fold(dn1),
        )

    qkv_bias, gain_1_grad, shift_1_grad = lax.fori_loop(
        0, steps, last, (jnp.zeros((8, QK), F32), zeros, zeros)
    )
    weight_grad(r.n1_s, r.dqkv_s, r.qk_g)
    start_1(QKV)
    for item in token_pair(1):
        item.start()
    token_cross(0)
    dense_grad = dot(ctxt, r.g_all[...])
    for e in range(NY * NZ * NX):
        r.dense_g[e // GROUP, e // NX % NZ, e % NX] = dense_grad[
            e * PART : (e + 1) * PART, :
        ].astype(BF)
    start_1(DENSE)

    g_here = r.g_all[rows_of(sp), :].astype(F32)
    values = (
        gain_1_grad, shift_1_grad, gain_2_grad, shift_2_grad, qkv_bias, fold(g_here), up_bias
    )
    result = jnp.zeros((n_rows, SMALL), F32)
    for (start, each, kind, _), item in zip(VECTORS_OUT, values):
        vector = jnp.sum(item, 0, keepdims=True)
        size = vector.shape[1]
        lane = column_of(iota((n_rows, size), 1), sp, kind)
        mine = lane // each == owner_rows(size)
        if kind == "qkv":
            mine = jnp.logical_and(mine, iota((n_rows, size), 1) < 3 * width)
        rest = jnp.where(mine, vector, 0.0)
        lane = column_of(iota((size, SMALL), 0), sp, kind)
        pick = (iota((size, SMALL), 1) == start + lax.rem(lane, each)).astype(BF)
        for _ in range(3):
            part = rest.astype(BF)
            result = result + dot(part, pick)
            rest = rest - part.astype(F32)
    for e in range(NY * NZ * NX):
        r.small_g[e // GROUP, e // NX % NZ, e % NX] = result[e * 8 : (e + 1) * 8, :]
    start_1(SMALLS)
    token_cross(1)
    start_2(QKV)

    up_total = finish(UP)
    for t in range(N_SP):
        r.up_p[t] = up_total[t * PART : (t + 1) * PART, :]

    def back(n, k):
        src, land = ((r.up_p, r.up_l), (r.qk_p, r.qk_l))[n]
        t = lax.rem(sp + k, N_SP)
        return send(src.at[t], land.at[sp], r.i_send.at[n, k], r.i_recv.at[n, sp], (dp, t))

    for k in range(1, N_SP):
        back(0, k).start()
    owned = ((r.down_t, r.down_out), (r.dense_t, r.dense_out))

    def own_copy(i):
        src, dst = owned[i]
        return send(src, dst, r.j_send.at[i], r.j_recv.at[i], to_owner)

    def start_own(i):
        @pl.when(moves)
        def _():
            own_copy(i).start()

        @pl.when(stays)
        def _():
            pltpu.make_async_copy(*owned[i], r.j_recv.at[i]).start()

    r.down_t[...] = finish(DOWN)
    start_own(0)
    start_2(DENSE)
    start_2(SMALLS)
    qk_total = finish(QKV)
    for t in range(N_SP):
        r.qk_p[t] = qk_total[t * PART : (t + 1) * PART, :]
    for k in range(1, N_SP):
        back(1, k).start()
    r.dense_t[...] = finish(DENSE)
    start_own(1)
    r.small_l[sp] = finish(SMALLS)

    def small_copy(k):
        there = r.small_l.at[sp]
        return send(
            there, there, r.k_send.at[k], r.k_recv.at[sp], (dp, lax.rem(sp + k, N_SP))
        )

    for k in range(1, N_SP):
        small_copy(k).start()

    x_here = r.x_all[rows_of(sp), :].astype(F32)
    r.hidden_out[...] = (x_here + token_total(0) + bias).astype(BF)
    dxhat = token_total(1)
    centered = x_here - jnp.mean(x_here, -1, keepdims=True)
    rstd = lax.rsqrt(jnp.mean(centered * centered, -1, keepdims=True) + 1e-05)
    xhat = centered * rstd
    r.hidden_grad[...] = (
        r.g_all[rows_of(sp), :].astype(F32)
        + rstd
        * (
            dxhat
            - jnp.mean(dxhat, -1, keepdims=True)
            - xhat * jnp.mean(dxhat * xhat, -1, keepdims=True)
        )
    ).astype(BF)

    r.up_l[sp] = r.up_p[sp]
    r.qk_l[sp] = r.qk_p[sp]
    for n, land in enumerate((r.up_l, r.qk_l)):
        for k in range(1, N_SP):
            s = lax.rem(sp + k, N_SP)
            local_wait(land.at[s], r.i_recv.at[n, s])
    for s in range(N_SP):
        r.up_out[:, s * PAGE : (s + 1) * PAGE] = r.up_l[s]
        block = r.qk_l[s]
        for j in range(3):
            to = j * D + s * width
            r.qkv_out[:, to : to + width] = block[:, j * width : (j + 1) * width]
    for k in range(1, N_SP):
        s = lax.rem(sp + k, N_SP)
        local_wait(r.small_l.at[s], r.k_recv.at[s])
    r.small_out[...] = jnp.sum(r.small_l[...], 0)
    for i in range(2):
        pltpu.make_async_copy(*owned[i], r.j_recv.at[i]).wait()

    for i in range(2):
        for kind in ("across", "sibling", "pass"):
            token_copies(i, kind).wait_send()

    @pl.when(moves)
    def _():
        for item in row_copies():
            item.wait_send()
        for i in range(2):
            own_copy(i).wait_send()

    for k in range(1, N_SP):
        piece(k).wait_send()
        back(0, k).wait_send()
        back(1, k).wait_send()
        small_copy(k).wait_send()
    for i in range(2):
        for item in token_pair(i):
            item.wait_send()
    for n in range(len(gathered)):
        for item in stage_a(n) + stage_b(n):
            item.wait_send()
    for n in range(len(reduced)):
        for item in stage_1(n) + stage_2(n):
            item.wait_send()


def layer(x, g, up, qkv, small, down, dense):
    tokens = x.shape[0]
    length = tokens * N_SP
    heads = HEADS // N_SP
    width = heads * HEAD_DIM
    grid = (NY, NZ, NX)
    own = PART * N_SP
    cosine, sine = rotary_tables(length)
    dma = pltpu.SemaphoreType.DMA
    anywhere = pl.BlockSpec(memory_space=pl.ANY)
    vmem = pl.BlockSpec(memory_space=pltpu.VMEM)
    ins = ("x_ref", "g_ref", "up_ref", "qkv_ref", "small_ref", "down_ref", "dense_ref")
    ins += ("cos_ref", "sin_ref")
    outs = {
        "hidden_out": ((tokens, D), BF),
        "hidden_grad": ((tokens, D), BF),
        "up_out": ((PART, FF), F32),
        "qkv_out": ((PART, 3 * D), F32),
        "down_out": ((own, D), F32),
        "dense_out": ((PART, D), F32),
        "small_out": ((8, SMALL), F32),
    }
    chunk = {
        "up": ((own, PAGE), BF),
        "down": ((own, D), BF),
        "qk": ((own, QK), BF),
        "dense": ((PART, D), BF),
        "small": ((8, SMALL), F32),
    }
    scratch = {}
    for name, (shape, kind) in chunk.items():
        if name in ("up", "down"):
            scratch[name + "_a"] = (grid + (own, PAGE // 2), kind)
            scratch[name + "_b"] = (grid + (own, PAGE // 2), kind)
        else:
            scratch[name + "_all"] = (grid + shape, kind)
        scratch[name + "_g"] = (grid + shape, kind)
        scratch[name + "_1"] = (grid + shape, kind)
        scratch[name + "_m"] = ((GROUP // NX, NX) + shape, kind)
        scratch[name + "_2"] = ((GROUP,) + shape, kind)
    per_head = (heads, length, HEAD_DIM)
    scratch.update(
        x_all=((length, D), BF),
        g_all=((length, D), BF),
        pieces=((N_SP, PART, PAGE + QK + SMALL), F32),
        landed=((N_SP, PART, PAGE + QK + SMALL), F32),
        tight=((own, PAGE + QK + SMALL), F32),
        up_s=((D, PAGE), BF),
        down_s=((PAGE, D), BF),
        qk_s=((D, QK), BF),
        down_in=((own, D), BF),
        dense_wide=((width, D), F32),
        dense_s=((width, D), BF),
        vec_s=((8, PAGE), F32),
        xhat_s=((length, D), F32),
        n1_s=((length, D), BF),
        n2_s=((length, D), BF),
        act_s=((length, PAGE), BF),
        dpre_s=((length, PAGE), BF),
        sum_s=((length, D), F32),
        dx_s=((length, D), F32),
        dqkv_s=((length, QK), BF),
        q_s=(per_head, BF),
        k_s=(per_head, BF),
        v_s=(per_head, BF),
        do_s=(per_head, BF),
        dq_s=(per_head, BF),
        dk_s=(per_head, F32),
        dv_s=(per_head, F32),
        kt_s=((HEAD_DIM, length), BF),
        vt_s=((HEAD_DIM, length), BF),
        ctxt_s=((heads, HEAD_DIM, length), BF),
        token_in=((2, 2, tokens, D), BF),
        token_mid=((2, tokens, D), BF),
        token_far=((2, tokens, D), BF),
        up_p=((N_SP, PART, PAGE), F32),
        up_l=((N_SP, PART, PAGE), F32),
        qk_p=((N_SP, PART, QK), F32),
        qk_l=((N_SP, PART, QK), F32),
        down_t=((own, D), F32),
        dense_t=((PART, D), F32),
        small_l=((N_SP, 8, SMALL), F32),
    )
    semaphores = {
        "r": (2,), "p": (N_SP,), "t": (2, N_SP), "a": (7, GROUP), "b": (7, NY), "e": (5, NY),
        "f": (5, GROUP), "g": (2, 2), "h": (2,), "i": (2, N_SP), "j": (2,), "k": (N_SP,),
    }
    names = list(ins) + list(outs) + list(scratch)
    shapes = [pltpu.VMEM(shape, kind) for shape, kind in scratch.values()]
    for name, shape in semaphores.items():
        names += [name + "_send", name + "_recv"]
        shapes += [dma(shape), dma(shape)]
    return pl.pallas_call(
        functools.partial(layer_kernel, names),
        out_shape=tuple(jax.ShapeDtypeStruct(*item) for item in outs.values()),
        in_specs=[anywhere, anywhere, vmem, vmem, vmem, anywhere, anywhere, vmem, vmem],
        out_specs=(vmem,) * len(outs),
        scratch_shapes=shapes,
        compiler_params=pltpu.CompilerParams(
            collective_id=0, has_side_effects=True, vmem_limit_bytes=61 * 1024 * 1024
        ),
        cost_estimate=pl.CostEstimate(
            flops=14_000_000_000, bytes_accessed=16_000_000, transcendentals=6_000_000
        ),
        name="layer",
    )(x, g, up, qkv, small, down, dense, cosine, sine)


def outputs_kernel(*refs):
    n = 6
    small_ref, outs = refs[n], refs[n + 1 :]
    for i in range(n):
        outs[i][...] = refs[i][...]
    mine = small_ref[pl.ds(lax.axis_index("sp"), 1), :]
    for (start, each, _, _), out in zip(VECTORS_OUT + VECTORS_OUT[5:6], outs[n:]):
        out[...] = mine[:, start : start + each]


def write_outputs(*arrays):
    vmem = pl.BlockSpec(memory_space=pltpu.VMEM)
    large = [jax.ShapeDtypeStruct(item.shape, item.dtype) for item in arrays[:-1]]
    small = [
        jax.ShapeDtypeStruct((1, each), F32) for _, each, _, _ in VECTORS_OUT + VECTORS_OUT[5:6]
    ]
    return pl.pallas_call(
        outputs_kernel,
        out_shape=tuple(large + small),
        in_specs=[vmem] * len(arrays),
        out_specs=(vmem,) * (len(large) + len(small)),
        name="outputs",
    )(*arrays)


def local(
    hidden_in,
    cotangent,
    attn_gain,
    attn_shift,
    mlp_gain,
    mlp_shift,
    qkv_weight,
    qkv_bias,
    dense_weight,
    dense_bias,
    up_weight,
    up_bias,
    down_weight,
    down_bias,
):
    small = (
        attn_gain,
        attn_shift,
        mlp_gain,
        mlp_shift,
        qkv_bias,
        dense_bias,
        up_bias,
        down_bias,
    )
    packed = jnp.zeros((SMALL,), F32)
    at = 0
    for item in small:
        size = item.shape[0]
        packed = packed + jnp.pad(item.astype(F32), (at, SMALL - at - size))
        at += size
    results = layer(
        hidden_in,
        cotangent,
        up_weight,
        qkv_weight,
        packed.reshape(1, SMALL),
        down_weight,
        dense_weight,
    )
    results = write_outputs(*results)
    hidden_out, hidden_grad, up_own, qkv_own, down_own, dense_own = results[:6]
    parts = [item.reshape(-1) for item in results[6:]]
    return (
        hidden_out,
        hidden_grad,
        parts[0],
        parts[1],
        parts[2],
        parts[3],
        qkv_own,
        parts[4],
        dense_own,
        parts[5],
        up_own,
        parts[6],
        down_own,
        parts[7],
    )


def solution(mesh):
    matrix = P(BOTH, None)
    vector = P(BOTH)
    split = (matrix, matrix) + (vector,) * 4 + (matrix, vector) * 4
    return jax.shard_map(local, mesh=mesh, in_specs=split, out_specs=split, check_vma=False)
```

```python
import functools
import types

import jax
import jax.numpy as jnp
import numpy as np
from jax import lax
from jax.experimental import pallas as pl
from jax.experimental.pallas import tpu as pltpu
from jax.sharding import PartitionSpec as P

D = 768
HEADS = 12
HEAD_DIM = 64
ROT = 16
FF = 3072
BF = jnp.bfloat16
F32 = jnp.float32
BOTH = ("dp", "sp")


def dot(left, right):
    return jnp.dot(left, right, preferred_element_type=F32)


MESH = pl.DeviceIdType.MESH
SMALL = 128
PAGE = 768
NY, NZ, NX = 4, 4, 2
GROUP = NZ * NX
N_SP = 4
PART = 6


def place():
    dp, sp = lax.axis_index("dp"), lax.axis_index("sp")
    return dp, sp, dp // GROUP, lax.rem(dp // NX, NZ), lax.rem(dp, NX)


def send(src, dst, send_sem, recv_sem, device):
    return pltpu.make_async_remote_copy(
        src_ref=src,
        dst_ref=dst,
        send_sem=send_sem,
        recv_sem=recv_sem,
        device_id=device,
        device_id_type=MESH,
    )


def index_of(y, z, x):
    return (y * NZ + z) * NX + x


def slot_device(dp, sp):
    line = dp * N_SP + sp
    return lax.rem(line, NY * GROUP), line // (NY * GROUP)


def owner_device(dp, sp):
    line = sp * NY * GROUP + dp
    return line // N_SP, lax.rem(line, N_SP)


def differs(device, dp, sp):
    return jnp.logical_or(device[0] != dp, device[1] != sp)


def other_half(dp):
    return dp + 1 - 2 * lax.rem(dp, NX)


class Path:
    def __init__(self, last):
        self.last = last
        dp, self.sp, self.y, self.z, self.x = place()
        self.first, self.axis = (self.z, self.y) if last == "y" else (self.y, self.z)

    def along_first(self, k):
        a = lax.rem(self.first + k, NY)
        y, z = (self.y, a) if self.last == "y" else (a, self.z)
        return (index_of(y, z, self.x), self.sp), a

    def along(self, k):
        a = lax.rem(self.axis + k, NY)
        y, z = (a, self.z) if self.last == "y" else (self.y, a)
        return (index_of(y, z, self.x), self.sp), a

    def block(self, ref, a):
        return ref.at[a] if self.last == "y" else ref.at[:, a]

    def pair(self, ref, a):
        return ref.at[self.y, a] if self.last == "y" else ref.at[a, self.z]


def greet(partners):
    dp, sp, y, z, x = place()
    barrier = pltpu.get_barrier_semaphore()

    def signal(device):
        pl.semaphore_signal(barrier, inc=1, device_id=device, device_id_type=MESH)

    for k in range(N_SP):
        if k:
            signal((dp, lax.rem(sp + k, N_SP)))
        signal((other_half(dp), lax.rem(sp + k, N_SP)))
    by_y, by_z = Path("y"), Path("z")
    for k in range(1, NY):
        signal(by_y.along(k)[0])
        signal(by_z.along(k)[0])
    for partner in partners:

        @pl.when(differs(partner, dp, sp))
        def _():
            signal(partner)


def await_greetings(partners):
    dp, sp, y, z, x = place()
    count = 2 * N_SP - 1 + 2 * (NY - 1)
    for partner in partners:
        count = count + jnp.where(differs(partner, dp, sp), 1, 0)
    pl.semaphore_wait(pltpu.get_barrier_semaphore(), count)


BLOCK = 256


def dot_nt(left, right):
    return lax.dot_general(left, right, (((1,), (1,)), ((), ())), preferred_element_type=F32)


def dot_tn(left, right):
    return lax.dot_general(left, right, (((0,), (0,)), ((), ())), preferred_element_type=F32)


def iota(shape, axis):
    return lax.broadcasted_iota(jnp.int32, shape, axis)


def rotary_tables(length):
    half = ROT // 2
    frequency = np.float32(10000.0) ** (np.float32(-2.0) * np.arange(half, dtype=np.float32) / ROT)
    angles = np.arange(length, dtype=np.float32)[:, None] * frequency[None, :].astype(np.float32)
    cosine = np.ones((length, HEAD_DIM), np.float32)
    sine = np.zeros((length, HEAD_DIM), np.float32)
    cosine[:, :half] = cosine[:, half:ROT] = np.cos(angles)
    sine[:, :half] = -np.sin(angles)
    sine[:, half:ROT] = np.sin(angles)
    return jnp.asarray(np.tile(cosine, (1, 2))), jnp.asarray(np.tile(sine, (1, 2)))


def swap_halves(u):
    low = lax.rem(iota(u.shape, 1), 16) < 8
    return jnp.where(low, pltpu.roll(u, 120, 1), pltpu.roll(u, 8, 1))


def column_of(c, sp, kind):
    if kind == "qkv":
        width = D // N_SP
        return (c // width) * D + sp * width + lax.rem(c, width)
    return c + sp * (FF // N_SP) if kind == "up" else c


VECTORS_IN = (
    (0, 6, "", D), (6, 6, "", D), (12, 6, "", D), (18, 6, "", D),
    (24, 18, "qkv", PAGE), (42, 6, "", D), (48, 24, "up", PAGE), (72, 6, "", D),
)
VECTORS_OUT = (
    (0, 6, "", D), (6, 6, "", D), (12, 6, "", D), (18, 6, "", D),
    (24, 18, "qkv", PAGE), (42, 6, "", D), (48, 24, "up", PAGE),
)


QK = 640


def layer_kernel(names, *refs):
    r = types.SimpleNamespace(**dict(zip(names, refs)))
    dp, sp, y, z, x = place()
    half_dp = (dp, other_half(dp))
    half_x = (x, 1 - x)
    slot, column = slot_device(dp, sp)
    to_slots = ((slot, column), (other_half(slot), column))
    to_owners = tuple(owner_device(d, sp) for d in half_dp)
    slot_x = lax.rem(slot, NX)
    sibling = sp + 1 - 2 * lax.rem(sp, 2)
    across = lax.rem(sp + 2, N_SP)
    sib_across = lax.rem(sibling + 2, N_SP)
    others = [(q, k) for q in range(NX) for k in range(N_SP) if q or k]
    by_y, by_z = Path("y"), Path("z")
    length = r.x_all.shape[0]
    tokens = length // N_SP
    heads = HEADS // N_SP
    width = heads * HEAD_DIM
    n_own = NY * NZ * NX * N_SP
    steps = length // BLOCK
    slot_at = (slot // GROUP, lax.rem(slot // NX, NZ), slot_x)

    def to_partner(device, copy, src, dst, recv, run):
        @pl.when(differs(device, dp, sp))
        def _():
            getattr(copy, run)()

        if run == "start":

            @pl.when(jnp.logical_not(differs(device, dp, sp)))
            def _():
                pltpu.make_async_copy(src, dst, recv).start()

    def local_wait(ref, sem):
        pltpu.make_async_copy(ref, ref, sem).wait()

    def rows_of(s):
        return pl.ds(pl.multiple_of(s * tokens, tokens), tokens)

    def rows_at(i):
        return pl.ds(pl.multiple_of(i * BLOCK, BLOCK), BLOCK)

    greet(to_slots + to_owners)

    wide = r.qkv_ref[...].astype(F32)
    fill = jnp.zeros((PART, QK - 3 * width), F32)
    small = jnp.concatenate([r.small_ref[...], jnp.zeros((PART - 1, SMALL), F32)], 0)
    for t in range(N_SP):
        parts = [r.up_ref[:, t * PAGE : (t + 1) * PAGE].astype(F32)]
        parts += [wide[:, j * D + t * width : j * D + (t + 1) * width] for j in range(3)]
        r.pieces[t] = jnp.concatenate(parts + [fill, small], 1).astype(BF)

    await_greetings(to_slots + to_owners)

    def piece(q, k):
        t = lax.rem(sp + k, N_SP)
        pair = (r.p_send.at[q, k], r.p_recv.at[x, sp])
        return send(r.pieces.at[t], r.landed.at[x, sp], *pair, (half_dp[q], t))

    for q, k in others:
        piece(q, k).start()
    pltpu.make_async_copy(r.pieces.at[sp], r.landed.at[x, sp], r.p_recv.at[x, sp]).start()

    def row_copies(run):
        for i, (src, dst) in enumerate(
            ((r.down_ref, r.down_in.at[slot_x]), (r.dense_ref, r.dense_all.at[slot_at]))
        ):
            recv = r.r_recv.at[i, slot_x]
            for q, device in enumerate(to_slots):
                copy = send(src, dst, r.r_send.at[i, q], recv, device)
                to_partner(device, copy, src, dst, recv, run)

    row_copies("start")

    token_arrays = ((r.x_ref, r.x_all), (r.g_ref, r.g_all))

    def token_copies(i, kind):
        src, dst = token_arrays[i]
        if kind == "pass":
            there = dst.at[rows_of(across)]
            pair = (r.t_send.at[i, 2], r.t_recv.at[i, across])
            return send(there, there, *pair, (dp, sibling))
        to, n = (across, 0) if kind == "across" else (sibling, 1)
        pair = (r.t_send.at[i, n], r.t_recv.at[i, sp])
        return send(src, dst.at[rows_of(sp)], *pair, (dp, to))

    def token_start(i):
        src, dst = token_arrays[i]
        token_copies(i, "across").start()
        token_copies(i, "sibling").start()
        pltpu.make_async_copy(src, dst.at[rows_of(sp)], r.t_recv.at[i, sp]).start()

    def token_wait(i, s):
        src, dst = token_arrays[i]
        pltpu.make_async_copy(src, dst.at[rows_of(s)], r.t_recv.at[i, s]).wait()

    def token_pass(i):
        token_wait(i, across)
        token_copies(i, "pass").start()

    def token_rest(i):
        for s in (sp, sibling, sib_across):
            token_wait(i, s)

    token_start(0)

    smalls, up_0, up_1, down_0, down_1, qkv_n, dense_n = range(7)
    gathered = (
        (by_y, r.small_all), (by_y, r.up_a), (by_z, r.up_b), (by_y, r.down_a), (by_z, r.down_b),
        (by_z, r.qk_all), (by_y, r.dense_all),
    )
    cut = PAGE // 2

    def stage_a(n):
        path, out = gathered[n]
        mine = path.pair(out, path.first)
        return [
            send(mine, mine, r.a_send.at[n, k], r.a_recv.at[n, path.first], path.along_first(k)[0])
            for k in range(1, NY)
        ]

    def stage_b(n):
        plane, out = gathered[n]
        there = plane.block(out, plane.axis)
        return [
            send(there, there, r.b_send.at[n, k], r.b_recv.at[n, plane.axis], plane.along(k)[0])
            for k in range(1, NY)
        ]

    def start_a(n):
        for item in stage_a(n):
            item.start()

    def start_b(n):
        plane, out = gathered[n]
        for k in range(1, NY):
            a = plane.along_first(k)[1]
            local_wait(plane.pair(out, a), r.a_recv.at[n, a])
        for item in stage_b(n):
            item.start()

    def wait_b(n):
        plane, out = gathered[n]
        for k in range(1, NY):
            a = plane.along(k)[1]
            local_wait(plane.block(out, a), r.b_recv.at[n, a])

    for xx in range(NX):
        for s in range(N_SP):
            local_wait(r.landed.at[xx, s], r.p_recv.at[xx, s])
    for xx in range(NX):
        r.small_all[y, z, xx] = jnp.zeros((8, SMALL), F32)
        for s in range(N_SP):
            own = r.landed[xx, s].astype(F32)
            r.tight[s * PART : (s + 1) * PART, :] = own
            r.small_all[y, z, xx, s : s + 1, :] = own[0:1, PAGE + QK :]
        r.up_a[y, z, xx] = r.tight[:, :cut].astype(BF)
        r.up_b[y, z, xx] = r.tight[:, cut:PAGE].astype(BF)
        r.qk_all[y, z, xx] = r.tight[:, PAGE : PAGE + QK].astype(BF)
    start_a(smalls)
    start_a(up_0)
    start_a(up_1)
    for xx in range(NX):
        local_wait(r.down_in.at[xx], r.r_recv.at[0, xx])
        r.down_a[y, z, xx] = r.down_in[xx, :, :cut]
        r.down_b[y, z, xx] = r.down_in[xx, :, cut:]
    start_a(down_0)
    start_a(down_1)
    token_start(1)
    start_b(smalls)
    start_b(up_0)
    start_b(up_1)
    token_pass(0)
    start_b(down_0)
    start_b(down_1)
    for xx in range(NX):
        local_wait(r.dense_all.at[y, z, xx], r.r_recv.at[1, xx])
    start_a(qkv_n)
    start_a(dense_n)

    wait_b(smalls)
    packed = r.small_all[...].reshape(2 * n_own, SMALL).astype(BF)
    n_rows = 2 * n_own

    def owner_rows(size):
        row = iota((n_rows, size), 0)
        inside = lax.rem(row, 8)
        return jnp.where(inside < N_SP, row // 8 * N_SP + inside, -1)

    for n, (start, each, kind, size) in enumerate(VECTORS_IN):
        lane = column_of(iota((SMALL, size), 1), sp, kind)
        spread = (iota((SMALL, size), 0) == start + lax.rem(lane, each)).astype(BF)
        lane = column_of(iota((n_rows, size), 1), sp, kind)
        values = jnp.where(lane // each == owner_rows(size), dot(packed, spread), 0.0)
        r.vec_s[n : n + 1, :] = jnp.sum(values, 0, keepdims=True)
    gain_1, shift_1, gain_2, shift_2 = (r.vec_s[n : n + 1, :] for n in range(4))
    qkv_add = r.vec_s[4:5, :QK]
    up_add = r.vec_s[6:7, :]
    bias = r.vec_s[5:6, :] + r.vec_s[7:8, :]

    def fold(values):
        return jnp.sum(values.reshape(-1, 8, values.shape[-1]), 0)

    token_rest(0)

    @pl.loop(0, steps)
    def _(i):
        rows = rows_at(i)
        values = r.x_all[rows, :].astype(F32)
        centered = values - jnp.mean(values, -1, keepdims=True)
        xhat = centered * lax.rsqrt(jnp.mean(centered * centered, -1, keepdims=True) + 1e-05)
        r.xhat_s[rows, :] = xhat
        r.n1_s[rows, :] = (xhat * gain_1 + shift_1).astype(BF)
        r.n2_s[rows, :] = (xhat * gain_2 + shift_2).astype(BF)

    def join(src, dst, lane=0):
        @pl.loop(0, NY * NZ)
        def _(i):
            a, b = i // NZ, lax.rem(i, NZ)
            pair = [src[a, b, e].astype(F32) for e in range(NX)]
            own, wide_here = pair[0].shape[0] * NX, pair[0].shape[1]
            here = (pl.ds(pl.multiple_of(i * own, own), own), pl.ds(lane, wide_here))
            dst[here] = jnp.concatenate(pair, 0).astype(BF)

    token_pass(1)
    wait_b(up_0)
    join(r.up_a, r.up_s)
    wait_b(up_1)
    join(r.up_b, r.up_s, cut)

    zeros = jnp.zeros((8, D), F32)

    @pl.loop(0, steps)
    def _(i):
        rows = rows_at(i)
        pre = dot(r.n2_s[rows, :], r.up_s[...]) + up_add
        cdf = 0.5 * (1.0 + lax.erf(pre * 0.7071067811865476))
        r.act_s[rows, :] = (pre * cdf).astype(BF)
        pdf = jnp.exp(-0.5 * pre * pre) * 0.3989422804014327
        r.sum_s[rows, :] = cdf + pre * pdf

    start_b(qkv_n)
    start_b(dense_n)
    wait_b(down_0)
    join(r.down_a, r.down_s)
    wait_b(down_1)
    join(r.down_b, r.down_s, cut)
    token_rest(1)

    def first(i, sums):
        rows = rows_at(i)
        dact = dot_nt(r.g_all[rows, :], r.down_s[...])
        dpre = (dact * r.sum_s[rows, :]).astype(BF)
        r.dpre_s[rows, :] = dpre
        r.sum_s[rows, :] = dot(r.act_s[rows, :], r.down_s[...])
        dn2 = dot_nt(dpre, r.up_s[...])
        r.dx_s[rows, :] = dn2 * gain_2
        one, two, three = sums
        return (
            one + fold(dpre.astype(F32)),
            two + fold(dn2 * r.xhat_s[rows, :]),
            three + fold(dn2),
        )

    up_bias, gain_2_grad, shift_2_grad = lax.fori_loop(0, steps, first, (zeros,) * 3)

    half = D // 2
    in_half = half // (PART * N_SP)

    def weight_grad(left, right, out):
        @pl.loop(0, 2)
        def _(i):
            lanes = pl.ds(pl.multiple_of(i * half, half), half)
            value = dot_tn(left[:, lanes], right[...])
            own = PART * N_SP
            for c in range(in_half):
                at = (i * (NY // 2) + c // GROUP, c // NX % NZ, c % NX)
                out[at[0], at[1], at[2]] = value[c * own : (c + 1) * own, :].astype(BF)

    SMALLS, UP, DOWN, QKV, DENSE = range(5)
    reduced = (
        (by_y, r.small_g, r.small_1, r.small_m, r.small_2),
        (by_y, r.up_g, r.up_1, r.up_m, r.up_2),
        (by_z, r.down_g, r.down_1, r.down_m, r.down_2),
        (by_z, r.qk_g, r.qk_1, r.qk_m, r.qk_2),
        (by_y, r.dense_g, r.dense_1, r.dense_m, r.dense_2),
    )

    def stage_1(n):
        plane, src, land = reduced[n][:3]
        made = []
        for k in range(1, NY):
            device, a = plane.along(k)
            pair = (r.e_send.at[n, k], r.e_recv.at[n, plane.axis])
            made.append(send(plane.block(src, a), land.at[plane.axis], *pair, device))
        return made

    def stage_2(n):
        path, _, _, mid, land = reduced[n]
        made = []
        for k in range(1, NY):
            device, a = path.along_first(k)
            pair = (r.f_send.at[n, k], r.f_recv.at[n, path.first])
            made.append(send(mid.at[a], land.at[path.first], *pair, device))
        return made

    def start_1(n):
        for item in stage_1(n):
            item.start()

    def start_2(n):
        plane, src, land, mid, _ = reduced[n]
        for k in range(1, NY):
            a = plane.along(k)[1]
            local_wait(land.at[a], r.e_recv.at[n, a])

        @pl.loop(0, GROUP)
        def _(e):
            a, xx = e // NX, lax.rem(e, NX)
            own = src[plane.axis, a, xx] if plane.last == "y" else src[a, plane.axis, xx]
            total = own.astype(F32)
            for k in range(1, NY):
                total = total + land[lax.rem(plane.axis + k, NY), a, xx].astype(F32)
            mid[a, xx] = total.astype(mid.dtype)

        for item in stage_2(n):
            item.start()

    def finish(n):
        path, _, _, mid, land = reduced[n]
        for k in range(1, NY):
            a = path.along_first(k)[1]
            local_wait(land.at[a], r.f_recv.at[n, a])
        totals = []
        for xx in half_x:
            total = mid[path.first, xx].astype(F32)
            for k in range(1, NY):
                total = total + land[path.along_first(k)[1], xx].astype(F32)
            totals.append(total)
        return totals

    weight_grad(r.act_s, r.g_all, r.down_g)
    start_1(DOWN)
    weight_grad(r.n2_s, r.dpre_s, r.up_g)
    start_1(UP)

    wait_b(qkv_n)
    join(r.qk_all, r.qk_s)
    wait_b(dense_n)
    for e in range(NY * NZ * NX):
        r.dense_wide[e * PART : (e + 1) * PART, :] = r.dense_all[
            e // GROUP, e // NX % NZ, e % NX
        ].astype(F32)
    r.dense_s[...] = r.dense_wide[...].astype(BF)

    @pl.loop(0, steps)
    def _(i):
        rows = rows_at(i)
        y_rows = dot(r.n1_s[rows, :], r.qk_s[...]) + qkv_add
        cosine, sine = r.cos_ref[rows, :], r.sin_ref[rows, :]
        turned = []
        for p in range(2 * width // 128):
            u = y_rows[:, p * 128 : (p + 1) * 128]
            turned.append(u * cosine + swap_halves(u) * sine)
        d = dot_nt(r.g_all[rows, :], r.dense_s[...])

        def head(n):
            u = turned[n // 2]
            return u[:, (n % 2) * HEAD_DIM : (n % 2 + 1) * HEAD_DIM]

        for h in range(heads):
            at = 2 * width + h * HEAD_DIM
            r.q_s[h, rows, :] = head(h).astype(BF)
            r.k_s[h, rows, :] = head(heads + h).astype(BF)
            r.v_s[h, rows, :] = y_rows[:, at : at + HEAD_DIM].astype(BF)
            r.do_s[h, rows, :] = d[:, h * HEAD_DIM : (h + 1) * HEAD_DIM].astype(BF)

    scale = HEAD_DIM ** (-0.5)

    def attend(h):
        r.kt_s[...] = r.k_s[h].astype(F32).T.astype(BF)
        r.vt_s[...] = r.v_s[h].astype(F32).T.astype(BF)
        for i in reversed(range(steps)):
            keys = (i + 1) * BLOCK
            rows = slice(i * BLOCK, (i + 1) * BLOCK)
            q, do = r.q_s[h, rows, :], r.do_s[h, rows, :]
            scores = dot_nt(r.k_s[h, :keys, :], q) * scale
            hidden = iota((BLOCK, BLOCK), 0) > iota((BLOCK, BLOCK), 1)
            corner = jnp.where(hidden, -1e30, scores[i * BLOCK :, :])
            scores = jnp.concatenate([scores[: i * BLOCK, :], corner], 0) if i else corner
            expo = jnp.exp(scores - jnp.max(scores, 0, keepdims=True))
            probs = expo * (1.0 / jnp.sum(expo, 0, keepdims=True))
            low = probs.astype(BF)
            r.ctxt_s[h, :, rows] = dot(r.vt_s[:, :keys], low).astype(BF)
            dprobs = dot_nt(r.v_s[h, :keys, :], do)
            delta = jnp.sum(probs * dprobs, 0, keepdims=True)
            dscores = (probs * (dprobs - delta) * scale).astype(BF)
            r.dq_s[h, rows, :] = dot(r.kt_s[:, :keys], dscores).T.astype(BF)
            dk = dot(dscores, q)
            dv = dot(low, do)
            if i == steps - 1:
                r.dk_s[h] = dk
                r.dv_s[h] = dv
            else:
                r.dk_s[h, :keys, :] += dk
                r.dv_s[h, :keys, :] += dv

    @pl.loop(0, heads)
    def _(h):
        attend(h)

        @pl.when(h == 0)
        def _():
            start_2(DOWN)

        @pl.when(h == 1)
        def _():
            start_2(UP)

    sums_of = (r.act_s, r.dpre_s)

    def token_pair(i):
        src = sums_of[i]
        return [
            send(
                src.at[rows_of(t)], r.token_in.at[i, n], r.g_send.at[i, n], r.g_recv.at[i, n],
                (dp, sibling),
            )
            for n, t in enumerate((sibling, sib_across))
        ]

    def token_far_copy(i):
        pair = (r.h_send.at[i], r.h_recv.at[i])
        return send(r.token_mid.at[i], r.token_far.at[i], *pair, (dp, across))

    def token_cross(i):
        for item in token_pair(i):
            item.wait_recv()
        own = sums_of[i][rows_of(across), :].astype(F32)
        r.token_mid[i] = (own + r.token_in[i, 1].astype(F32)).astype(BF)
        token_far_copy(i).start()

    def token_total(i):
        token_far_copy(i).wait()
        own = sums_of[i][rows_of(sp), :].astype(F32)
        return own + r.token_in[i, 0].astype(F32) + r.token_far[i].astype(F32)

    ctxt = r.ctxt_s[...].reshape(width, length)
    for i in range(steps):
        rows = slice(i * BLOCK, (i + 1) * BLOCK)
        r.act_s[rows, :] = (r.sum_s[rows, :] + dot_tn(ctxt[:, rows], r.dense_s[...])).astype(BF)
    for item in token_pair(0):
        item.start()

    def last(i, sums):
        rows = rows_at(i)
        cosine, sine = r.cos_ref[rows, :], r.sin_ref[rows, :]
        parts = [
            ref[h, rows, :].astype(F32) for ref in (r.dq_s, r.dk_s, r.dv_s) for h in range(heads)
        ]
        blocks = []
        for p in range(2 * width // 128):
            u = jnp.concatenate(parts[2 * p : 2 * p + 2], 1).astype(BF).astype(F32)
            blocks.append((u * cosine - swap_halves(u) * sine).astype(BF))
        rest = parts[2 * heads :] + [jnp.zeros((BLOCK, QK - 3 * width), F32)]
        dqkv = jnp.concatenate(blocks + [jnp.concatenate(rest, 1).astype(BF)], 1)
        r.dqkv_s[rows, :] = dqkv
        dn1 = dot_nt(dqkv, r.qk_s[...])
        r.dpre_s[rows, :] = (r.dx_s[rows, :] + dn1 * gain_1).astype(BF)
        one, two, three = sums
        return (
            one + fold(dqkv.astype(F32)),
            two + fold(dn1 * r.xhat_s[rows, :]),
            three + fold(dn1),
        )

    qkv_bias, gain_1_grad, shift_1_grad = lax.fori_loop(
        0, steps, last, (jnp.zeros((8, QK), F32), zeros, zeros)
    )
    weight_grad(r.n1_s, r.dqkv_s, r.qk_g)
    start_1(QKV)
    for item in token_pair(1):
        item.start()
    token_cross(0)
    dense_grad = dot(ctxt, r.g_all[...])
    for e in range(NY * NZ * NX):
        r.dense_g[e // GROUP, e // NX % NZ, e % NX] = dense_grad[
            e * PART : (e + 1) * PART, :
        ].astype(BF)
    start_1(DENSE)

    g_here = r.g_all[rows_of(sp), :].astype(F32)
    values = (
        gain_1_grad, shift_1_grad, gain_2_grad, shift_2_grad, qkv_bias, fold(g_here), up_bias
    )
    result = jnp.zeros((n_rows, SMALL), F32)
    for (start, each, kind, _), item in zip(VECTORS_OUT, values):
        vector = jnp.sum(item, 0, keepdims=True)
        size = vector.shape[1]
        lane = column_of(iota((n_rows, size), 1), sp, kind)
        mine = lane // each == owner_rows(size)
        if kind == "qkv":
            mine = jnp.logical_and(mine, iota((n_rows, size), 1) < 3 * width)
        rest = jnp.where(mine, vector, 0.0)
        lane = column_of(iota((size, SMALL), 0), sp, kind)
        pick = (iota((size, SMALL), 1) == start + lax.rem(lane, each)).astype(BF)
        for _ in range(3):
            part = rest.astype(BF)
            result = result + dot(part, pick)
            rest = rest - part.astype(F32)
    for e in range(NY * NZ * NX):
        r.small_g[e // GROUP, e // NX % NZ, e % NX] = result[e * 8 : (e + 1) * 8, :]
    start_1(SMALLS)
    token_cross(1)
    start_2(QKV)

    def store_pieces(totals, out):
        for q, total in enumerate(totals):
            for t in range(N_SP):
                out[q, t] = total[t * PART : (t + 1) * PART, :]

    def back(n, q, k):
        src, land = ((r.up_p, r.up_l), (r.qk_p, r.qk_l), (r.small_t, r.small_l))[n]
        t = lax.rem(sp + k, N_SP)
        pair = (r.i_send.at[n, q, k], r.i_recv.at[n, x, sp])
        here = src.at[q] if n == 2 else src.at[q, t]
        return send(here, land.at[x, sp], *pair, (half_dp[q], t))

    def start_back(n):
        for q, k in others:
            back(n, q, k).start()

    store_pieces(finish(UP), r.up_p)
    start_back(0)
    owned = ((r.down_t, r.down_l), (r.dense_t, r.dense_l))

    def own_copies(i, run):
        src, dst = owned[i]
        recv = r.j_recv.at[i, x]
        for q, device in enumerate(to_owners):
            copy = send(src.at[q], dst.at[x], r.j_send.at[i, q], recv, device)
            to_partner(device, copy, src.at[q], dst.at[x], recv, run)

    for q, total in enumerate(finish(DOWN)):
        r.down_t[q] = total
    own_copies(0, "start")
    start_2(DENSE)
    start_2(SMALLS)
    store_pieces(finish(QKV), r.qk_p)
    start_back(1)
    for q, total in enumerate(finish(DENSE)):
        r.dense_t[q] = total
    own_copies(1, "start")
    for q, total in enumerate(finish(SMALLS)):
        r.small_t[q] = total
    start_back(2)

    x_here = r.x_all[rows_of(sp), :].astype(F32)
    r.hidden_out[...] = (x_here + token_total(0) + bias).astype(BF)
    dxhat = token_total(1)
    centered = x_here - jnp.mean(x_here, -1, keepdims=True)
    rstd = lax.rsqrt(jnp.mean(centered * centered, -1, keepdims=True) + 1e-05)
    xhat = centered * rstd
    r.hidden_grad[...] = (
        r.g_all[rows_of(sp), :].astype(F32)
        + rstd
        * (
            dxhat
            - jnp.mean(dxhat, -1, keepdims=True)
            - xhat * jnp.mean(dxhat * xhat, -1, keepdims=True)
        )
    ).astype(BF)

    r.up_l[x, sp] = r.up_p[0, sp]
    r.qk_l[x, sp] = r.qk_p[0, sp]
    r.small_l[x, sp] = r.small_t[0]

    def wait_back(n, land):
        for q, k in others:
            s = lax.rem(sp + k, N_SP)
            local_wait(land.at[half_x[q], s], r.i_recv.at[n, half_x[q], s])

    wait_back(0, r.up_l)
    for s in range(N_SP):
        r.up_out[:, s * PAGE : (s + 1) * PAGE] = r.up_l[0, s] + r.up_l[1, s]
    for i, out in enumerate((r.down_out, r.dense_out)):
        land = owned[i][1]
        for xx in range(NX):
            local_wait(land.at[xx], r.j_recv.at[i, xx])
        out[...] = land[0] + land[1]
    wait_back(1, r.qk_l)
    for s in range(N_SP):
        block = r.qk_l[0, s] + r.qk_l[1, s]
        for j in range(3):
            to = j * D + s * width
            r.qkv_out[:, to : to + width] = block[:, j * width : (j + 1) * width]
    wait_back(2, r.small_l)
    r.small_out[...] = jnp.sum(jnp.sum(r.small_l[...], 0), 0)

    for i in range(2):
        for kind in ("across", "sibling", "pass"):
            token_copies(i, kind).wait_send()

    row_copies("wait_send")
    for i in range(2):
        own_copies(i, "wait_send")
    for q, k in others:
        piece(q, k).wait_send()
        for n in range(3):
            back(n, q, k).wait_send()
    for i in range(2):
        for item in token_pair(i):
            item.wait_send()
    for n in range(len(gathered)):
        for item in stage_a(n) + stage_b(n):
            item.wait_send()
    for n in range(len(reduced)):
        for item in stage_1(n) + stage_2(n):
            item.wait_send()


def layer(x, g, up, qkv, small, down, dense):
    tokens = x.shape[0]
    length = tokens * N_SP
    heads = HEADS // N_SP
    width = heads * HEAD_DIM
    grid = (NY, NZ, NX)
    own = PART * N_SP
    cosine, sine = rotary_tables(length)
    dma = pltpu.SemaphoreType.DMA
    anywhere = pl.BlockSpec(memory_space=pl.ANY)
    vmem = pl.BlockSpec(memory_space=pltpu.VMEM)
    ins = ("x_ref", "g_ref", "up_ref", "qkv_ref", "small_ref", "down_ref", "dense_ref")
    ins += ("cos_ref", "sin_ref")
    outs = {
        "hidden_out": ((tokens, D), BF),
        "hidden_grad": ((tokens, D), BF),
        "up_out": ((PART, FF), F32),
        "qkv_out": ((PART, 3 * D), F32),
        "down_out": ((own, D), F32),
        "dense_out": ((PART, D), F32),
        "small_out": ((8, SMALL), F32),
    }
    chunk = {
        "up": ((own, PAGE), BF),
        "down": ((own, D), BF),
        "qk": ((own, QK), BF),
        "dense": ((PART, D), BF),
        "small": ((8, SMALL), F32),
    }
    scratch = {}
    for name, (shape, kind) in chunk.items():
        if name in ("up", "down"):
            scratch[name + "_a"] = (grid + (own, PAGE // 2), kind)
            scratch[name + "_b"] = (grid + (own, PAGE // 2), kind)
        else:
            scratch[name + "_all"] = (grid + shape, kind)
        scratch[name + "_g"] = (grid + shape, kind)
        scratch[name + "_1"] = (grid + shape, kind)
        scratch[name + "_m"] = ((GROUP // NX, NX) + shape, kind)
        scratch[name + "_2"] = ((GROUP // NX, NX) + shape, kind)
    per_head = (heads, length, HEAD_DIM)
    scratch.update(
        x_all=((length, D), BF),
        g_all=((length, D), BF),
        pieces=((N_SP, PART, PAGE + QK + SMALL), BF),
        landed=((NX, N_SP, PART, PAGE + QK + SMALL), BF),
        tight=((own, PAGE + QK + SMALL), F32),
        up_s=((D, PAGE), BF),
        down_s=((PAGE, D), BF),
        qk_s=((D, QK), BF),
        down_in=((NX, own, D), BF),
        dense_wide=((width, D), F32),
        dense_s=((width, D), BF),
        vec_s=((8, PAGE), F32),
        xhat_s=((length, D), F32),
        n1_s=((length, D), BF),
        n2_s=((length, D), BF),
        act_s=((length, PAGE), BF),
        dpre_s=((length, PAGE), BF),
        sum_s=((length, D), F32),
        dx_s=((length, D), F32),
        dqkv_s=((length, QK), BF),
        q_s=(per_head, BF),
        k_s=(per_head, BF),
        v_s=(per_head, BF),
        do_s=(per_head, BF),
        dq_s=(per_head, BF),
        dk_s=(per_head, F32),
        dv_s=(per_head, F32),
        kt_s=((HEAD_DIM, length), BF),
        vt_s=((HEAD_DIM, length), BF),
        ctxt_s=((heads, HEAD_DIM, length), BF),
        token_in=((2, 2, tokens, D), BF),
        token_mid=((2, tokens, D), BF),
        token_far=((2, tokens, D), BF),
        up_p=((NX, N_SP, PART, PAGE), F32),
        up_l=((NX, N_SP, PART, PAGE), F32),
        qk_p=((NX, N_SP, PART, QK), F32),
        qk_l=((NX, N_SP, PART, QK), F32),
        down_t=((NX, own, D), F32),
        down_l=((NX, own, D), F32),
        dense_t=((NX, PART, D), F32),
        dense_l=((NX, PART, D), F32),
        small_t=((NX, 8, SMALL), F32),
        small_l=((NX, N_SP, 8, SMALL), F32),
    )
    semaphores = {
        "r": (2, NX), "p": (NX, N_SP), "t": (2, N_SP), "a": (7, NY), "b": (7, NY), "e": (5, NY),
        "f": (5, NY), "g": (2, 2), "h": (2,), "j": (2, NX),
    }
    names = list(ins) + list(outs) + list(scratch)
    shapes = [pltpu.VMEM(shape, kind) for shape, kind in scratch.values()]
    for name, shape in semaphores.items():
        names += [name + "_send", name + "_recv"]
        shapes += [dma(shape), dma(shape)]
    names += ["i_send", "i_recv"]
    shapes += [dma((3, NX, N_SP)), dma((3, NX, N_SP))]
    return pl.pallas_call(
        functools.partial(layer_kernel, names),
        out_shape=tuple(jax.ShapeDtypeStruct(*item) for item in outs.values()),
        in_specs=[anywhere, anywhere, vmem, vmem, vmem, anywhere, anywhere, vmem, vmem],
        out_specs=(vmem,) * len(outs),
        scratch_shapes=shapes,
        compiler_params=pltpu.CompilerParams(
            collective_id=0, has_side_effects=True, vmem_limit_bytes=61 * 1024 * 1024
        ),
        cost_estimate=pl.CostEstimate(
            flops=14_000_000_000, bytes_accessed=16_000_000, transcendentals=6_000_000
        ),
        name="layer",
    )(x, g, up, qkv, small, down, dense, cosine, sine)


def outputs_kernel(*refs):
    n = 6
    small_ref, outs = refs[n], refs[n + 1 :]
    for i in range(n):
        outs[i][...] = refs[i][...]
    mine = small_ref[pl.ds(lax.axis_index("sp"), 1), :]
    for (start, each, _, _), out in zip(VECTORS_OUT + VECTORS_OUT[5:6], outs[n:]):
        out[...] = mine[:, start : start + each]


def write_outputs(*arrays):
    vmem = pl.BlockSpec(memory_space=pltpu.VMEM)
    large = [jax.ShapeDtypeStruct(item.shape, item.dtype) for item in arrays[:-1]]
    small = [
        jax.ShapeDtypeStruct((1, each), F32) for _, each, _, _ in VECTORS_OUT + VECTORS_OUT[5:6]
    ]
    return pl.pallas_call(
        outputs_kernel,
        out_shape=tuple(large + small),
        in_specs=[vmem] * len(arrays),
        out_specs=(vmem,) * (len(large) + len(small)),
        name="outputs",
    )(*arrays)


def local(
    hidden_in,
    cotangent,
    attn_gain,
    attn_shift,
    mlp_gain,
    mlp_shift,
    qkv_weight,
    qkv_bias,
    dense_weight,
    dense_bias,
    up_weight,
    up_bias,
    down_weight,
    down_bias,
):
    small = (
        attn_gain,
        attn_shift,
        mlp_gain,
        mlp_shift,
        qkv_bias,
        dense_bias,
        up_bias,
        down_bias,
    )
    packed = jnp.zeros((SMALL,), F32)
    at = 0
    for item in small:
        size = item.shape[0]
        packed = packed + jnp.pad(item.astype(F32), (at, SMALL - at - size))
        at += size
    results = layer(
        hidden_in,
        cotangent,
        up_weight,
        qkv_weight,
        packed.reshape(1, SMALL),
        down_weight,
        dense_weight,
    )
    results = write_outputs(*results)
    hidden_out, hidden_grad, up_own, qkv_own, down_own, dense_own = results[:6]
    parts = [item.reshape(-1) for item in results[6:]]
    return (
        hidden_out,
        hidden_grad,
        parts[0],
        parts[1],
        parts[2],
        parts[3],
        qkv_own,
        parts[4],
        dense_own,
        parts[5],
        up_own,
        parts[6],
        down_own,
        parts[7],
    )


def solution(mesh):
    matrix = P(BOTH, None)
    vector = P(BOTH)
    split = (matrix, matrix) + (vector,) * 4 + (matrix, vector) * 4
    return jax.shard_map(local, mesh=mesh, in_specs=split, out_specs=split, check_vma=False)
```

```python
import functools
import types

import jax
import jax.numpy as jnp
import numpy as np
from jax import lax
from jax.experimental import pallas as pl
from jax.experimental.pallas import tpu as pltpu
from jax.sharding import PartitionSpec as P

D = 768
HEADS = 12
HEAD_DIM = 64
ROT = 16
FF = 3072
BF = jnp.bfloat16
F32 = jnp.float32
BOTH = ("dp", "sp")


def dot(left, right):
    return jnp.dot(left, right, preferred_element_type=F32)


MESH = pl.DeviceIdType.MESH
SMALL = 128
PAGE = 768
NY, NZ, NX = 4, 4, 2
GROUP = NZ * NX
N_SP = 4
PART = 6


def place():
    dp, sp = lax.axis_index("dp"), lax.axis_index("sp")
    return dp, sp, dp // GROUP, lax.rem(dp // NX, NZ), lax.rem(dp, NX)


def send(src, dst, send_sem, recv_sem, device):
    return pltpu.make_async_remote_copy(
        src_ref=src,
        dst_ref=dst,
        send_sem=send_sem,
        recv_sem=recv_sem,
        device_id=device,
        device_id_type=MESH,
    )


def index_of(y, z, x):
    return (y * NZ + z) * NX + x


def slot_device(dp, sp):
    line = dp * N_SP + sp
    return lax.rem(line, NY * GROUP), line // (NY * GROUP)


def owner_device(dp, sp):
    line = sp * NY * GROUP + dp
    return line // N_SP, lax.rem(line, N_SP)


def differs(device, dp, sp):
    return jnp.logical_or(device[0] != dp, device[1] != sp)


def other_half(dp):
    return dp + 1 - 2 * lax.rem(dp, NX)


class Path:
    def __init__(self, last):
        self.last = last
        dp, self.sp, self.y, self.z, self.x = place()
        self.first, self.axis = (self.z, self.y) if last == "y" else (self.y, self.z)

    def along_first(self, k):
        a = lax.rem(self.first + k, NY)
        y, z = (self.y, a) if self.last == "y" else (a, self.z)
        return (index_of(y, z, self.x), self.sp), a

    def along(self, k):
        a = lax.rem(self.axis + k, NY)
        y, z = (a, self.z) if self.last == "y" else (self.y, a)
        return (index_of(y, z, self.x), self.sp), a

    def block(self, ref, a):
        return ref.at[a] if self.last == "y" else ref.at[:, a]

    def pair(self, ref, a):
        return ref.at[self.y, a] if self.last == "y" else ref.at[a, self.z]


def greet(partners):
    dp, sp, y, z, x = place()
    barrier = pltpu.get_barrier_semaphore()

    def signal(device):
        pl.semaphore_signal(barrier, inc=1, device_id=device, device_id_type=MESH)

    for k in range(N_SP):
        if k:
            signal((dp, lax.rem(sp + k, N_SP)))
        signal((other_half(dp), lax.rem(sp + k, N_SP)))
    by_y, by_z = Path("y"), Path("z")
    for k in range(1, NY):
        signal(by_y.along(k)[0])
        signal(by_z.along(k)[0])
    for partner in partners:

        @pl.when(differs(partner, dp, sp))
        def _():
            signal(partner)


def await_greetings(partners):
    dp, sp, y, z, x = place()
    count = 2 * N_SP - 1 + 2 * (NY - 1)
    for partner in partners:
        count = count + jnp.where(differs(partner, dp, sp), 1, 0)
    pl.semaphore_wait(pltpu.get_barrier_semaphore(), count)


BLOCK = 256


def dot_nt(left, right):
    return lax.dot_general(left, right, (((1,), (1,)), ((), ())), preferred_element_type=F32)


def dot_tn(left, right):
    return lax.dot_general(left, right, (((0,), (0,)), ((), ())), preferred_element_type=F32)


def iota(shape, axis):
    return lax.broadcasted_iota(jnp.int32, shape, axis)


def rotary_tables(length):
    half = ROT // 2
    frequency = np.float32(10000.0) ** (np.float32(-2.0) * np.arange(half, dtype=np.float32) / ROT)
    angles = np.arange(length, dtype=np.float32)[:, None] * frequency[None, :].astype(np.float32)
    cosine = np.ones((length, HEAD_DIM), np.float32)
    sine = np.zeros((length, HEAD_DIM), np.float32)
    cosine[:, :half] = cosine[:, half:ROT] = np.cos(angles)
    sine[:, :half] = -np.sin(angles)
    sine[:, half:ROT] = np.sin(angles)
    return jnp.asarray(np.tile(cosine, (1, 2))), jnp.asarray(np.tile(sine, (1, 2)))


def swap_halves(u):
    low = lax.rem(iota(u.shape, 1), 16) < 8
    return jnp.where(low, pltpu.roll(u, 120, 1), pltpu.roll(u, 8, 1))


def column_of(c, sp, kind):
    if kind == "qkv":
        width = D // N_SP
        return (c // width) * D + sp * width + lax.rem(c, width)
    return c + sp * (FF // N_SP) if kind == "up" else c


VECTORS_IN = (
    (0, 6, "", D), (6, 6, "", D), (12, 6, "", D), (18, 6, "", D),
    (24, 18, "qkv", PAGE), (42, 6, "", D), (48, 24, "up", PAGE), (72, 6, "", D),
)
VECTORS_OUT = (
    (0, 6, "", D), (6, 6, "", D), (12, 6, "", D), (18, 6, "", D),
    (24, 18, "qkv", PAGE), (42, 6, "", D), (48, 24, "up", PAGE),
)


QK = 640


def layer_kernel(names, *refs):
    r = types.SimpleNamespace(**dict(zip(names, refs)))
    dp, sp, y, z, x = place()
    half_dp = (dp, other_half(dp))
    half_x = (x, 1 - x)
    slot, column = slot_device(dp, sp)
    to_slots = ((slot, column), (other_half(slot), column))
    to_owners = tuple(owner_device(d, sp) for d in half_dp)
    slot_x = lax.rem(slot, NX)
    sibling = sp + 1 - 2 * lax.rem(sp, 2)
    across = lax.rem(sp + 2, N_SP)
    sib_across = lax.rem(sibling + 2, N_SP)
    others = [(q, k) for q in range(NX) for k in range(N_SP) if q or k]
    by_y, by_z = Path("y"), Path("z")
    length = r.x_all.shape[0]
    tokens = length // N_SP
    heads = HEADS // N_SP
    width = heads * HEAD_DIM
    n_own = NY * NZ * NX * N_SP
    steps = length // BLOCK
    slot_at = (slot // GROUP, lax.rem(slot // NX, NZ), slot_x)

    def to_partner(device, copy, src, dst, recv, run):
        @pl.when(differs(device, dp, sp))
        def _():
            getattr(copy, run)()

        if run == "start":

            @pl.when(jnp.logical_not(differs(device, dp, sp)))
            def _():
                pltpu.make_async_copy(src, dst, recv).start()

    def local_wait(ref, sem):
        pltpu.make_async_copy(ref, ref, sem).wait()

    def rows_of(s):
        return pl.ds(pl.multiple_of(s * tokens, tokens), tokens)

    def rows_at(i):
        return pl.ds(pl.multiple_of(i * BLOCK, BLOCK), BLOCK)

    greet(to_slots + to_owners)

    wide = r.qkv_ref[...].astype(F32)
    fill = jnp.zeros((PART, QK - 3 * width), F32)
    small = jnp.concatenate([r.small_ref[...], jnp.zeros((PART - 1, SMALL), F32)], 0)
    for t in range(N_SP):
        parts = [r.up_ref[:, t * PAGE : (t + 1) * PAGE].astype(F32)]
        parts += [wide[:, j * D + t * width : j * D + (t + 1) * width] for j in range(3)]
        r.pieces[t] = jnp.concatenate(parts + [fill, small], 1).astype(BF)

    await_greetings(to_slots + to_owners)

    def piece(q, k):
        t = lax.rem(sp + k, N_SP)
        pair = (r.p_send.at[q, k], r.p_recv.at[x, sp])
        return send(r.pieces.at[t], r.landed.at[x, sp], *pair, (half_dp[q], t))

    for q, k in others:
        piece(q, k).start()
    pltpu.make_async_copy(r.pieces.at[sp], r.landed.at[x, sp], r.p_recv.at[x, sp]).start()

    def row_copies(run):
        for i, (src, dst) in enumerate(
            ((r.down_ref, r.down_in.at[slot_x]), (r.dense_ref, r.dense_all.at[slot_at]))
        ):
            recv = r.r_recv.at[i, slot_x]
            for q, device in enumerate(to_slots):
                copy = send(src, dst, r.r_send.at[i, q], recv, device)
                to_partner(device, copy, src, dst, recv, run)

    row_copies("start")

    token_arrays = ((r.x_ref, r.x_all), (r.g_ref, r.g_all))

    def token_copies(i, kind):
        src, dst = token_arrays[i]
        if kind == "pass":
            there = dst.at[rows_of(across)]
            pair = (r.t_send.at[i, 2], r.t_recv.at[i, across])
            return send(there, there, *pair, (dp, sibling))
        to, n = (across, 0) if kind == "across" else (sibling, 1)
        pair = (r.t_send.at[i, n], r.t_recv.at[i, sp])
        return send(src, dst.at[rows_of(sp)], *pair, (dp, to))

    def token_start(i):
        src, dst = token_arrays[i]
        token_copies(i, "across").start()
        token_copies(i, "sibling").start()
        pltpu.make_async_copy(src, dst.at[rows_of(sp)], r.t_recv.at[i, sp]).start()

    def token_wait(i, s):
        src, dst = token_arrays[i]
        pltpu.make_async_copy(src, dst.at[rows_of(s)], r.t_recv.at[i, s]).wait()

    def token_pass(i):
        token_wait(i, across)
        token_copies(i, "pass").start()

    def token_rest(i):
        for s in (sp, sibling, sib_across):
            token_wait(i, s)

    token_start(0)

    smalls, up_0, up_1, down_0, down_1, qkv_n, dense_n = range(7)
    gathered = (
        (by_y, r.small_all), (by_y, r.up_a), (by_z, r.up_b), (by_y, r.down_a), (by_z, r.down_b),
        (by_z, r.qk_all), (by_y, r.dense_all),
    )
    cut = PAGE // 2

    def stage_a(n):
        path, out = gathered[n]
        mine = path.pair(out, path.first)
        return [
            send(mine, mine, r.a_send.at[n, k], r.a_recv.at[n, path.first], path.along_first(k)[0])
            for k in range(1, NY)
        ]

    def stage_b(n):
        path, out = gathered[n]
        there = path.block(out, path.axis)
        return [
            send(there, there, r.b_send.at[n, k], r.b_recv.at[n, path.axis], path.along(k)[0])
            for k in ((1, 2, 3) if n == smalls else (1, 3))
        ]

    def half_block(n, a, part):
        path, out = gathered[n]
        some = pl.ds(part * (NZ // 2), NZ // 2)
        return out.at[a, some] if path.last == "y" else out.at[some, a]

    def passed_on(n, part):
        path = gathered[n][0]
        there = half_block(n, path.along((3, 1)[part])[1], part)
        pair = (r.q_send.at[n, part], r.q_recv.at[n, part])
        return send(there, there, *pair, path.along((1, 3)[part])[0])

    def start_on(n):
        path, out = gathered[n]
        for part in range(2):
            a = path.along((3, 1)[part])[1]
            local_wait(path.block(out, a), r.b_recv.at[n, a])
            passed_on(n, part).start()

    def start_a(n):
        for item in stage_a(n):
            item.start()

    def start_b(n):
        plane, out = gathered[n]
        for k in range(1, NY):
            a = plane.along_first(k)[1]
            local_wait(plane.pair(out, a), r.a_recv.at[n, a])
        for item in stage_b(n):
            item.start()

    def wait_b(n):
        path, out = gathered[n]
        if n == smalls:
            for k in range(1, NY):
                a = path.along(k)[1]
                local_wait(path.block(out, a), r.b_recv.at[n, a])
        else:
            for part in range(2):
                local_wait(half_block(n, path.along(2)[1], part), r.q_recv.at[n, part])

    for xx in range(NX):
        for s in range(N_SP):
            local_wait(r.landed.at[xx, s], r.p_recv.at[xx, s])
    for xx in range(NX):
        r.small_all[y, z, xx] = jnp.zeros((8, SMALL), F32)
        for s in range(N_SP):
            own = r.landed[xx, s].astype(F32)
            r.tight[s * PART : (s + 1) * PART, :] = own
            r.small_all[y, z, xx, s : s + 1, :] = own[0:1, PAGE + QK :]
        r.up_a[y, z, xx] = r.tight[:, :cut].astype(BF)
        r.up_b[y, z, xx] = r.tight[:, cut:PAGE].astype(BF)
        r.qk_all[y, z, xx] = r.tight[:, PAGE : PAGE + QK].astype(BF)
    start_a(smalls)
    start_a(up_0)
    start_a(up_1)
    for xx in range(NX):
        local_wait(r.down_in.at[xx], r.r_recv.at[0, xx])
        r.down_a[y, z, xx] = r.down_in[xx, :, :cut]
        r.down_b[y, z, xx] = r.down_in[xx, :, cut:]
    start_a(down_0)
    start_a(down_1)
    token_start(1)
    start_b(smalls)
    start_b(up_0)
    start_b(up_1)
    token_pass(0)
    start_b(down_0)
    start_b(down_1)
    start_on(up_0)
    start_on(up_1)
    for xx in range(NX):
        local_wait(r.dense_all.at[y, z, xx], r.r_recv.at[1, xx])
    start_a(qkv_n)
    start_a(dense_n)

    wait_b(smalls)
    packed = r.small_all[...].reshape(2 * n_own, SMALL).astype(BF)
    n_rows = 2 * n_own

    def owner_rows(size):
        row = iota((n_rows, size), 0)
        inside = lax.rem(row, 8)
        return jnp.where(inside < N_SP, row // 8 * N_SP + inside, -1)

    for n, (start, each, kind, size) in enumerate(VECTORS_IN):
        lane = column_of(iota((SMALL, size), 1), sp, kind)
        spread = (iota((SMALL, size), 0) == start + lax.rem(lane, each)).astype(BF)
        lane = column_of(iota((n_rows, size), 1), sp, kind)
        values = jnp.where(lane // each == owner_rows(size), dot(packed, spread), 0.0)
        r.vec_s[n : n + 1, :] = jnp.sum(values, 0, keepdims=True)
    gain_1, shift_1, gain_2, shift_2 = (r.vec_s[n : n + 1, :] for n in range(4))
    qkv_add = r.vec_s[4:5, :QK]
    up_add = r.vec_s[6:7, :]
    bias = r.vec_s[5:6, :] + r.vec_s[7:8, :]

    def fold(values):
        return jnp.sum(values.reshape(-1, 8, values.shape[-1]), 0)

    token_rest(0)

    @pl.loop(0, steps)
    def _(i):
        rows = rows_at(i)
        values = r.x_all[rows, :].astype(F32)
        centered = values - jnp.mean(values, -1, keepdims=True)
        xhat = centered * lax.rsqrt(jnp.mean(centered * centered, -1, keepdims=True) + 1e-05)
        r.xhat_s[rows, :] = xhat
        r.n1_s[rows, :] = (xhat * gain_1 + shift_1).astype(BF)
        r.n2_s[rows, :] = (xhat * gain_2 + shift_2).astype(BF)

    def join(src, dst, lane=0):
        @pl.loop(0, NY * NZ)
        def _(i):
            a, b = i // NZ, lax.rem(i, NZ)
            pair = [src[a, b, e].astype(F32) for e in range(NX)]
            own, wide_here = pair[0].shape[0] * NX, pair[0].shape[1]
            here = (pl.ds(pl.multiple_of(i * own, own), own), pl.ds(lane, wide_here))
            dst[here] = jnp.concatenate(pair, 0).astype(BF)

    start_on(down_0)
    start_on(down_1)
    token_pass(1)
    wait_b(up_0)
    join(r.up_a, r.up_s)
    wait_b(up_1)
    join(r.up_b, r.up_s, cut)

    zeros = jnp.zeros((8, D), F32)

    @pl.loop(0, steps)
    def _(i):
        rows = rows_at(i)
        pre = dot(r.n2_s[rows, :], r.up_s[...]) + up_add
        cdf = 0.5 * (1.0 + lax.erf(pre * 0.7071067811865476))
        r.act_s[rows, :] = (pre * cdf).astype(BF)
        pdf = jnp.exp(-0.5 * pre * pre) * 0.3989422804014327
        r.sum_s[rows, :] = cdf + pre * pdf

    start_b(qkv_n)
    start_b(dense_n)
    wait_b(down_0)
    join(r.down_a, r.down_s)
    wait_b(down_1)
    join(r.down_b, r.down_s, cut)
    token_rest(1)

    def first(i, sums):
        rows = rows_at(i)
        dact = dot_nt(r.g_all[rows, :], r.down_s[...])
        dpre = (dact * r.sum_s[rows, :]).astype(BF)
        r.dpre_s[rows, :] = dpre
        r.sum_s[rows, :] = dot(r.act_s[rows, :], r.down_s[...])
        dn2 = dot_nt(dpre, r.up_s[...])
        r.dx_s[rows, :] = dn2 * gain_2
        one, two, three = sums
        return (
            one + fold(dpre.astype(F32)),
            two + fold(dn2 * r.xhat_s[rows, :]),
            three + fold(dn2),
        )

    up_bias, gain_2_grad, shift_2_grad = lax.fori_loop(0, steps, first, (zeros,) * 3)
    start_on(qkv_n)
    start_on(dense_n)

    half = D // 2
    in_half = half // (PART * N_SP)

    def weight_grad(left, right, out):
        @pl.loop(0, 2)
        def _(i):
            lanes = pl.ds(pl.multiple_of(i * half, half), half)
            value = dot_tn(left[:, lanes], right[...])
            own = PART * N_SP
            for c in range(in_half):
                at = (i * (NY // 2) + c // GROUP, c // NX % NZ, c % NX)
                out[at[0], at[1], at[2]] = value[c * own : (c + 1) * own, :].astype(BF)

    SMALLS, UP, DOWN, QKV, DENSE = range(5)
    reduced = (
        (by_y, r.small_g, r.small_1, r.small_m, r.small_2),
        (by_y, r.up_g, r.up_1, r.up_m, r.up_2),
        (by_z, r.down_g, r.down_1, r.down_m, r.down_2),
        (by_z, r.qk_g, r.qk_1, r.qk_m, r.qk_2),
        (by_y, r.dense_g, r.dense_1, r.dense_m, r.dense_2),
    )

    def stage_1(n):
        plane, src, land = reduced[n][:3]
        made = []
        for k in range(1, NY):
            device, a = plane.along(k)
            pair = (r.e_send.at[n, k], r.e_recv.at[n, plane.axis])
            made.append(send(plane.block(src, a), land.at[plane.axis], *pair, device))
        return made

    def stage_2(n):
        path, _, _, mid, land = reduced[n]
        made = []
        for k in range(1, NY):
            device, a = path.along_first(k)
            pair = (r.f_send.at[n, k], r.f_recv.at[n, path.first])
            made.append(send(mid.at[a], land.at[path.first], *pair, device))
        return made

    def start_1(n):
        for item in stage_1(n):
            item.start()

    def start_2(n):
        plane, src, land, mid, _ = reduced[n]
        for k in range(1, NY):
            a = plane.along(k)[1]
            local_wait(land.at[a], r.e_recv.at[n, a])

        @pl.loop(0, GROUP)
        def _(e):
            a, xx = e // NX, lax.rem(e, NX)
            own = src[plane.axis, a, xx] if plane.last == "y" else src[a, plane.axis, xx]
            total = own.astype(F32)
            for k in range(1, NY):
                total = total + land[lax.rem(plane.axis + k, NY), a, xx].astype(F32)
            mid[a, xx] = total.astype(mid.dtype)

        for item in stage_2(n):
            item.start()

    def finish(n):
        path, _, _, mid, land = reduced[n]
        for k in range(1, NY):
            a = path.along_first(k)[1]
            local_wait(land.at[a], r.f_recv.at[n, a])
        totals = []
        for xx in half_x:
            total = mid[path.first, xx].astype(F32)
            for k in range(1, NY):
                total = total + land[path.along_first(k)[1], xx].astype(F32)
            totals.append(total)
        return totals

    weight_grad(r.act_s, r.g_all, r.down_g)
    start_1(DOWN)
    weight_grad(r.n2_s, r.dpre_s, r.up_g)
    start_1(UP)

    wait_b(qkv_n)
    join(r.qk_all, r.qk_s)
    wait_b(dense_n)
    for e in range(NY * NZ * NX):
        r.dense_wide[e * PART : (e + 1) * PART, :] = r.dense_all[
            e // GROUP, e // NX % NZ, e % NX
        ].astype(F32)
    r.dense_s[...] = r.dense_wide[...].astype(BF)

    @pl.loop(0, steps)
    def _(i):
        rows = rows_at(i)
        y_rows = dot(r.n1_s[rows, :], r.qk_s[...]) + qkv_add
        cosine, sine = r.cos_ref[rows, :], r.sin_ref[rows, :]
        turned = []
        for p in range(2 * width // 128):
            u = y_rows[:, p * 128 : (p + 1) * 128]
            turned.append(u * cosine + swap_halves(u) * sine)
        d = dot_nt(r.g_all[rows, :], r.dense_s[...])

        def head(n):
            u = turned[n // 2]
            return u[:, (n % 2) * HEAD_DIM : (n % 2 + 1) * HEAD_DIM]

        for h in range(heads):
            at = 2 * width + h * HEAD_DIM
            r.q_s[h, rows, :] = head(h).astype(BF)
            r.k_s[h, rows, :] = head(heads + h).astype(BF)
            r.v_s[h, rows, :] = y_rows[:, at : at + HEAD_DIM].astype(BF)
            r.do_s[h, rows, :] = d[:, h * HEAD_DIM : (h + 1) * HEAD_DIM].astype(BF)

    scale = HEAD_DIM ** (-0.5)

    def attend(h):
        r.kt_s[...] = r.k_s[h].astype(F32).T.astype(BF)
        r.vt_s[...] = r.v_s[h].astype(F32).T.astype(BF)
        for i in reversed(range(steps)):
            keys = (i + 1) * BLOCK
            rows = slice(i * BLOCK, (i + 1) * BLOCK)
            q, do = r.q_s[h, rows, :], r.do_s[h, rows, :]
            scores = dot_nt(r.k_s[h, :keys, :], q) * scale
            hidden = iota((BLOCK, BLOCK), 0) > iota((BLOCK, BLOCK), 1)
            corner = jnp.where(hidden, -1e30, scores[i * BLOCK :, :])
            scores = jnp.concatenate([scores[: i * BLOCK, :], corner], 0) if i else corner
            expo = jnp.exp(scores - jnp.max(scores, 0, keepdims=True))
            probs = expo * (1.0 / jnp.sum(expo, 0, keepdims=True))
            low = probs.astype(BF)
            r.ctxt_s[h, :, rows] = dot(r.vt_s[:, :keys], low).astype(BF)
            dprobs = dot_nt(r.v_s[h, :keys, :], do)
            delta = jnp.sum(probs * dprobs, 0, keepdims=True)
            dscores = (probs * (dprobs - delta) * scale).astype(BF)
            r.dq_s[h, rows, :] = dot(r.kt_s[:, :keys], dscores).T.astype(BF)
            dk = dot(dscores, q)
            dv = dot(low, do)
            if i == steps - 1:
                r.dk_s[h] = dk
                r.dv_s[h] = dv
            else:
                r.dk_s[h, :keys, :] += dk
                r.dv_s[h, :keys, :] += dv

    @pl.loop(0, heads)
    def _(h):
        attend(h)

        @pl.when(h == 0)
        def _():
            start_2(DOWN)

        @pl.when(h == 1)
        def _():
            start_2(UP)

    sums_of = (r.act_s, r.dpre_s)

    def token_pair(i):
        src = sums_of[i]
        return [
            send(
                src.at[rows_of(t)], r.token_in.at[i, n], r.g_send.at[i, n], r.g_recv.at[i, n],
                (dp, sibling),
            )
            for n, t in enumerate((sibling, sib_across))
        ]

    def token_far_copy(i):
        pair = (r.h_send.at[i], r.h_recv.at[i])
        return send(r.token_mid.at[i], r.token_far.at[i], *pair, (dp, across))

    def token_cross(i):
        for item in token_pair(i):
            item.wait_recv()
        own = sums_of[i][rows_of(across), :].astype(F32)
        r.token_mid[i] = (own + r.token_in[i, 1].astype(F32)).astype(BF)
        token_far_copy(i).start()

    def token_total(i):
        token_far_copy(i).wait()
        own = sums_of[i][rows_of(sp), :].astype(F32)
        return own + r.token_in[i, 0].astype(F32) + r.token_far[i].astype(F32)

    ctxt = r.ctxt_s[...].reshape(width, length)
    for i in range(steps):
        rows = slice(i * BLOCK, (i + 1) * BLOCK)
        r.act_s[rows, :] = (r.sum_s[rows, :] + dot_tn(ctxt[:, rows], r.dense_s[...])).astype(BF)
    for item in token_pair(0):
        item.start()

    def last(i, sums):
        rows = rows_at(i)
        cosine, sine = r.cos_ref[rows, :], r.sin_ref[rows, :]
        parts = [
            ref[h, rows, :].astype(F32) for ref in (r.dq_s, r.dk_s, r.dv_s) for h in range(heads)
        ]
        blocks = []
        for p in range(2 * width // 128):
            u = jnp.concatenate(parts[2 * p : 2 * p + 2], 1).astype(BF).astype(F32)
            blocks.append((u * cosine - swap_halves(u) * sine).astype(BF))
        rest = parts[2 * heads :] + [jnp.zeros((BLOCK, QK - 3 * width), F32)]
        dqkv = jnp.concatenate(blocks + [jnp.concatenate(rest, 1).astype(BF)], 1)
        r.dqkv_s[rows, :] = dqkv
        dn1 = dot_nt(dqkv, r.qk_s[...])
        r.dpre_s[rows, :] = (r.dx_s[rows, :] + dn1 * gain_1).astype(BF)
        one, two, three = sums
        return (
            one + fold(dqkv.astype(F32)),
            two + fold(dn1 * r.xhat_s[rows, :]),
            three + fold(dn1),
        )

    qkv_bias, gain_1_grad, shift_1_grad = lax.fori_loop(
        0, steps, last, (jnp.zeros((8, QK), F32), zeros, zeros)
    )
    weight_grad(r.n1_s, r.dqkv_s, r.qk_g)
    start_1(QKV)
    for item in token_pair(1):
        item.start()
    token_cross(0)
    dense_grad = dot(ctxt, r.g_all[...])
    for e in range(NY * NZ * NX):
        r.dense_g[e // GROUP, e // NX % NZ, e % NX] = dense_grad[
            e * PART : (e + 1) * PART, :
        ].astype(BF)
    start_1(DENSE)

    g_here = r.g_all[rows_of(sp), :].astype(F32)
    values = (
        gain_1_grad, shift_1_grad, gain_2_grad, shift_2_grad, qkv_bias, fold(g_here), up_bias
    )
    result = jnp.zeros((n_rows, SMALL), F32)
    for (start, each, kind, _), item in zip(VECTORS_OUT, values):
        vector = jnp.sum(item, 0, keepdims=True)
        size = vector.shape[1]
        lane = column_of(iota((n_rows, size), 1), sp, kind)
        mine = lane // each == owner_rows(size)
        if kind == "qkv":
            mine = jnp.logical_and(mine, iota((n_rows, size), 1) < 3 * width)
        rest = jnp.where(mine, vector, 0.0)
        lane = column_of(iota((size, SMALL), 0), sp, kind)
        pick = (iota((size, SMALL), 1) == start + lax.rem(lane, each)).astype(BF)
        for _ in range(3):
            part = rest.astype(BF)
            result = result + dot(part, pick)
            rest = rest - part.astype(F32)
    for e in range(NY * NZ * NX):
        r.small_g[e // GROUP, e // NX % NZ, e % NX] = result[e * 8 : (e + 1) * 8, :]
    start_1(SMALLS)
    token_cross(1)
    start_2(QKV)

    def store_pieces(totals, out):
        for q, total in enumerate(totals):
            for t in range(N_SP):
                out[q, t] = total[t * PART : (t + 1) * PART, :]

    def back(n, q, k):
        src, land = ((r.up_p, r.up_l), (r.qk_p, r.qk_l), (r.small_t, r.small_l))[n]
        t = lax.rem(sp + k, N_SP)
        pair = (r.i_send.at[n, q, k], r.i_recv.at[n, x, sp])
        here = src.at[q] if n == 2 else src.at[q, t]
        return send(here, land.at[x, sp], *pair, (half_dp[q], t))

    def start_back(n):
        for q, k in others:
            back(n, q, k).start()

    store_pieces(finish(UP), r.up_p)
    start_back(0)
    owned = ((r.down_t, r.down_l), (r.dense_t, r.dense_l))

    def own_copies(i, run):
        src, dst = owned[i]
        recv = r.j_recv.at[i, x]
        for q, device in enumerate(to_owners):
            copy = send(src.at[q], dst.at[x], r.j_send.at[i, q], recv, device)
            to_partner(device, copy, src.at[q], dst.at[x], recv, run)

    for q, total in enumerate(finish(DOWN)):
        r.down_t[q] = total
    own_copies(0, "start")
    start_2(DENSE)
    start_2(SMALLS)
    store_pieces(finish(QKV), r.qk_p)
    start_back(1)
    for q, total in enumerate(finish(DENSE)):
        r.dense_t[q] = total
    own_copies(1, "start")
    for q, total in enumerate(finish(SMALLS)):
        r.small_t[q] = total
    start_back(2)

    x_here = r.x_all[rows_of(sp), :].astype(F32)
    r.hidden_out[...] = (x_here + token_total(0) + bias).astype(BF)
    dxhat = token_total(1)
    centered = x_here - jnp.mean(x_here, -1, keepdims=True)
    rstd = lax.rsqrt(jnp.mean(centered * centered, -1, keepdims=True) + 1e-05)
    xhat = centered * rstd
    r.hidden_grad[...] = (
        r.g_all[rows_of(sp), :].astype(F32)
        + rstd
        * (
            dxhat
            - jnp.mean(dxhat, -1, keepdims=True)
            - xhat * jnp.mean(dxhat * xhat, -1, keepdims=True)
        )
    ).astype(BF)

    r.up_l[x, sp] = r.up_p[0, sp]
    r.qk_l[x, sp] = r.qk_p[0, sp]
    r.small_l[x, sp] = r.small_t[0]

    def wait_back(n, land):
        for q, k in others:
            s = lax.rem(sp + k, N_SP)
            local_wait(land.at[half_x[q], s], r.i_recv.at[n, half_x[q], s])

    wait_back(0, r.up_l)
    for s in range(N_SP):
        r.up_out[:, s * PAGE : (s + 1) * PAGE] = r.up_l[0, s] + r.up_l[1, s]
    for i, out in enumerate((r.down_out, r.dense_out)):
        land = owned[i][1]
        for xx in range(NX):
            local_wait(land.at[xx], r.j_recv.at[i, xx])
        out[...] = land[0] + land[1]
    wait_back(1, r.qk_l)
    for s in range(N_SP):
        block = r.qk_l[0, s] + r.qk_l[1, s]
        for j in range(3):
            to = j * D + s * width
            r.qkv_out[:, to : to + width] = block[:, j * width : (j + 1) * width]
    wait_back(2, r.small_l)
    r.small_out[...] = jnp.sum(jnp.sum(r.small_l[...], 0), 0)

    for i in range(2):
        for kind in ("across", "sibling", "pass"):
            token_copies(i, kind).wait_send()

    row_copies("wait_send")
    for i in range(2):
        own_copies(i, "wait_send")
    for q, k in others:
        piece(q, k).wait_send()
        for n in range(3):
            back(n, q, k).wait_send()
    for i in range(2):
        for item in token_pair(i):
            item.wait_send()
    for n in range(len(gathered)):
        for item in stage_a(n) + stage_b(n):
            item.wait_send()
        if n != smalls:
            for part in range(2):
                passed_on(n, part).wait_send()
    for n in range(len(reduced)):
        for item in stage_1(n) + stage_2(n):
            item.wait_send()


def layer(x, g, up, qkv, small, down, dense):
    tokens = x.shape[0]
    length = tokens * N_SP
    heads = HEADS // N_SP
    width = heads * HEAD_DIM
    grid = (NY, NZ, NX)
    own = PART * N_SP
    cosine, sine = rotary_tables(length)
    dma = pltpu.SemaphoreType.DMA
    anywhere = pl.BlockSpec(memory_space=pl.ANY)
    vmem = pl.BlockSpec(memory_space=pltpu.VMEM)
    ins = ("x_ref", "g_ref", "up_ref", "qkv_ref", "small_ref", "down_ref", "dense_ref")
    ins += ("cos_ref", "sin_ref")
    outs = {
        "hidden_out": ((tokens, D), BF),
        "hidden_grad": ((tokens, D), BF),
        "up_out": ((PART, FF), F32),
        "qkv_out": ((PART, 3 * D), F32),
        "down_out": ((own, D), F32),
        "dense_out": ((PART, D), F32),
        "small_out": ((8, SMALL), F32),
    }
    chunk = {
        "up": ((own, PAGE), BF),
        "down": ((own, D), BF),
        "qk": ((own, QK), BF),
        "dense": ((PART, D), BF),
        "small": ((8, SMALL), F32),
    }
    scratch = {}
    for name, (shape, kind) in chunk.items():
        if name in ("up", "down"):
            scratch[name + "_a"] = (grid + (own, PAGE // 2), kind)
            scratch[name + "_b"] = (grid + (own, PAGE // 2), kind)
        else:
            scratch[name + "_all"] = (grid + shape, kind)
        scratch[name + "_g"] = (grid + shape, kind)
        scratch[name + "_1"] = (grid + shape, kind)
        scratch[name + "_m"] = ((GROUP // NX, NX) + shape, kind)
        scratch[name + "_2"] = ((GROUP // NX, NX) + shape, kind)
    per_head = (heads, length, HEAD_DIM)
    scratch.update(
        x_all=((length, D), BF),
        g_all=((length, D), BF),
        pieces=((N_SP, PART, PAGE + QK + SMALL), BF),
        landed=((NX, N_SP, PART, PAGE + QK + SMALL), BF),
        tight=((own, PAGE + QK + SMALL), F32),
        up_s=((D, PAGE), BF),
        down_s=((PAGE, D), BF),
        qk_s=((D, QK), BF),
        down_in=((NX, own, D), BF),
        dense_wide=((width, D), F32),
        dense_s=((width, D), BF),
        vec_s=((8, PAGE), F32),
        xhat_s=((length, D), F32),
        n1_s=((length, D), BF),
        n2_s=((length, D), BF),
        act_s=((length, PAGE), BF),
        dpre_s=((length, PAGE), BF),
        sum_s=((length, D), F32),
        dx_s=((length, D), F32),
        dqkv_s=((length, QK), BF),
        q_s=(per_head, BF),
        k_s=(per_head, BF),
        v_s=(per_head, BF),
        do_s=(per_head, BF),
        dq_s=(per_head, BF),
        dk_s=(per_head, F32),
        dv_s=(per_head, F32),
        kt_s=((HEAD_DIM, length), BF),
        vt_s=((HEAD_DIM, length), BF),
        ctxt_s=((heads, HEAD_DIM, length), BF),
        token_in=((2, 2, tokens, D), BF),
        token_mid=((2, tokens, D), BF),
        token_far=((2, tokens, D), BF),
        up_p=((NX, N_SP, PART, PAGE), F32),
        up_l=((NX, N_SP, PART, PAGE), F32),
        qk_p=((NX, N_SP, PART, QK), F32),
        qk_l=((NX, N_SP, PART, QK), F32),
        down_t=((NX, own, D), F32),
        down_l=((NX, own, D), F32),
        dense_t=((NX, PART, D), F32),
        dense_l=((NX, PART, D), F32),
        small_t=((NX, 8, SMALL), F32),
        small_l=((NX, N_SP, 8, SMALL), F32),
    )
    semaphores = {
        "r": (2, NX), "p": (NX, N_SP), "t": (2, N_SP), "a": (7, NY), "b": (7, NY), "q": (7, 2), "e": (5, NY),
        "f": (5, NY), "g": (2, 2), "h": (2,), "j": (2, NX),
    }
    names = list(ins) + list(outs) + list(scratch)
    shapes = [pltpu.VMEM(shape, kind) for shape, kind in scratch.values()]
    for name, shape in semaphores.items():
        names += [name + "_send", name + "_recv"]
        shapes += [dma(shape), dma(shape)]
    names += ["i_send", "i_recv"]
    shapes += [dma((3, NX, N_SP)), dma((3, NX, N_SP))]
    return pl.pallas_call(
        functools.partial(layer_kernel, names),
        out_shape=tuple(jax.ShapeDtypeStruct(*item) for item in outs.values()),
        in_specs=[anywhere, anywhere, vmem, vmem, vmem, anywhere, anywhere, vmem, vmem],
        out_specs=(vmem,) * len(outs),
        scratch_shapes=shapes,
        compiler_params=pltpu.CompilerParams(
            collective_id=0, has_side_effects=True, vmem_limit_bytes=61 * 1024 * 1024
        ),
        cost_estimate=pl.CostEstimate(
            flops=14_000_000_000, bytes_accessed=16_000_000, transcendentals=6_000_000
        ),
        name="layer",
    )(x, g, up, qkv, small, down, dense, cosine, sine)


def outputs_kernel(*refs):
    n = 6
    small_ref, outs = refs[n], refs[n + 1 :]
    for i in range(n):
        outs[i][...] = refs[i][...]
    mine = small_ref[pl.ds(lax.axis_index("sp"), 1), :]
    for (start, each, _, _), out in zip(VECTORS_OUT + VECTORS_OUT[5:6], outs[n:]):
        out[...] = mine[:, start : start + each]


def write_outputs(*arrays):
    vmem = pl.BlockSpec(memory_space=pltpu.VMEM)
    large = [jax.ShapeDtypeStruct(item.shape, item.dtype) for item in arrays[:-1]]
    small = [
        jax.ShapeDtypeStruct((1, each), F32) for _, each, _, _ in VECTORS_OUT + VECTORS_OUT[5:6]
    ]
    return pl.pallas_call(
        outputs_kernel,
        out_shape=tuple(large + small),
        in_specs=[vmem] * len(arrays),
        out_specs=(vmem,) * (len(large) + len(small)),
        name="outputs",
    )(*arrays)


def local(
    hidden_in,
    cotangent,
    attn_gain,
    attn_shift,
    mlp_gain,
    mlp_shift,
    qkv_weight,
    qkv_bias,
    dense_weight,
    dense_bias,
    up_weight,
    up_bias,
    down_weight,
    down_bias,
):
    small = (
        attn_gain,
        attn_shift,
        mlp_gain,
        mlp_shift,
        qkv_bias,
        dense_bias,
        up_bias,
        down_bias,
    )
    packed = jnp.zeros((SMALL,), F32)
    at = 0
    for item in small:
        size = item.shape[0]
        packed = packed + jnp.pad(item.astype(F32), (at, SMALL - at - size))
        at += size
    results = layer(
        hidden_in,
        cotangent,
        up_weight,
        qkv_weight,
        packed.reshape(1, SMALL),
        down_weight,
        dense_weight,
    )
    results = write_outputs(*results)
    hidden_out, hidden_grad, up_own, qkv_own, down_own, dense_own = results[:6]
    parts = [item.reshape(-1) for item in results[6:]]
    return (
        hidden_out,
        hidden_grad,
        parts[0],
        parts[1],
        parts[2],
        parts[3],
        qkv_own,
        parts[4],
        dense_own,
        parts[5],
        up_own,
        parts[6],
        down_own,
        parts[7],
    )


def solution(mesh):
    matrix = P(BOTH, None)
    vector = P(BOTH)
    split = (matrix, matrix) + (vector,) * 4 + (matrix, vector) * 4
    return jax.shard_map(local, mesh=mesh, in_specs=split, out_specs=split, check_vma=False)
```

```python
import functools
import types

import jax
import jax.numpy as jnp
import numpy as np
from jax import lax
from jax.experimental import pallas as pl
from jax.experimental.pallas import tpu as pltpu
from jax.sharding import PartitionSpec as P

D = 768
HEADS = 12
HEAD_DIM = 64
ROT = 16
FF = 3072
BF = jnp.bfloat16
F32 = jnp.float32
BOTH = ("dp", "sp")


def dot(left, right):
    return jnp.dot(left, right, preferred_element_type=F32)


MESH = pl.DeviceIdType.MESH
SMALL = 128
PAGE = 768
NY, NZ, NX = 4, 4, 2
GROUP = NZ * NX
N_SP = 4
PART = 6


def place():
    dp, sp = lax.axis_index("dp"), lax.axis_index("sp")
    return dp, sp, dp // GROUP, lax.rem(dp // NX, NZ), lax.rem(dp, NX)


def send(src, dst, send_sem, recv_sem, device):
    return pltpu.make_async_remote_copy(
        src_ref=src,
        dst_ref=dst,
        send_sem=send_sem,
        recv_sem=recv_sem,
        device_id=device,
        device_id_type=MESH,
    )


def index_of(y, z, x):
    return (y * NZ + z) * NX + x


def slot_device(dp, sp):
    line = dp * N_SP + sp
    return lax.rem(line, NY * GROUP), line // (NY * GROUP)


def owner_device(dp, sp):
    line = sp * NY * GROUP + dp
    return line // N_SP, lax.rem(line, N_SP)


def differs(device, dp, sp):
    return jnp.logical_or(device[0] != dp, device[1] != sp)


def other_half(dp):
    return dp + 1 - 2 * lax.rem(dp, NX)


class Path:
    def __init__(self, last):
        self.last = last
        dp, self.sp, self.y, self.z, self.x = place()
        self.first, self.axis = (self.z, self.y) if last == "y" else (self.y, self.z)

    def along_first(self, k):
        a = lax.rem(self.first + k, NY)
        y, z = (self.y, a) if self.last == "y" else (a, self.z)
        return (index_of(y, z, self.x), self.sp), a

    def along(self, k):
        a = lax.rem(self.axis + k, NY)
        y, z = (a, self.z) if self.last == "y" else (self.y, a)
        return (index_of(y, z, self.x), self.sp), a

    def block(self, ref, a):
        return ref.at[a] if self.last == "y" else ref.at[:, a]

    def pair(self, ref, a):
        return ref.at[self.y, a] if self.last == "y" else ref.at[a, self.z]


def greet(partners):
    dp, sp, y, z, x = place()
    barrier = pltpu.get_barrier_semaphore()

    def signal(device):
        pl.semaphore_signal(barrier, inc=1, device_id=device, device_id_type=MESH)

    for k in range(N_SP):
        if k:
            signal((dp, lax.rem(sp + k, N_SP)))
        signal((other_half(dp), lax.rem(sp + k, N_SP)))
    by_y, by_z = Path("y"), Path("z")
    for k in range(1, NY):
        signal(by_y.along(k)[0])
        signal(by_z.along(k)[0])
    for partner in partners:

        @pl.when(differs(partner, dp, sp))
        def _():
            signal(partner)


def await_greetings(partners):
    dp, sp, y, z, x = place()
    count = 2 * N_SP - 1 + 2 * (NY - 1)
    for partner in partners:
        count = count + jnp.where(differs(partner, dp, sp), 1, 0)
    pl.semaphore_wait(pltpu.get_barrier_semaphore(), count)


BLOCK = 256


def dot_nt(left, right):
    return lax.dot_general(left, right, (((1,), (1,)), ((), ())), preferred_element_type=F32)


def dot_tn(left, right):
    return lax.dot_general(left, right, (((0,), (0,)), ((), ())), preferred_element_type=F32)


def iota(shape, axis):
    return lax.broadcasted_iota(jnp.int32, shape, axis)


def rotary_tables(length):
    half = ROT // 2
    frequency = np.float32(10000.0) ** (np.float32(-2.0) * np.arange(half, dtype=np.float32) / ROT)
    angles = np.arange(length, dtype=np.float32)[:, None] * frequency[None, :].astype(np.float32)
    cosine = np.ones((length, HEAD_DIM), np.float32)
    sine = np.zeros((length, HEAD_DIM), np.float32)
    cosine[:, :half] = cosine[:, half:ROT] = np.cos(angles)
    sine[:, :half] = -np.sin(angles)
    sine[:, half:ROT] = np.sin(angles)
    return jnp.asarray(np.tile(cosine, (1, 2))), jnp.asarray(np.tile(sine, (1, 2)))


def swap_halves(u):
    low = lax.rem(iota(u.shape, 1), 16) < 8
    return jnp.where(low, pltpu.roll(u, 120, 1), pltpu.roll(u, 8, 1))


def column_of(c, sp, kind):
    if kind == "qkv":
        width = D // N_SP
        return (c // width) * D + sp * width + lax.rem(c, width)
    return c + sp * (FF // N_SP) if kind == "up" else c


VECTORS_IN = (
    (0, 6, "", D), (6, 6, "", D), (12, 6, "", D), (18, 6, "", D),
    (24, 18, "qkv", PAGE), (42, 6, "", D), (48, 24, "up", PAGE), (72, 6, "", D),
)
VECTORS_OUT = (
    (0, 6, "", D), (6, 6, "", D), (12, 6, "", D), (18, 6, "", D),
    (24, 18, "qkv", PAGE), (42, 6, "", D), (48, 24, "up", PAGE),
)


QK = 640


def layer_kernel(names, *refs):
    r = types.SimpleNamespace(**dict(zip(names, refs)))
    dp, sp, y, z, x = place()
    half_dp = (dp, other_half(dp))
    half_x = (x, 1 - x)
    slot, column = slot_device(dp, sp)
    to_slots = ((slot, column), (other_half(slot), column))
    to_owners = tuple(owner_device(d, sp) for d in half_dp)
    slot_x = lax.rem(slot, NX)
    sibling = sp + 1 - 2 * lax.rem(sp, 2)
    across = lax.rem(sp + 2, N_SP)
    sib_across = lax.rem(sibling + 2, N_SP)
    others = [(q, k) for q in range(NX) for k in range(N_SP) if q or k]
    by_y, by_z = Path("y"), Path("z")
    length = r.x_all.shape[0]
    tokens = length // N_SP
    heads = HEADS // N_SP
    width = heads * HEAD_DIM
    n_own = NY * NZ * NX * N_SP
    steps = length // BLOCK
    slot_at = (slot // GROUP, lax.rem(slot // NX, NZ), slot_x)

    def to_partner(device, copy, src, dst, recv, run):
        @pl.when(differs(device, dp, sp))
        def _():
            getattr(copy, run)()

        if run == "start":

            @pl.when(jnp.logical_not(differs(device, dp, sp)))
            def _():
                pltpu.make_async_copy(src, dst, recv).start()

    def local_wait(ref, sem):
        pltpu.make_async_copy(ref, ref, sem).wait()

    def rows_of(s):
        return pl.ds(pl.multiple_of(s * tokens, tokens), tokens)

    def rows_at(i):
        return pl.ds(pl.multiple_of(i * BLOCK, BLOCK), BLOCK)

    greet(to_slots + to_owners)

    wide = r.qkv_ref[...].astype(F32)
    fill = jnp.zeros((PART, QK - 3 * width), F32)
    small = jnp.concatenate([r.small_ref[...], jnp.zeros((PART - 1, SMALL), F32)], 0)
    for t in range(N_SP):
        parts = [r.up_ref[:, t * PAGE : (t + 1) * PAGE].astype(F32)]
        parts += [wide[:, j * D + t * width : j * D + (t + 1) * width] for j in range(3)]
        r.pieces[t] = jnp.concatenate(parts + [fill, small], 1).astype(BF)

    await_greetings(to_slots + to_owners)

    def piece(q, k):
        t = lax.rem(sp + k, N_SP)
        pair = (r.p_send.at[q, k], r.p_recv.at[x, sp])
        return send(r.pieces.at[t], r.landed.at[x, sp], *pair, (half_dp[q], t))

    for q, k in others:
        piece(q, k).start()
    pltpu.make_async_copy(r.pieces.at[sp], r.landed.at[x, sp], r.p_recv.at[x, sp]).start()

    def row_copies(run):
        for i, (src, dst) in enumerate(
            ((r.down_ref, r.down_in.at[slot_x]), (r.dense_ref, r.dense_all.at[slot_at]))
        ):
            recv = r.r_recv.at[i, slot_x]
            for q, device in enumerate(to_slots):
                copy = send(src, dst, r.r_send.at[i, q], recv, device)
                to_partner(device, copy, src, dst, recv, run)

    row_copies("start")

    token_arrays = ((r.x_ref, r.x_all), (r.g_ref, r.g_all))

    def token_copies(i, kind):
        src, dst = token_arrays[i]
        if kind == "pass":
            there = dst.at[rows_of(across)]
            pair = (r.t_send.at[i, 2], r.t_recv.at[i, across])
            return send(there, there, *pair, (dp, sibling))
        to, n = (across, 0) if kind == "across" else (sibling, 1)
        pair = (r.t_send.at[i, n], r.t_recv.at[i, sp])
        return send(src, dst.at[rows_of(sp)], *pair, (dp, to))

    def token_start(i):
        src, dst = token_arrays[i]
        token_copies(i, "across").start()
        token_copies(i, "sibling").start()
        pltpu.make_async_copy(src, dst.at[rows_of(sp)], r.t_recv.at[i, sp]).start()

    def token_wait(i, s):
        src, dst = token_arrays[i]
        pltpu.make_async_copy(src, dst.at[rows_of(s)], r.t_recv.at[i, s]).wait()

    def token_pass(i):
        token_wait(i, across)
        token_copies(i, "pass").start()

    def token_rest(i):
        for s in (sp, sibling, sib_across):
            token_wait(i, s)

    token_start(0)

    smalls, up_0, up_1, down_0, down_1, qkv_n, dense_n = range(7)
    gathered = (
        (by_y, r.small_all), (by_y, r.up_a), (by_z, r.up_b), (by_y, r.down_a), (by_z, r.down_b),
        (by_z, r.qk_all), (by_y, r.dense_all),
    )
    cut = PAGE // 2

    def stage_a(n):
        path, out = gathered[n]
        mine = path.pair(out, path.first)
        return [
            send(mine, mine, r.a_send.at[n, k], r.a_recv.at[n, path.first], path.along_first(k)[0])
            for k in range(1, NY)
        ]

    def stage_b(n):
        path, out = gathered[n]
        there = path.block(out, path.axis)
        return [
            send(there, there, r.b_send.at[n, k], r.b_recv.at[n, path.axis], path.along(k)[0])
            for k in ((1, 2, 3) if n == smalls else (1, 3))
        ]

    def half_block(n, a, part):
        path, out = gathered[n]
        some = pl.ds(part * (NZ // 2), NZ // 2)
        return out.at[a, some] if path.last == "y" else out.at[some, a]

    def passed_on(n, part):
        path = gathered[n][0]
        there = half_block(n, path.along((3, 1)[part])[1], part)
        pair = (r.q_send.at[n, part], r.q_recv.at[n, part])
        return send(there, there, *pair, path.along((1, 3)[part])[0])

    def start_on(n):
        path, out = gathered[n]
        for part in range(2):
            a = path.along((3, 1)[part])[1]
            local_wait(path.block(out, a), r.b_recv.at[n, a])
            passed_on(n, part).start()

    def start_a(n):
        for item in stage_a(n):
            item.start()

    def start_b(n):
        plane, out = gathered[n]
        for k in range(1, NY):
            a = plane.along_first(k)[1]
            local_wait(plane.pair(out, a), r.a_recv.at[n, a])
        for item in stage_b(n):
            item.start()

    def wait_b(n):
        path, out = gathered[n]
        if n == smalls:
            for k in range(1, NY):
                a = path.along(k)[1]
                local_wait(path.block(out, a), r.b_recv.at[n, a])
        else:
            for part in range(2):
                local_wait(half_block(n, path.along(2)[1], part), r.q_recv.at[n, part])

    for xx in range(NX):
        for s in range(N_SP):
            local_wait(r.landed.at[xx, s], r.p_recv.at[xx, s])
    for xx in range(NX):
        r.small_all[y, z, xx] = jnp.zeros((8, SMALL), F32)
        for s in range(N_SP):
            own = r.landed[xx, s].astype(F32)
            r.tight[s * PART : (s + 1) * PART, :] = own
            r.small_all[y, z, xx, s : s + 1, :] = own[0:1, PAGE + QK :]
        r.up_a[y, z, xx] = r.tight[:, :cut].astype(BF)
        r.up_b[y, z, xx] = r.tight[:, cut:PAGE].astype(BF)
        r.qk_all[y, z, xx] = r.tight[:, PAGE : PAGE + QK].astype(BF)
    start_a(smalls)
    start_a(up_0)
    start_a(up_1)
    for xx in range(NX):
        local_wait(r.down_in.at[xx], r.r_recv.at[0, xx])
        r.down_a[y, z, xx] = r.down_in[xx, :, :cut]
        r.down_b[y, z, xx] = r.down_in[xx, :, cut:]
    start_a(down_0)
    start_a(down_1)
    token_start(1)
    start_b(smalls)
    start_b(up_0)
    start_b(up_1)
    token_pass(0)
    start_b(down_0)
    start_b(down_1)
    start_on(up_0)
    start_on(up_1)
    for xx in range(NX):
        local_wait(r.dense_all.at[y, z, xx], r.r_recv.at[1, xx])
    start_a(qkv_n)
    start_a(dense_n)

    wait_b(smalls)
    packed = r.small_all[...].reshape(2 * n_own, SMALL).astype(BF)
    n_rows = 2 * n_own

    def owner_rows(size):
        row = iota((n_rows, size), 0)
        inside = lax.rem(row, 8)
        return jnp.where(inside < N_SP, row // 8 * N_SP + inside, -1)

    for n, (start, each, kind, size) in enumerate(VECTORS_IN):
        lane = column_of(iota((SMALL, size), 1), sp, kind)
        spread = (iota((SMALL, size), 0) == start + lax.rem(lane, each)).astype(BF)
        lane = column_of(iota((n_rows, size), 1), sp, kind)
        values = jnp.where(lane // each == owner_rows(size), dot(packed, spread), 0.0)
        r.vec_s[n : n + 1, :] = jnp.sum(values, 0, keepdims=True)
    gain_1, shift_1, gain_2, shift_2 = (r.vec_s[n : n + 1, :] for n in range(4))
    qkv_add = r.vec_s[4:5, :QK]
    up_add = r.vec_s[6:7, :]
    bias = r.vec_s[5:6, :] + r.vec_s[7:8, :]

    def fold(values):
        return jnp.sum(values.reshape(-1, 8, values.shape[-1]), 0)

    token_rest(0)

    @pl.loop(0, steps)
    def _(i):
        rows = rows_at(i)
        values = r.x_all[rows, :].astype(F32)
        centered = values - jnp.mean(values, -1, keepdims=True)
        xhat = centered * lax.rsqrt(jnp.mean(centered * centered, -1, keepdims=True) + 1e-05)
        r.xhat_s[rows, :] = xhat
        r.n1_s[rows, :] = (xhat * gain_1 + shift_1).astype(BF)
        r.n2_s[rows, :] = (xhat * gain_2 + shift_2).astype(BF)

    def join(src, dst, lane=0):
        @pl.loop(0, NY * NZ)
        def _(i):
            a, b = i // NZ, lax.rem(i, NZ)
            pair = [src[a, b, e].astype(F32) for e in range(NX)]
            own, wide_here = pair[0].shape[0] * NX, pair[0].shape[1]
            here = (pl.ds(pl.multiple_of(i * own, own), own), pl.ds(lane, wide_here))
            dst[here] = jnp.concatenate(pair, 0).astype(BF)

    start_on(down_0)
    start_on(down_1)
    token_pass(1)
    wait_b(up_0)
    join(r.up_a, r.up_s)
    wait_b(up_1)
    join(r.up_b, r.up_s, cut)

    zeros = jnp.zeros((8, D), F32)

    @pl.loop(0, steps)
    def _(i):
        rows = rows_at(i)
        pre = dot(r.n2_s[rows, :], r.up_s[...]) + up_add
        cdf = 0.5 * (1.0 + lax.erf(pre * 0.7071067811865476))
        r.act_s[rows, :] = (pre * cdf).astype(BF)
        pdf = jnp.exp(-0.5 * pre * pre) * 0.3989422804014327
        r.sum_s[rows, :] = cdf + pre * pdf

    start_b(qkv_n)
    start_b(dense_n)
    wait_b(down_0)
    join(r.down_a, r.down_s)
    wait_b(down_1)
    join(r.down_b, r.down_s, cut)
    token_rest(1)

    def first(i, sums):
        rows = rows_at(i)
        dact = dot_nt(r.g_all[rows, :], r.down_s[...])
        dpre = (dact * r.sum_s[rows, :]).astype(BF)
        r.dpre_s[rows, :] = dpre
        r.sum_s[rows, :] = dot(r.act_s[rows, :], r.down_s[...])
        dn2 = dot_nt(dpre, r.up_s[...])
        r.dx_s[rows, :] = dn2 * gain_2
        one, two, three = sums
        return (
            one + fold(dpre.astype(F32)),
            two + fold(dn2 * r.xhat_s[rows, :]),
            three + fold(dn2),
        )

    up_bias, gain_2_grad, shift_2_grad = lax.fori_loop(0, steps, first, (zeros,) * 3)
    start_on(qkv_n)
    start_on(dense_n)

    half = D // 2
    in_half = half // (PART * N_SP)

    def weight_grad(left, right, out):
        @pl.loop(0, 2)
        def _(i):
            lanes = pl.ds(pl.multiple_of(i * half, half), half)
            value = dot_tn(left[:, lanes], right[...])
            own = PART * N_SP
            for c in range(in_half):
                at = (i * (NY // 2) + c // GROUP, c // NX % NZ, c % NX)
                out[at[0], at[1], at[2]] = value[c * own : (c + 1) * own, :].astype(BF)

    SMALLS, UP, DOWN, QKV, DENSE = range(5)
    reduced = (
        (by_y, r.small_g, r.small_1, r.small_m, r.small_2),
        (by_y, r.up_g, r.up_1, r.up_m, r.up_2),
        (by_z, r.down_g, r.down_1, r.down_m, r.down_2),
        (by_z, r.qk_g, r.qk_1, r.qk_m, r.qk_2),
        (by_y, r.dense_g, r.dense_1, r.dense_m, r.dense_2),
    )

    def stage_1(n):
        plane, src, land = reduced[n][:3]
        made = []
        for k in range(1, NY):
            device, a = plane.along(k)
            pair = (r.e_send.at[n, k], r.e_recv.at[n, plane.axis])
            made.append(send(plane.block(src, a), land.at[plane.axis], *pair, device))
        return made

    def stage_2(n):
        path, _, _, mid, land = reduced[n]
        made = []
        for k in range(1, NY):
            device, a = path.along_first(k)
            pair = (r.f_send.at[n, k], r.f_recv.at[n, path.first])
            made.append(send(mid.at[a], land.at[path.first], *pair, device))
        return made

    def start_1(n):
        for item in stage_1(n):
            item.start()

    def start_2(n):
        plane, src, land, mid, _ = reduced[n]
        for k in range(1, NY):
            a = plane.along(k)[1]
            local_wait(land.at[a], r.e_recv.at[n, a])

        @pl.loop(0, GROUP)
        def _(e):
            a, xx = e // NX, lax.rem(e, NX)
            own = src[plane.axis, a, xx] if plane.last == "y" else src[a, plane.axis, xx]
            total = own.astype(F32)
            for k in range(1, NY):
                total = total + land[lax.rem(plane.axis + k, NY), a, xx].astype(F32)
            mid[a, xx] = total.astype(mid.dtype)

        for item in stage_2(n):
            item.start()

    def finish(n):
        path, _, _, mid, land = reduced[n]
        for k in range(1, NY):
            a = path.along_first(k)[1]
            local_wait(land.at[a], r.f_recv.at[n, a])
        totals = []
        for xx in half_x:
            total = mid[path.first, xx].astype(F32)
            for k in range(1, NY):
                total = total + land[path.along_first(k)[1], xx].astype(F32)
            totals.append(total)
        return totals

    weight_grad(r.act_s, r.g_all, r.down_g)
    start_1(DOWN)
    weight_grad(r.n2_s, r.dpre_s, r.up_g)
    start_1(UP)

    scale = HEAD_DIM ** (-0.5)
    wait_b(qkv_n)
    join(r.qk_all, r.qk_s)
    wait_b(dense_n)
    for e in range(NY * NZ * NX):
        r.dense_wide[e * PART : (e + 1) * PART, :] = r.dense_all[
            e // GROUP, e // NX % NZ, e % NX
        ].astype(F32)
    r.dense_s[...] = r.dense_wide[...].astype(BF)

    @pl.loop(0, steps)
    def _(i):
        rows = rows_at(i)
        y_rows = dot(r.n1_s[rows, :], r.qk_s[...]) + qkv_add
        cosine, sine = r.cos_ref[rows, :], r.sin_ref[rows, :]
        turned = []
        for p in range(2 * width // 128):
            u = y_rows[:, p * 128 : (p + 1) * 128]
            turned.append(u * cosine + swap_halves(u) * sine)
        d = dot_nt(r.g_all[rows, :], r.dense_s[...])

        def head(n):
            u = turned[n // 2]
            return u[:, (n % 2) * HEAD_DIM : (n % 2 + 1) * HEAD_DIM]

        for h in range(heads):
            at = 2 * width + h * HEAD_DIM
            r.q_s[h, rows, :] = (head(h).astype(BF).astype(F32) * scale).astype(BF)
            r.k_s[h, rows, :] = head(heads + h).astype(BF)
            r.v_s[h, rows, :] = y_rows[:, at : at + HEAD_DIM].astype(BF)
            r.do_s[h, rows, :] = d[:, h * HEAD_DIM : (h + 1) * HEAD_DIM].astype(BF)

    def attend(h):
        r.kt_s[...] = (r.k_s[h].astype(F32).T * scale).astype(BF)
        r.vt_s[...] = r.v_s[h].astype(F32).T.astype(BF)
        for i in reversed(range(steps)):
            keys = (i + 1) * BLOCK
            rows = slice(i * BLOCK, (i + 1) * BLOCK)
            q, do = r.q_s[h, rows, :], r.do_s[h, rows, :]
            scores = dot_nt(r.k_s[h, :keys, :], q)
            hidden = iota((BLOCK, BLOCK), 0) > iota((BLOCK, BLOCK), 1)
            corner = jnp.where(hidden, -1e30, scores[i * BLOCK :, :])
            scores = jnp.concatenate([scores[: i * BLOCK, :], corner], 0) if i else corner
            expo = jnp.exp(scores - jnp.max(scores, 0, keepdims=True))
            probs = expo * (1.0 / jnp.sum(expo, 0, keepdims=True))
            low = probs.astype(BF)
            r.ctxt_s[h, :, rows] = dot(r.vt_s[:, :keys], low).astype(BF)
            dprobs = dot_nt(r.v_s[h, :keys, :], do)
            delta = jnp.sum(probs * dprobs, 0, keepdims=True)
            dscores = (probs * (dprobs - delta)).astype(BF)
            r.dq_s[h, rows, :] = dot(r.kt_s[:, :keys], dscores).T.astype(BF)
            dk = dot(dscores, q)
            dv = dot(low, do)
            if i == steps - 1:
                r.dk_s[h] = dk
                r.dv_s[h] = dv
            else:
                r.dk_s[h, :keys, :] += dk
                r.dv_s[h, :keys, :] += dv

    @pl.loop(0, heads)
    def _(h):
        attend(h)

        @pl.when(h == 0)
        def _():
            start_2(DOWN)

        @pl.when(h == 1)
        def _():
            start_2(UP)

    sums_of = (r.act_s, r.dpre_s)

    def token_pair(i):
        src = sums_of[i]
        return [
            send(
                src.at[rows_of(t)], r.token_in.at[i, n], r.g_send.at[i, n], r.g_recv.at[i, n],
                (dp, sibling),
            )
            for n, t in enumerate((sibling, sib_across))
        ]

    def token_far_copy(i):
        pair = (r.h_send.at[i], r.h_recv.at[i])
        return send(r.token_mid.at[i], r.token_far.at[i], *pair, (dp, across))

    def token_cross(i):
        for item in token_pair(i):
            item.wait_recv()
        own = sums_of[i][rows_of(across), :].astype(F32)
        r.token_mid[i] = (own + r.token_in[i, 1].astype(F32)).astype(BF)
        token_far_copy(i).start()

    def token_total(i):
        token_far_copy(i).wait()
        own = sums_of[i][rows_of(sp), :].astype(F32)
        return own + r.token_in[i, 0].astype(F32) + r.token_far[i].astype(F32)

    ctxt = r.ctxt_s[...].reshape(width, length)
    for i in range(steps):
        rows = slice(i * BLOCK, (i + 1) * BLOCK)
        r.act_s[rows, :] = (r.sum_s[rows, :] + dot_tn(ctxt[:, rows], r.dense_s[...])).astype(BF)
    for item in token_pair(0):
        item.start()

    def last(i, sums):
        rows = rows_at(i)
        cosine, sine = r.cos_ref[rows, :], r.sin_ref[rows, :]
        parts = [
            ref[h, rows, :].astype(F32) for ref in (r.dq_s, r.dk_s, r.dv_s) for h in range(heads)
        ]
        blocks = []
        for p in range(2 * width // 128):
            u = jnp.concatenate(parts[2 * p : 2 * p + 2], 1).astype(BF).astype(F32)
            blocks.append((u * cosine - swap_halves(u) * sine).astype(BF))
        rest = parts[2 * heads :] + [jnp.zeros((BLOCK, QK - 3 * width), F32)]
        dqkv = jnp.concatenate(blocks + [jnp.concatenate(rest, 1).astype(BF)], 1)
        r.dqkv_s[rows, :] = dqkv
        dn1 = dot_nt(dqkv, r.qk_s[...])
        r.dpre_s[rows, :] = (r.dx_s[rows, :] + dn1 * gain_1).astype(BF)
        one, two, three = sums
        return (
            one + fold(dqkv.astype(F32)),
            two + fold(dn1 * r.xhat_s[rows, :]),
            three + fold(dn1),
        )

    qkv_bias, gain_1_grad, shift_1_grad = lax.fori_loop(
        0, steps, last, (jnp.zeros((8, QK), F32), zeros, zeros)
    )
    for item in token_pair(1):
        item.start()
    weight_grad(r.n1_s, r.dqkv_s, r.qk_g)
    start_1(QKV)
    token_cross(0)
    dense_grad = dot(ctxt, r.g_all[...])
    for e in range(NY * NZ * NX):
        r.dense_g[e // GROUP, e // NX % NZ, e % NX] = dense_grad[
            e * PART : (e + 1) * PART, :
        ].astype(BF)
    start_1(DENSE)

    token_cross(1)

    g_here = r.g_all[rows_of(sp), :].astype(F32)
    values = (
        gain_1_grad, shift_1_grad, gain_2_grad, shift_2_grad, qkv_bias, fold(g_here), up_bias
    )
    result = jnp.zeros((n_rows, SMALL), F32)
    for (start, each, kind, _), item in zip(VECTORS_OUT, values):
        vector = jnp.sum(item, 0, keepdims=True)
        size = vector.shape[1]
        lane = column_of(iota((n_rows, size), 1), sp, kind)
        mine = lane // each == owner_rows(size)
        if kind == "qkv":
            mine = jnp.logical_and(mine, iota((n_rows, size), 1) < 3 * width)
        rest = jnp.where(mine, vector, 0.0)
        lane = column_of(iota((size, SMALL), 0), sp, kind)
        pick = (iota((size, SMALL), 1) == start + lax.rem(lane, each)).astype(BF)
        for _ in range(3):
            part = rest.astype(BF)
            result = result + dot(part, pick)
            rest = rest - part.astype(F32)
    for e in range(NY * NZ * NX):
        r.small_g[e // GROUP, e // NX % NZ, e % NX] = result[e * 8 : (e + 1) * 8, :]
    start_1(SMALLS)
    start_2(QKV)

    def store_pieces(totals, out):
        for q, total in enumerate(totals):
            for t in range(N_SP):
                out[q, t] = total[t * PART : (t + 1) * PART, :]

    def back(n, q, k):
        src, land = ((r.up_p, r.up_l), (r.qk_p, r.qk_l), (r.small_t, r.small_l))[n]
        t = lax.rem(sp + k, N_SP)
        pair = (r.i_send.at[n, q, k], r.i_recv.at[n, x, sp])
        here = src.at[q] if n == 2 else src.at[q, t]
        return send(here, land.at[x, sp], *pair, (half_dp[q], t))

    def start_back(n):
        for q, k in others:
            back(n, q, k).start()

    store_pieces(finish(UP), r.up_p)
    start_back(0)
    owned = ((r.down_t, r.down_l), (r.dense_t, r.dense_l))

    def own_copies(i, run):
        src, dst = owned[i]
        recv = r.j_recv.at[i, x]
        for q, device in enumerate(to_owners):
            copy = send(src.at[q], dst.at[x], r.j_send.at[i, q], recv, device)
            to_partner(device, copy, src.at[q], dst.at[x], recv, run)

    for q, total in enumerate(finish(DOWN)):
        r.down_t[q] = total
    own_copies(0, "start")
    start_2(DENSE)
    start_2(SMALLS)
    store_pieces(finish(QKV), r.qk_p)
    start_back(1)
    for q, total in enumerate(finish(DENSE)):
        r.dense_t[q] = total
    own_copies(1, "start")
    for q, total in enumerate(finish(SMALLS)):
        r.small_t[q] = total
    start_back(2)

    x_here = r.x_all[rows_of(sp), :].astype(F32)
    r.hidden_out[...] = (x_here + token_total(0) + bias).astype(BF)
    dxhat = token_total(1)
    centered = x_here - jnp.mean(x_here, -1, keepdims=True)
    rstd = lax.rsqrt(jnp.mean(centered * centered, -1, keepdims=True) + 1e-05)
    xhat = centered * rstd
    r.hidden_grad[...] = (
        r.g_all[rows_of(sp), :].astype(F32)
        + rstd
        * (
            dxhat
            - jnp.mean(dxhat, -1, keepdims=True)
            - xhat * jnp.mean(dxhat * xhat, -1, keepdims=True)
        )
    ).astype(BF)

    r.up_l[x, sp] = r.up_p[0, sp]
    r.qk_l[x, sp] = r.qk_p[0, sp]
    r.small_l[x, sp] = r.small_t[0]

    def wait_back(n, land):
        for q, k in others:
            s = lax.rem(sp + k, N_SP)
            local_wait(land.at[half_x[q], s], r.i_recv.at[n, half_x[q], s])

    wait_back(0, r.up_l)
    for s in range(N_SP):
        r.up_out[:, s * PAGE : (s + 1) * PAGE] = r.up_l[0, s] + r.up_l[1, s]
    for i, out in enumerate((r.down_out, r.dense_out)):
        land = owned[i][1]
        for xx in range(NX):
            local_wait(land.at[xx], r.j_recv.at[i, xx])
        out[...] = land[0] + land[1]
    wait_back(1, r.qk_l)
    for s in range(N_SP):
        block = r.qk_l[0, s] + r.qk_l[1, s]
        for j in range(3):
            to = j * D + s * width
            r.qkv_out[:, to : to + width] = block[:, j * width : (j + 1) * width]
    wait_back(2, r.small_l)
    r.small_out[...] = jnp.sum(jnp.sum(r.small_l[...], 0), 0)

    for i in range(2):
        for kind in ("across", "sibling", "pass"):
            token_copies(i, kind).wait_send()

    row_copies("wait_send")
    for i in range(2):
        own_copies(i, "wait_send")
    for q, k in others:
        piece(q, k).wait_send()
        for n in range(3):
            back(n, q, k).wait_send()
    for i in range(2):
        for item in token_pair(i):
            item.wait_send()
    for n in range(len(gathered)):
        for item in stage_a(n) + stage_b(n):
            item.wait_send()
        if n != smalls:
            for part in range(2):
                passed_on(n, part).wait_send()
    for n in range(len(reduced)):
        for item in stage_1(n) + stage_2(n):
            item.wait_send()


def layer(x, g, up, qkv, small, down, dense):
    tokens = x.shape[0]
    length = tokens * N_SP
    heads = HEADS // N_SP
    width = heads * HEAD_DIM
    grid = (NY, NZ, NX)
    own = PART * N_SP
    cosine, sine = rotary_tables(length)
    dma = pltpu.SemaphoreType.DMA
    anywhere = pl.BlockSpec(memory_space=pl.ANY)
    vmem = pl.BlockSpec(memory_space=pltpu.VMEM)
    ins = ("x_ref", "g_ref", "up_ref", "qkv_ref", "small_ref", "down_ref", "dense_ref")
    ins += ("cos_ref", "sin_ref")
    outs = {
        "hidden_out": ((tokens, D), BF),
        "hidden_grad": ((tokens, D), BF),
        "up_out": ((PART, FF), F32),
        "qkv_out": ((PART, 3 * D), F32),
        "down_out": ((own, D), F32),
        "dense_out": ((PART, D), F32),
        "small_out": ((8, SMALL), F32),
    }
    chunk = {
        "up": ((own, PAGE), BF),
        "down": ((own, D), BF),
        "qk": ((own, QK), BF),
        "dense": ((PART, D), BF),
        "small": ((8, SMALL), F32),
    }
    scratch = {}
    for name, (shape, kind) in chunk.items():
        if name in ("up", "down"):
            scratch[name + "_a"] = (grid + (own, PAGE // 2), kind)
            scratch[name + "_b"] = (grid + (own, PAGE // 2), kind)
        else:
            scratch[name + "_all"] = (grid + shape, kind)
        scratch[name + "_g"] = (grid + shape, kind)
        scratch[name + "_1"] = (grid + shape, kind)
        scratch[name + "_m"] = ((GROUP // NX, NX) + shape, kind)
        scratch[name + "_2"] = ((GROUP // NX, NX) + shape, kind)
    per_head = (heads, length, HEAD_DIM)
    scratch.update(
        x_all=((length, D), BF),
        g_all=((length, D), BF),
        pieces=((N_SP, PART, PAGE + QK + SMALL), BF),
        landed=((NX, N_SP, PART, PAGE + QK + SMALL), BF),
        tight=((own, PAGE + QK + SMALL), F32),
        up_s=((D, PAGE), BF),
        down_s=((PAGE, D), BF),
        qk_s=((D, QK), BF),
        down_in=((NX, own, D), BF),
        dense_wide=((width, D), F32),
        dense_s=((width, D), BF),
        vec_s=((8, PAGE), F32),
        xhat_s=((length, D), F32),
        n1_s=((length, D), BF),
        n2_s=((length, D), BF),
        act_s=((length, PAGE), BF),
        dpre_s=((length, PAGE), BF),
        sum_s=((length, D), F32),
        dx_s=((length, D), F32),
        dqkv_s=((length, QK), BF),
        q_s=(per_head, BF),
        k_s=(per_head, BF),
        v_s=(per_head, BF),
        do_s=(per_head, BF),
        dq_s=(per_head, BF),
        dk_s=(per_head, F32),
        dv_s=(per_head, F32),
        kt_s=((HEAD_DIM, length), BF),
        vt_s=((HEAD_DIM, length), BF),
        ctxt_s=((heads, HEAD_DIM, length), BF),
        token_in=((2, 2, tokens, D), BF),
        token_mid=((2, tokens, D), BF),
        token_far=((2, tokens, D), BF),
        up_p=((NX, N_SP, PART, PAGE), F32),
        up_l=((NX, N_SP, PART, PAGE), F32),
        qk_p=((NX, N_SP, PART, QK), F32),
        qk_l=((NX, N_SP, PART, QK), F32),
        down_t=((NX, own, D), F32),
        down_l=((NX, own, D), F32),
        dense_t=((NX, PART, D), F32),
        dense_l=((NX, PART, D), F32),
        small_t=((NX, 8, SMALL), F32),
        small_l=((NX, N_SP, 8, SMALL), F32),
    )
    semaphores = {
        "r": (2, NX), "p": (NX, N_SP), "t": (2, N_SP), "a": (7, NY), "b": (7, NY), "q": (7, 2), "e": (5, NY),
        "f": (5, NY), "g": (2, 2), "h": (2,), "j": (2, NX),
    }
    names = list(ins) + list(outs) + list(scratch)
    shapes = [pltpu.VMEM(shape, kind) for shape, kind in scratch.values()]
    for name, shape in semaphores.items():
        names += [name + "_send", name + "_recv"]
        shapes += [dma(shape), dma(shape)]
    names += ["i_send", "i_recv"]
    shapes += [dma((3, NX, N_SP)), dma((3, NX, N_SP))]
    return pl.pallas_call(
        functools.partial(layer_kernel, names),
        out_shape=tuple(jax.ShapeDtypeStruct(*item) for item in outs.values()),
        in_specs=[anywhere, anywhere, vmem, vmem, vmem, anywhere, anywhere, vmem, vmem],
        out_specs=(vmem,) * len(outs),
        scratch_shapes=shapes,
        compiler_params=pltpu.CompilerParams(
            collective_id=0, has_side_effects=True, vmem_limit_bytes=61 * 1024 * 1024
        ),
        cost_estimate=pl.CostEstimate(
            flops=14_000_000_000, bytes_accessed=16_000_000, transcendentals=6_000_000
        ),
        name="layer",
    )(x, g, up, qkv, small, down, dense, cosine, sine)


def outputs_kernel(*refs):
    n = 6
    small_ref, outs = refs[n], refs[n + 1 :]
    for i in range(n):
        outs[i][...] = refs[i][...]
    mine = small_ref[pl.ds(lax.axis_index("sp"), 1), :]
    for (start, each, _, _), out in zip(VECTORS_OUT + VECTORS_OUT[5:6], outs[n:]):
        out[...] = mine[:, start : start + each]


def write_outputs(*arrays):
    vmem = pl.BlockSpec(memory_space=pltpu.VMEM)
    large = [jax.ShapeDtypeStruct(item.shape, item.dtype) for item in arrays[:-1]]
    small = [
        jax.ShapeDtypeStruct((1, each), F32) for _, each, _, _ in VECTORS_OUT + VECTORS_OUT[5:6]
    ]
    return pl.pallas_call(
        outputs_kernel,
        out_shape=tuple(large + small),
        in_specs=[vmem] * len(arrays),
        out_specs=(vmem,) * (len(large) + len(small)),
        name="outputs",
    )(*arrays)


def local(
    hidden_in,
    cotangent,
    attn_gain,
    attn_shift,
    mlp_gain,
    mlp_shift,
    qkv_weight,
    qkv_bias,
    dense_weight,
    dense_bias,
    up_weight,
    up_bias,
    down_weight,
    down_bias,
):
    small = (
        attn_gain,
        attn_shift,
        mlp_gain,
        mlp_shift,
        qkv_bias,
        dense_bias,
        up_bias,
        down_bias,
    )
    packed = jnp.zeros((SMALL,), F32)
    at = 0
    for item in small:
        size = item.shape[0]
        packed = packed + jnp.pad(item.astype(F32), (at, SMALL - at - size))
        at += size
    results = layer(
        hidden_in,
        cotangent,
        up_weight,
        qkv_weight,
        packed.reshape(1, SMALL),
        down_weight,
        dense_weight,
    )
    results = write_outputs(*results)
    hidden_out, hidden_grad, up_own, qkv_own, down_own, dense_own = results[:6]
    parts = [item.reshape(-1) for item in results[6:]]
    return (
        hidden_out,
        hidden_grad,
        parts[0],
        parts[1],
        parts[2],
        parts[3],
        qkv_own,
        parts[4],
        dense_own,
        parts[5],
        up_own,
        parts[6],
        down_own,
        parts[7],
    )


def solution(mesh):
    matrix = P(BOTH, None)
    vector = P(BOTH)
    split = (matrix, matrix) + (vector,) * 4 + (matrix, vector) * 4
    return jax.shard_map(local, mesh=mesh, in_specs=split, out_specs=split, check_vma=False)
```
